32 devices in a mesh: rows: 16 (over z, y, x), mp: 2 (over core).
Axes of the slice: x: 2, y: 2, z: 4, core: 2. Of those that a mesh axis runs over, the one named last changes fastest.
Arguments:
- atoms: bfloat16 [16384, 768], P(('rows', 'mp')), may hold values from -6 to 6
- time_embedding: bfloat16 [48, 768], replicated, may hold values from -6 to 6
- coordinates: int32 [3, 16384], P(None, ('rows', 'mp')), may hold values from -24 to 24
- item_lengths: int32 [48], replicated, may hold values from 1 to 896, as said below
- item_group: int32 [48], replicated, may hold values from 0 to 15, as said below
- query_weight: bfloat16 [768, 768], P(('rows', 'mp')), may hold values from -0.21875 to 0.21875
- key_weight: bfloat16 [768, 768], P(('rows', 'mp')), may hold values from -0.21875 to 0.21875
- value_weight: bfloat16 [768, 768], P(('rows', 'mp')), may hold values from -0.21875 to 0.21875
- out_weight: bfloat16 [768, 768], P(('rows', 'mp')), may hold values from -0.625 to 0.625
- up_weight: bfloat16 [768, 3072], P(('rows', 'mp')), may hold values from -0.21875 to 0.21875
- down_weight: bfloat16 [3072, 768], P(('rows', 'mp')), may hold values from -0.109375 to 0.109375
- value_bias: bfloat16 [768], P(('rows', 'mp')), may hold values from -2 to 2
- out_bias: bfloat16 [768], P(('rows', 'mp')), may hold values from -2 to 2
- up_bias: bfloat16 [3072], P(('rows', 'mp')), may hold values from -3 to 3
- down_bias: bfloat16 [768], P(('rows', 'mp')), may hold values from -2 to 2
- first_gain: bfloat16 [768], P(('rows', 'mp')), may hold values from 0.099609375 to 1.8984375
- first_shift: bfloat16 [768], P(('rows', 'mp')), may hold values from -2 to 2
- second_gain: bfloat16 [768], P(('rows', 'mp')), may hold values from 0.099609375 to 1.8984375
- second_shift: bfloat16 [768], P(('rows', 'mp')), may hold values from -2 to 2
- kernel_params: bfloat16 [4352], P(('rows', 'mp')), may hold values from -4 to 12, as said below
- cotangent: bfloat16 [16384, 768], P(('rows', 'mp')), may hold values from -6 to 6
Outputs:
- layer_out: bfloat16 [16384, 768], P(('rows', 'mp'))
- atoms_grad: float32 [16384, 768], P(('rows', 'mp'))
- query_weight_grad: float32 [768, 768], P(('rows', 'mp'))
- key_weight_grad: float32 [768, 768], P(('rows', 'mp'))
- value_weight_grad: float32 [768, 768], P(('rows', 'mp'))
- out_weight_grad: float32 [768, 768], P(('rows', 'mp'))
- up_weight_grad: float32 [768, 3072], P(('rows', 'mp'))
- down_weight_grad: float32 [3072, 768], P(('rows', 'mp'))
- value_bias_grad: float32 [768], P(('rows', 'mp'))
- out_bias_grad: float32 [768], P(('rows', 'mp'))
- up_bias_grad: float32 [3072], P(('rows', 'mp'))
- down_bias_grad: float32 [768], P(('rows', 'mp'))
- first_gain_grad: float32 [768], P(('rows', 'mp'))
- first_shift_grad: float32 [768], P(('rows', 'mp'))
- second_gain_grad: float32 [768], P(('rows', 'mp'))
- second_shift_grad: float32 [768], P(('rows', 'mp'))
- kernel_params_grad: float32 [4352], P(('rows', 'mp'))
The draws below stay inside these ranges and needn't reach their ends.
Inputs may be any that keep to these rules, and one draw needn't show every extreme that they name: `item_group`: each row group is named by exactly 3 items. `item_lengths`: in every row group one item has more than 512 rows and the others at most 64; a group's items fill at most 1024 rows. `kernel_params`: widths lie in 0.5 to 4.
All inputs are finite; a program needn't handle non-finite values.
Results may differ from the reference program's by a relative error of at most 0.02.
Values may be sent and summed in bfloat16 or wider, within the bound.
A program may use at most 576 MiB of HBM per device.

```python
import math
import jax
import jax.numpy as jnp
from jax import lax

D = 768
HEADS = 32
HEAD = 24
FF = 3072
KERN = 128
TOK_DEV = 512
PER_GROUP = 3
GROUP_ROWS = 1024
ITEMS = 48
ROWS = 16384
N_MP = 2


def shuffled_items(key):
    return jax.random.permutation(key, ITEMS).astype(jnp.int32)


def draw_item_group(key, part):
    order = shuffled_items(key)
    return (order // PER_GROUP).astype(jnp.int32)


def draw_item_lengths(key, part):
    order = shuffled_items(key)
    key = jax.random.fold_in(key, 2)
    long_key, short_key = jax.random.split(key)
    longest = GROUP_ROWS - 2 * (TOK_DEV // 8)
    longs = jax.random.randint(long_key, (ITEMS,), TOK_DEV + 1, longest + 1)
    shorts = jax.random.randint(short_key, (ITEMS,), 1, TOK_DEV // 8 + 1)
    lengths = jnp.where(order % PER_GROUP == 0, longs, shorts)
    lengths = jnp.where(order == 0, longest, lengths)
    lengths = jnp.where(order == 1, 1, lengths)
    return lengths.astype(jnp.int32)


def draw_kernel_params(key, part):
    key = jax.random.fold_in(key, 3)
    mean_key, width_key, mix_key = jax.random.split(key, 3)
    means = jax.random.uniform(mean_key, (KERN,), jnp.float32, 0.0, 12.0)
    widths = jnp.exp(jax.random.uniform(width_key, (KERN,), jnp.float32, jnp.log(0.5), jnp.log(4.0)))
    mix = jnp.clip(jax.random.normal(mix_key, (KERN * HEADS,), jnp.float32), -4.0, 4.0)
    return jnp.concatenate([means, widths, mix]).astype(jnp.bfloat16)


def with_ends(values, rng, smallest, largest):
    shape = values.shape
    spot = [jax.random.randint(jax.random.fold_in(rng, axis), (), 0, shape[axis]) for axis in range(len(shape))]
    values = values.at[tuple(spot)].set(smallest)
    longest = shape.index(max(shape))
    spot[longest] = (spot[longest] + 1) % shape[longest]
    return values.at[tuple(spot)].set(largest)


def block_levels(own_key, shape, pieces, smallest, top_value):
    loudness, own = 1.0, jax.random.fold_in(own_key, 6)
    for position, parts in pieces:
        heights = jnp.exp(jax.random.uniform(jax.random.fold_in(own, position), (parts,), jnp.float32, smallest / len(pieces), top_value / len(pieces)))
        loudness = loudness * jnp.repeat(heights, shape[position] // parts).reshape([-1 if axis == position else 1 for axis in range(len(shape))])
    return loudness


def noise(own_key, dims, scale, reach, cuts=(), held_as=jnp.bfloat16):
    values = scale * jax.random.normal(own_key, dims, jnp.float32)
    if cuts:
        values = values * block_levels(own_key, dims, cuts, -0.22, 0.18)
    return jnp.clip(values, -reach, reach).astype(held_as)


def setup_inputs(seed: int = 0) -> dict:
    key_list = jax.random.split(jax.random.key(seed), 22)
    return {
        "atoms": noise(key_list[0], (ROWS, D), 1.0, 6.0, ((0, 32),)),
        "time_embedding": noise(key_list[1], (ITEMS, D), 1.0, 6.0),
        "coordinates": with_ends(jax.random.randint(key_list[2], (3, ROWS), -24, 25), jax.random.fold_in(key_list[2], 1), -24, 24).astype(jnp.int32),
        "item_lengths": draw_item_lengths(jax.random.fold_in(key_list[21], 71), 0),
        "item_group": draw_item_group(jax.random.fold_in(key_list[21], 71), 0),
        "query_weight": noise(key_list[5], (D, D), D ** -0.5, 0.21875, ((0, 32),)),
        "key_weight": noise(key_list[6], (D, D), D ** -0.5, 0.21875, ((0, 32),)),
        "value_weight": noise(key_list[7], (D, D), D ** -0.5, 0.21875, ((0, 32),)),
        "out_weight": noise(key_list[8], (D, D), (D // 8) ** -0.5, 0.625, ((0, 32),)),
        "up_weight": noise(key_list[9], (D, FF), D ** -0.5, 0.21875, ((0, 32),)),
        "down_weight": noise(key_list[10], (FF, D), FF ** -0.5, 0.109375, ((0, 32),)),
        "value_bias": noise(key_list[11], (D,), 0.3, 2.0, ((0, 32),)),
        "out_bias": noise(key_list[12], (D,), 0.3, 2.0, ((0, 32),)),
        "up_bias": noise(key_list[13], (FF,), 0.5, 3.0, ((0, 32),)),
        "down_bias": noise(key_list[14], (D,), 0.3, 2.0, ((0, 32),)),
        "first_gain": jnp.clip(1.0 + 0.18 * jax.random.normal(key_list[15], (D,), jnp.float32), 0.099609375, 1.8984375).astype(jnp.bfloat16),
        "first_shift": noise(key_list[16], (D,), 0.3, 2.0, ((0, 32),)),
        "second_gain": jnp.clip(1.0 + 0.18 * jax.random.normal(key_list[17], (D,), jnp.float32), 0.099609375, 1.8984375).astype(jnp.bfloat16),
        "second_shift": noise(key_list[18], (D,), 0.3, 2.0, ((0, 32),)),
        "kernel_params": draw_kernel_params(jax.random.fold_in(key_list[21], 71), 0),
        "cotangent": noise(key_list[20], (ROWS, D), 1.0, 6.0, ((0, 32),)),
    }


@jax.custom_vjp
def low(v):
    return lax.optimization_barrier(v.astype(jnp.bfloat16)).astype(jnp.float32)

@jax.custom_vjp
def low_back(v):
    return v

def low_keep(v):
    return (low(v), None)

def low_pass(kept, grad):
    return (grad,)

def back_keep(v):
    return (v, None)

def back_low(kept, grad):
    return (low(grad),)
low.defvjp(low_keep, low_pass)
low_back.defvjp(back_keep, back_low)

def row_items(global_rows, group_rows, lengths, groups):
    count = lengths.shape[0]
    order = jnp.arange(count, dtype=jnp.int32)
    earlier = (groups[:, None] == groups[None, :]) & (order[None, :] < order[:, None])
    starts = lax.optimization_barrier(jnp.sum(jnp.where(earlier, lengths[None, :], 0), axis=1)).astype(jnp.int32)
    group_of = (global_rows // group_rows).astype(jnp.int32)
    place = (global_rows - group_of * group_rows).astype(jnp.int32)
    hits = (groups[None, :] == group_of[:, None]) & (place[:, None] >= starts[None, :]) & (place[:, None] < starts[None, :] + lengths[None, :])
    item = lax.optimization_barrier(jnp.sum(jnp.where(hits, order[None, :], 0), axis=1)).astype(jnp.int32)
    return (item, jnp.any(hits, axis=1))

def layer_norm(value, gain, shift):
    centre = value - lax.optimization_barrier(jnp.mean(value, axis=-1, keepdims=True))
    spread = lax.optimization_barrier(jnp.mean(centre * centre, axis=-1, keepdims=True))
    return centre * lax.rsqrt(spread + 1e-05) * gain + shift

def densities(coord_near, coord_all, means, widths):
    diff = coord_near[:, :, None] - coord_all[:, None, :]
    dist = jnp.sqrt(lax.optimization_barrier(jnp.sum(diff * diff, axis=0))) * 0.25
    scaled = (dist[:, :, None] - means) / widths
    return jnp.exp(-0.5 * scaled * scaled) / (widths * math.sqrt(2.0 * math.pi))

def both(value):
    return low(low_back(value))

def reference(atoms, time_embedding, coordinates, item_lengths, item_group, query_weight, key_weight, value_weight, out_weight, up_weight, down_weight, value_bias, out_bias, up_bias, down_bias, first_gain, first_shift, second_gain, second_shift, kernel_params, cotangent):
    f32 = jnp.float32
    highest = lax.Precision.HIGHEST
    rows_all = atoms.shape[0]
    glob = jnp.arange(rows_all, dtype=jnp.int32)
    items, valid = row_items(glob, GROUP_ROWS, item_lengths, item_group)
    embed = jnp.where(valid[:, None], time_embedding.astype(f32)[items], 0.0)
    coords = coordinates.astype(f32)
    params = tuple((p.astype(f32) for p in (query_weight, key_weight, value_weight, out_weight, up_weight, down_weight, value_bias, out_bias, up_bias, down_bias, first_gain, first_shift, second_gain, second_shift, kernel_params)))
    blocks = rows_all // TOK_DEV

    def hdot(left, right):
        return jnp.dot(left, right, precision=highest, preferred_element_type=f32)

    def forward(params, inputs):
        query_w, key_w, value_w, out_w, up_w, down_w, value_b, out_b, up_b, down_b, gain_one, shift_one, gain_two, shift_two, kernel_table = params
        means = kernel_table[:KERN]
        widths = kernel_table[KERN:2 * KERN]
        mix = kernel_table[2 * KERN:].reshape(KERN, HEADS)
        h_zero = inputs + embed
        normed = low(layer_norm(h_zero, gain_one, shift_one))
        query = both(hdot(normed, query_w))
        keys = both(hdot(normed, key_w))
        values = both(hdot(normed, value_w) + value_b)

        def block(index):
            start = index * TOK_DEV
            base = index // N_MP * GROUP_ROWS
            query_part = lax.dynamic_slice_in_dim(query, start, TOK_DEV, 0).reshape(TOK_DEV, HEADS, HEAD)
            key_part = lax.dynamic_slice_in_dim(keys, base, GROUP_ROWS, 0).reshape(GROUP_ROWS, HEADS, HEAD)
            value_part = lax.dynamic_slice_in_dim(values, base, GROUP_ROWS, 0).reshape(GROUP_ROWS, HEADS, HEAD)
            near = lax.dynamic_slice_in_dim(coords, start, TOK_DEV, 1)
            whole = lax.dynamic_slice_in_dim(coords, base, GROUP_ROWS, 1)
            phi = low(densities(near, whole, means, widths))
            bias = jnp.dot(phi.reshape(-1, KERN), mix, precision=highest).reshape(TOK_DEV, GROUP_ROWS, HEADS).transpose(2, 0, 1)
            raw = jnp.einsum('ihd,jhd->hij', query_part, key_part, precision=highest)
            item_near = lax.dynamic_slice_in_dim(items, start, TOK_DEV, 0)
            item_all = lax.dynamic_slice_in_dim(items, base, GROUP_ROWS, 0)
            valid_near = lax.dynamic_slice_in_dim(valid, start, TOK_DEV, 0)
            valid_all = lax.dynamic_slice_in_dim(valid, base, GROUP_ROWS, 0)
            row_near = lax.dynamic_slice_in_dim(glob, start, TOK_DEV, 0)
            row_all = lax.dynamic_slice_in_dim(glob, base, GROUP_ROWS, 0)
            allowed = jnp.where(valid_near[:, None], (item_near[:, None] == item_all[None, :]) & valid_all[None, :], row_near[:, None] == row_all[None, :])
            scores = low_back(jnp.where(allowed[None], raw * HEAD ** (-0.5) + bias, -1e+30))
            top = lax.optimization_barrier(jnp.max(scores, axis=-1, keepdims=True))
            expo = jnp.exp(scores - top)
            probs = both(expo / lax.optimization_barrier(jnp.sum(expo, axis=-1, keepdims=True)))
            return jnp.einsum('hij,jhd->ihd', probs, value_part, precision=highest).reshape(TOK_DEV, D)
        mixed = lax.map(jax.checkpoint(block), jnp.arange(blocks, dtype=jnp.int32)).reshape(rows_all, D)
        mixed = both(mixed)
        h_one = h_zero + low_back(hdot(mixed, out_w) + out_b)
        second = low(layer_norm(h_one, gain_two, shift_two))
        up = low_back(hdot(second, up_w) + up_b)
        act = low(jax.nn.gelu(up, approximate=False))
        h_two = h_one + low_back(hdot(act, down_w) + down_b)
        return jnp.where(valid[:, None], h_two, 0.0)
    result, pull = jax.vjp(forward, params, atoms.astype(f32))
    grads, atoms_grad = pull(cotangent.astype(f32))
    return (result.astype(jnp.bfloat16), atoms_grad, grads[0], grads[1], grads[2], grads[3], grads[4], grads[5], grads[6], grads[7], grads[8], grads[9], grads[10], grads[11], grads[12], grads[13], grads[14])
```

```python
import functools
import math

import jax
import jax.numpy as jnp
import numpy as np
from jax import lax
from jax.experimental import pallas as pl
from jax.experimental.pallas import tpu as pltpu
from jax.sharding import PartitionSpec as P

HEADS = 32
KERN = 128
HEAD = 24
GH = 8
NG = HEADS // GH
GW = GH * HEAD
MIB = 2**20
CENTRE = 6.0
STORED = 1
AXES = ("rows", "mp")
f32 = jnp.float32
bf16 = jnp.bfloat16


def dot(left, right):
    return jnp.dot(left, right, preferred_element_type=f32)


def whole(shape):
    return pl.BlockSpec(shape, lambda i: (0,) * len(shape))


def high_low(value):
    high = value.astype(bf16)
    return high, (value - high.astype(f32)).astype(bf16)


def distances(near_ref, all_ref):
    total = None
    for c in range(3):
        diff = near_ref[:, c : c + 1] - all_ref[c : c + 1, :]
        total = diff * diff if total is None else total + diff * diff
    return jnp.sqrt(total) * 0.25


def bias_kernel(
    pairs_step, near_ref, all_ref, code_near_ref, code_all_ref, means_ref, curve_ref, mix_ref,
    bias_ref, phi_ref, dist_ref, mask_ref,
):
    dist_ref[...] = distances(near_ref, all_ref)
    mask_ref[...] = jnp.where(code_near_ref[:, 0:1] == code_all_ref[0:1, :], 0.0, -1e30)
    rows, span = dist_ref.shape

    def body(step, carry):
        for q in range(pairs_step):
            pair = step * pairs_step + q
            drow = [dist_ref[pl.ds(pair * 2 + e, 1), :] for e in range(2)]
            mrow = [mask_ref[pl.ds(pair * 2 + e, 1), :] for e in range(2)]
            for lane in range(0, span, 256):
                tall = []
                for e in range(2):
                    wide = []
                    for low in (lane, lane + 128):
                        u = drow[e][:, low : low + 128] - means_ref[...]
                        wide.append(jnp.exp2((u * curve_ref[...]) * u).astype(bf16))
                    wide = jnp.concatenate(wide, axis=1)
                    if e < STORED:
                        phi_ref[pair * STORED + e, :, lane : lane + 256] = wide
                    tall.append(wide)
                out = dot(mix_ref[...], jnp.concatenate(tall, axis=0)).reshape(NG, 2, GH, 256)
                out = jnp.concatenate(
                    [out[:, e : e + 1] + mrow[e][:, lane : lane + 256].reshape(1, 1, 1, 256) for e in range(2)],
                    axis=1,
                )
                bias_ref[:, pl.ds(pl.multiple_of(pair * 16, 16), 16), lane : lane + 256] = out.reshape(
                    NG, 16, 256
                ).astype(bf16)
        return carry

    lax.fori_loop(0, rows // 2 // pairs_step, body, 0)


def lane_wide(values):
    return jnp.broadcast_to(values[:, None], (KERN, 128))


def pair_bias(near, coord_all, code_near, code_all, means, curve, mix_low, tile=32, pairs_step=8):
    rows, span = near.shape[0], coord_all.shape[1]
    m4 = mix_low.T.reshape(NG, GH, KERN)
    zero = jnp.zeros_like(m4)
    left = jnp.stack([jnp.concatenate([m4, zero], -1), jnp.concatenate([zero, m4], -1)], axis=1)
    left = left.reshape(2 * HEADS, 2 * KERN)
    return pl.pallas_call(
        functools.partial(bias_kernel, pairs_step),
        grid=(rows // tile,),
        in_specs=[
            pl.BlockSpec((tile, 3), lambda i: (i, 0)),
            whole((3, span)),
            pl.BlockSpec((tile, 1), lambda i: (i, 0)),
            whole((1, span)),
            whole((KERN, 128)),
            whole((KERN, 128)),
            whole((2 * HEADS, 2 * KERN)),
        ],
        out_specs=[
            pl.BlockSpec((NG, tile * GH, span), lambda i: (0, i, 0)),
            pl.BlockSpec((tile * STORED // 2, KERN, span), lambda i: (i, 0, 0)),
        ],
        out_shape=[
            jax.ShapeDtypeStruct((NG, rows * GH, span), bf16),
            jax.ShapeDtypeStruct((rows * STORED // 2, KERN, span), bf16),
        ],
        scratch_shapes=[pltpu.VMEM((tile, span), f32), pltpu.VMEM((tile, span), f32)],
        compiler_params=pltpu.CompilerParams(vmem_limit_bytes=50 * MIB),
        cost_estimate=pl.CostEstimate(
            flops=2 * rows * span * KERN * HEADS * 8,
            bytes_accessed=rows * span * (KERN * STORED + 2 * HEADS),
            transcendentals=rows * span * KERN,
        ),
        name="bias",
    )(near, coord_all, code_near, code_all, lane_wide(means), lane_wide(curve), left)


def repeat_tables(tile):
    row = np.arange(tile * GH)
    repeat = row[:, None] // GH == np.arange(tile)[None, :]
    own = row[:, None] % GH == np.arange(GW)[None, :] // HEAD
    return repeat, own


def attend_kernel(
    tiles, q_ref, kt_ref, v_ref, b_ref, rep_ref, rept_ref, own_ref, scaled_ref,
    e_ref, mixed_ref, inv_ref, qa, qb, sa, sb, ea, oa, ob, wa, wb,
):
    query, scores, outs, wides = (qa, qb), (sa, sb), (oa, ob), (wa, wb)
    rows, span = sa.shape
    held = rows // GH
    units = NG * tiles
    parts, chunk, ahead = 4, 8, 3
    step, some = span // parts, rows // parts
    pid = pl.program_id(0)

    def place(unit):
        unit = jnp.clip(unit, 0, units - 1)
        group = unit // tiles
        return group, pl.ds(pl.multiple_of((unit - group * tiles) * held, held), held)

    def spread(unit, par):
        g, i = place(unit)
        query[par][...] = (dot(rep_ref[...], q_ref[g, i, :]) * scaled_ref[...]).astype(bf16)

    def score(unit, par, part):
        g, _ = place(unit)
        cols = slice(part * step, (part + 1) * step)
        scores[par][:, cols] = dot(query[par][...], kt_ref[g, :, cols])

    def soften(par, part):
        chunks = range(part * some, (part + 1) * some, chunk)
        held_x = {}
        for n in range(len(chunks) + ahead):
            if n < len(chunks):
                here = slice(chunks[n], chunks[n] + chunk)
                x = scores[par][here, :] + b_ref[par, here, :].astype(f32)
                held_x[n] = x, jnp.max(x, axis=1, keepdims=True)
            if n >= ahead:
                here = slice(chunks[n - ahead], chunks[n - ahead] + chunk)
                x, top = held_x.pop(n - ahead)
                e = jnp.exp2(x - top).astype(bf16)
                e_ref[par, here, :] = e
                if par == 1:
                    ea[here, :] = e

    def mix(unit, par, part):
        g, _ = place(unit)
        here = slice(part * some, (part + 1) * some)
        source = e_ref.at[0] if par == 0 else ea
        outs[par][here, :] = dot(source[here, :], v_ref[g])

    def scale(par, part):
        here = slice(part * some, (part + 1) * some)
        out = outs[par][here, :]
        inv = 1.0 / out[:, GW : GW + 1]
        own = own_ref[here, :]
        wides[par][here, :] = jnp.concatenate(
            [*high_low(out[:, :GW] * inv * own), *high_low(inv * own)], axis=1
        )

    def gather(unit, par):
        g, i = place(unit)
        out = dot(rept_ref[...], wides[par][...])
        mixed_ref[g, i, :] = out[:, :GW] + out[:, GW : 2 * GW]
        inv_ref[g, i, :] = out[:, 2 * GW : 3 * GW] + out[:, 3 * GW :]

    @pl.when(pid == 0)
    def _():
        spread(0, 0)
        for part in range(parts):
            score(0, 0, part)
        spread(1, 1)
        ea[...] = jnp.ones_like(ea)
        for ref in (oa, ob):
            ref[...] = jnp.ones_like(ref)
        for ref in (wa, wb):
            ref[...] = jnp.zeros_like(ref)

    for par in range(2):
        unit = pid * 2 + par
        gather(unit - 3, 1 - par)
        for part in range(parts):
            score(unit + 1, 1 - par, part)
            scale(par, part)
            mix(unit - 1, 1 - par, part)
            soften(par, part)
        spread(unit + 2, par)

    @pl.when(pid == units // 2 - 1)
    def _():
        for part in range(parts):
            scale(0, part)
            mix(units - 1, 1, part)
        gather(units - 3, 1)
        gather(units - 2, 0)
        for part in range(parts):
            scale(1, part)
        gather(units - 1, 1)


def attend(q4, kt4, vx4, bias, tile=64):
    rows, span = q4.shape[1], kt4.shape[2]
    tiles = rows // tile
    repeat, own = repeat_tables(tile)
    deep = tile * GH
    bias = bias.reshape(NG * tiles, deep, span)
    big = pl.BlockSpec((2, deep, span), lambda i: (i, 0, 0))
    scale = HEAD**-0.5 * math.log2(math.e)
    e, mixed, inv = pl.pallas_call(
        functools.partial(attend_kernel, tiles),
        grid=(NG * tiles // 2,),
        in_specs=[
            whole((NG, rows, GW)),
            whole((NG, GW, span)),
            whole(vx4.shape),
            big,
            whole((deep, tile)),
            whole((tile, deep)),
            whole((deep, GW)),
            whole((deep, GW)),
        ],
        out_specs=[big, whole((NG, rows, GW)), whole((NG, rows, GW))],
        out_shape=[
            jax.ShapeDtypeStruct((NG * tiles, deep, span), bf16),
            jax.ShapeDtypeStruct((NG, rows, GW), f32),
            jax.ShapeDtypeStruct((NG, rows, GW), f32),
        ],
        scratch_shapes=[pltpu.VMEM((deep, GW), bf16)] * 2
        + [pltpu.VMEM((deep, span), f32)] * 2
        + [pltpu.VMEM((deep, span), bf16)]
        + [pltpu.VMEM((deep, 256), f32)] * 2
        + [pltpu.VMEM((deep, 4 * GW), bf16)] * 2,
        compiler_params=pltpu.CompilerParams(vmem_limit_bytes=50 * MIB),
        cost_estimate=pl.CostEstimate(
            flops=4 * rows * GH * NG * span * GW,
            bytes_accessed=rows * span * HEADS * 4,
            transcendentals=rows * span * HEADS,
        ),
        name="attend",
    )(
        q4, kt4, vx4, bias, jnp.asarray(repeat, bf16), jnp.asarray(repeat.T, bf16),
        jnp.asarray(own, f32), jnp.asarray(own * scale, f32),
    )
    return e.reshape(NG, rows * GH, span), mixed, inv


def attend_back_kernel(
    chunk, q_ref, gs_ref, mx_ref, k_ref, vt_ref, e_ref, rep_ref, rept_ref, own_ref, ownt_ref,
    ds_ref, dq_ref, dkt_ref, dvt_ref, s0, s1,
):
    groups_here = q_ref.shape[0]
    rows, span = s0.shape
    scores = (s0, s1)
    parts = 4
    step = span // parts
    count = rows // chunk
    scale = HEAD**-0.5

    @pl.when(pl.program_id(0) == 0)
    def _():
        dkt_ref[...] = jnp.zeros_like(dkt_ref)
        dvt_ref[...] = jnp.zeros_like(dvt_ref)

    def begin(g):
        grad = dot(rep_ref[...], gs_ref[g]) * own_ref[...]
        high, low = high_low(gs_ref[g].astype(f32) * mx_ref[g])
        wide = dot(rep_ref[...], jnp.concatenate([high, low], axis=1))
        delta = jnp.sum((wide[:, :GW] + wide[:, GW:]) * own_ref[...], axis=1, keepdims=True)
        return grad.astype(bf16), delta

    def across(value):
        wide = lax.dot_general(value, rept_ref[...], (((0,), (0,)), ((), ())), preferred_element_type=f32)
        return (wide * ownt_ref[...]).astype(bf16)

    def grad_probs(g, grad, part):
        cols = slice(part * step, (part + 1) * step)
        scores[g % 2][:, cols] = dot(grad, vt_ref[g, :, cols])

    def soft_back(g, delta, part):
        for c in range(part * count // parts, (part + 1) * count // parts):
            here = slice(c * chunk, (c + 1) * chunk)
            ds_ref[g, here, :] = (
                e_ref[g, here, :].astype(f32) * (scores[g % 2][here, :] - delta[here])
            ).astype(bf16)

    def finish(g, query_t, grad_t, part):
        cols = slice(part * step, (part + 1) * step)
        dvt_ref[g, :, cols] += dot(grad_t, e_ref[g, :, cols])
        dkt_ref[g, :, cols] += dot(query_t, ds_ref[g, :, cols])

    def query_grad(g):
        out = dot(ds_ref[g], k_ref[g])
        dq_ref[g] = (dot(rept_ref[...], (out * own_ref[...]).astype(bf16)) * scale).astype(bf16)

    begun = [begin(g) for g in range(groups_here)]
    for part in range(parts):
        grad_probs(0, begun[0][0], part)
    turned = None
    for g in range(groups_here):
        for part in range(parts):
            if g + 1 < groups_here:
                grad_probs(g + 1, begun[g + 1][0], part)
            if g > 0:
                if part == 0:
                    turned = across(q_ref[g - 1]), across(gs_ref[g - 1])
                finish(g - 1, *turned, part)
                if part == 2:
                    query_grad(g - 1)
            soft_back(g, begun[g][1], part)
    turned = across(q_ref[groups_here - 1]), across(gs_ref[groups_here - 1])
    for part in range(parts):
        finish(groups_here - 1, *turned, part)
    query_grad(groups_here - 1)


def attend_back(q4, gs4, mx4, k4, vt4, e, first, groups, tile=64, chunk=8):
    rows, span = q4.shape[1], k4.shape[1]
    repeat, own = repeat_tables(tile)
    block = first // groups
    big = pl.BlockSpec((groups, tile * GH, span), lambda i: (block, i, 0))
    small = pl.BlockSpec((groups, tile, GW), lambda i: (block, i, 0))
    held = lambda shape: pl.BlockSpec(shape, lambda i: (block, 0, 0))
    return pl.pallas_call(
        functools.partial(attend_back_kernel, chunk),
        grid=(rows // tile,),
        in_specs=[
            small,
            small,
            small,
            held((groups, span, GW)),
            held((groups, GW, span)),
            big,
            whole((tile * GH, tile)),
            whole((tile, tile * GH)),
            whole((tile * GH, GW)),
            whole((GW, tile * GH)),
        ],
        out_specs=[
            pl.BlockSpec((groups, tile * GH, span), lambda i: (0, i, 0)),
            pl.BlockSpec((groups, tile, GW), lambda i: (0, i, 0)),
            whole((groups, GW, span)),
            whole((groups, GW, span)),
        ],
        out_shape=[
            jax.ShapeDtypeStruct((groups, rows * GH, span), bf16),
            jax.ShapeDtypeStruct((groups, rows, GW), bf16),
            jax.ShapeDtypeStruct((groups, GW, span), f32),
            jax.ShapeDtypeStruct((groups, GW, span), f32),
        ],
        scratch_shapes=[pltpu.VMEM((tile * GH, span), f32)] * 2,
        compiler_params=pltpu.CompilerParams(vmem_limit_bytes=58 * MIB),
        cost_estimate=pl.CostEstimate(
            flops=8 * rows * GH * groups * span * GW,
            bytes_accessed=rows * span * HEADS * 4,
            transcendentals=0,
        ),
        name="attend_back",
    )(
        q4, gs4, mx4, k4, vt4, e, jnp.asarray(repeat, bf16), jnp.asarray(repeat.T, bf16),
        jnp.asarray(own, f32), jnp.asarray(own.T, f32),
    )


def bias_back_kernel(
    pairs_step, near_ref, all_ref, means_ref, curve_ref, ds0_ref, ds1_ref, phi_ref, out_ref, dist_ref
):
    dist_ref[...] = distances(near_ref, all_ref)
    rows, span = dist_ref.shape

    @pl.when(pl.program_id(0) == 0)
    def _():
        out_ref[...] = jnp.zeros_like(out_ref)

    def body(step, acc):
        for q in range(pairs_step):
            pair = step * pairs_step + q
            here = pl.ds(pl.multiple_of(pair * 16, 16), 16)
            both = jnp.concatenate([ds0_ref[:, here, :].astype(f32), ds1_ref[:, here, :].astype(f32)], axis=0)
            for e in range(2):
                d = dist_ref[pl.ds(pair * 2 + e, 1), :]
                if e < STORED:
                    phi = phi_ref[pair * STORED + e]
                else:
                    wide = []
                    for lane in range(0, span, 128):
                        u = d[:, lane : lane + 128] - means_ref[...]
                        wide.append(jnp.exp2((u * curve_ref[...]) * u).astype(bf16))
                    phi = jnp.concatenate(wide, axis=1)
                d = d - CENTRE
                s = both[:, e * GH : (e + 1) * GH, :].reshape(HEADS, span)
                one = s * d
                x = jnp.concatenate([s.astype(bf16), *high_low(one), *high_low(one * d)], axis=0)
                acc = acc + lax.dot_general(
                    x, phi, (((1,), (1,)), ((), ())), preferred_element_type=f32
                )
        return acc

    out_ref[...] += lax.fori_loop(0, rows // 2 // pairs_step, body, jnp.zeros(out_ref.shape, f32))


def bias_back(near, coord_all, means, curve, ds, phi, first, count, tile=32, pairs_step=4):
    span = coord_all.shape[1]
    rows = count * tile
    return pl.pallas_call(
        functools.partial(bias_back_kernel, pairs_step),
        grid=(count,),
        in_specs=[
            pl.BlockSpec((tile, 3), lambda i: (i + first, 0)),
            whole((3, span)),
            whole((KERN, 128)),
            whole((KERN, 128)),
            pl.BlockSpec((NG // 2, tile * GH, span), lambda i: (0, i + first, 0)),
            pl.BlockSpec((NG // 2, tile * GH, span), lambda i: (0, i + first, 0)),
            pl.BlockSpec((tile * STORED // 2, KERN, span), lambda i: (i + first, 0, 0)),
        ],
        out_specs=whole((5 * HEADS, KERN)),
        out_shape=jax.ShapeDtypeStruct((5 * HEADS, KERN), f32),
        scratch_shapes=[pltpu.VMEM((tile, span), f32)],
        compiler_params=pltpu.CompilerParams(vmem_limit_bytes=50 * MIB),
        cost_estimate=pl.CostEstimate(
            flops=4 * rows * span * KERN * 5 * HEADS,
            bytes_accessed=rows * span * (KERN * STORED + 2 * HEADS),
            transcendentals=0,
        ),
        name="bias_back",
    )(near, coord_all, lane_wide(means), lane_wide(curve), *ds, phi)


def row_items(global_rows, group_rows, lengths, groups):
    count = lengths.shape[0]
    order = jnp.arange(count, dtype=jnp.int32)
    earlier = (groups[:, None] == groups[None, :]) & (order[None, :] < order[:, None])
    starts = jnp.sum(jnp.where(earlier, lengths[None, :], 0), axis=1)
    group_of = global_rows // group_rows
    place = global_rows - group_of * group_rows
    hits = (
        (groups[None, :] == group_of[:, None])
        & (place[:, None] >= starts[None, :])
        & (place[:, None] < starts[None, :] + lengths[None, :])
    )
    item = jnp.sum(jnp.where(hits, order[None, :], 0), axis=1)
    return (item, jnp.any(hits, axis=1))


def layer_norm(value, gain, shift):
    centre = value - jnp.mean(value, axis=-1, keepdims=True)
    spread = jnp.mean(centre * centre, axis=-1, keepdims=True)
    return centre * lax.rsqrt(spread + 1e-05) * gain + shift


def col_sum(value):
    return jnp.sum(value.astype(f32), axis=0)


def left_dot(left, right):
    return lax.dot_general(left, right, (((0,), (0,)), ((), ())), preferred_element_type=f32)


def right_dot(left, right):
    return lax.dot_general(left, right, (((1,), (1,)), ((), ())), preferred_element_type=f32)


AXES = ("rows", "mp")


def swap_sides(block):
    return lax.ppermute(block, "mp", [(0, 1), (1, 0)])


def halves(pair, axis, mine):
    kept, come = pair

    def half(index, dtype):
        part = lax.dynamic_index_in_dim(kept, index, axis, keepdims=False)
        if come is not None:
            part = part + lax.dynamic_index_in_dim(come, index, axis, keepdims=False).astype(f32)
        return part.astype(dtype)

    return half(1 - mine, bf16), half(mine, f32)


class Shards:
    def __init__(self, partial, first_bits):
        chips = lax.axis_size("rows")
        bits = chips.bit_length() - 1
        stack, rows, columns = partial.shape
        kept = partial.reshape(stack, *[2] * bits, 2, rows // (2 * chips), columns)
        self.pair = (kept, None)
        self.left = list(range(bits))[::-1]
        self.order = [None] + [b for b in first_bits if b < bits] + [b for b in range(bits) if b not in first_bits]

    def exchange(self):
        if not self.order:
            return
        bit = self.order.pop(0)
        if bit is None:
            send, kept = halves(self.pair, 1 + len(self.left), lax.axis_index("mp"))
            self.pair = kept, swap_sides(send)
            return
        chips = lax.axis_size("rows")
        send, kept = halves(self.pair, 1 + self.left.index(bit), (lax.axis_index("rows") >> bit) & 1)
        self.pair = kept, lax.ppermute(send, "rows", [(n, n ^ (1 << bit)) for n in range(chips)])
        self.left.remove(bit)

    def total(self):
        while self.order:
            self.exchange()
        return self.pair[0] + self.pair[1].astype(f32)


def tied(shards, value, begin):
    which = 0 if begin else 1
    flat = [s.pair[which] for s in shards]
    flat, value = lax.optimization_barrier((flat, value))
    for s, new in zip(shards, flat):
        s.pair = (new, s.pair[1]) if begin else (s.pair[0], new)
    return value


def by_group(value):
    return value.reshape(-1, NG, GW).transpose(1, 0, 2)


def from_group(value):
    return value.transpose(1, 0, 2).reshape(-1, NG * GW)


def by_group_t(value):
    return value.T.reshape(NG, GW, -1)


def everyone(visit):
    side_count = lax.axis_size("mp")
    count = lax.axis_size("rows") * side_count
    me = lax.axis_index("rows") * side_count + lax.axis_index("mp")

    def body(step, carry):
        visit(step, lax.rem(me + step, count), lax.rem(me + count - step, count))
        return carry

    lax.fori_loop(1, count, body, 0)
    return me


def address(device):
    side_count = lax.axis_size("mp")
    return (device // side_count, lax.rem(device, side_count))


def meet_everyone():
    barrier = pltpu.get_barrier_semaphore()

    def greet(step, target, source):
        pl.semaphore_signal(
            barrier, inc=1, device_id=address(target), device_id_type=pl.DeviceIdType.MESH
        )

    everyone(greet)
    pl.semaphore_wait(barrier, lax.axis_size("rows") * lax.axis_size("mp") - 1)


def remote(source_ref, target_ref, send_sem, recv_sem, device):
    return pltpu.make_async_remote_copy(
        src_ref=source_ref,
        dst_ref=target_ref,
        send_sem=send_sem,
        recv_sem=recv_sem,
        device_id=address(device),
        device_id_type=pl.DeviceIdType.MESH,
    )


def gather_kernel(x_ref, out_ref, send_sem, recv_sem):
    count = out_ref.shape[0]
    side_count = lax.axis_size("mp")
    me = lax.axis_index("rows") * side_count + lax.axis_index("mp")
    meet_everyone()
    out_ref[me] = x_ref[...]

    def send(step, target, source):
        remote(x_ref, out_ref.at[me], send_sem.at[step], recv_sem.at[step], target).start()

    def wait(step, target, source):
        remote(x_ref, out_ref.at[source], send_sem.at[step], recv_sem.at[step], target).wait()

    everyone(send)
    everyone(wait)


def gather_small(block, count):
    return pl.pallas_call(
        gather_kernel,
        out_shape=jax.ShapeDtypeStruct((count, *block.shape), block.dtype),
        in_specs=[pl.BlockSpec(memory_space=pltpu.VMEM)],
        out_specs=pl.BlockSpec(memory_space=pltpu.VMEM),
        scratch_shapes=[pltpu.SemaphoreType.DMA((count,)), pltpu.SemaphoreType.DMA((count,))],
        compiler_params=pltpu.CompilerParams(
            collective_id=1, has_side_effects=True, vmem_limit_bytes=16 * MIB
        ),
        name="gather_small",
    )(block)


def sum_kernel(x_ref, out_ref, come_ref, send_sem, recv_sem):
    side_count = lax.axis_size("mp")
    me = lax.axis_index("rows") * side_count + lax.axis_index("mp")
    meet_everyone()

    def send(step, target, source):
        remote(x_ref.at[target], come_ref.at[step], send_sem.at[step], recv_sem.at[step], target).start()

    def wait(step, target, source):
        remote(x_ref.at[target], come_ref.at[step], send_sem.at[step], recv_sem.at[step], target).wait()

    everyone(send)
    come_ref[0] = x_ref[me]
    everyone(wait)
    out_ref[...] = jnp.sum(come_ref[...].astype(f32), axis=0)


def sum_small(blocks):
    count = blocks.shape[0]
    return pl.pallas_call(
        sum_kernel,
        out_shape=jax.ShapeDtypeStruct(blocks.shape[1:], f32),
        in_specs=[pl.BlockSpec(memory_space=pltpu.VMEM)],
        out_specs=pl.BlockSpec(memory_space=pltpu.VMEM),
        scratch_shapes=[
            pltpu.VMEM(blocks.shape, blocks.dtype),
            pltpu.SemaphoreType.DMA((count,)),
            pltpu.SemaphoreType.DMA((count,)),
        ],
        compiler_params=pltpu.CompilerParams(
            collective_id=2, has_side_effects=True, vmem_limit_bytes=16 * MIB
        ),
        name="sum_small",
    )(blocks)


def lay_tables(share, count):
    lane = np.arange(share * count)
    place = lane[None, :] % share == np.arange(share)[:, None]
    mark = lane[None, :] // share == np.arange(count)[:, None]
    return jnp.asarray(place, bf16), jnp.asarray(mark, f32)


def joined(shares):
    count, vectors, share = shares.shape
    place, mark = lay_tables(share, count)
    wide = dot(shares.reshape(count * vectors, share), place).reshape(count, vectors, count * share)
    return jnp.sum(wide * mark[:, None, :], axis=0)


def cut(vectors, share):
    number, size = vectors.shape
    place, mark = lay_tables(share, size // share)
    wide = (vectors[None] * mark[:, None, :]).astype(bf16)
    out = lax.dot_general(wide, place, (((2,), (1,)), ((), ())), preferred_element_type=f32)
    return out.astype(bf16)


def on_device(
    atoms,
    time_embedding,
    coordinates,
    item_lengths,
    item_group,
    query_weight,
    key_weight,
    value_weight,
    out_weight,
    up_weight,
    down_weight,
    value_bias,
    out_bias,
    up_bias,
    down_bias,
    first_gain,
    first_shift,
    second_gain,
    second_shift,
    kernel_params,
    cotangent,
):
    rows_here = atoms.shape[0]
    pair_size = lax.axis_size("mp")
    side = lax.axis_index("mp")
    pair_index = lax.axis_index("rows")
    group_rows = rows_here * pair_size
    counter = jnp.arange(rows_here, dtype=jnp.int32)
    near_rows = (pair_index * pair_size + side) * rows_here + counter
    far_rows = (pair_index * pair_size + 1 - side) * rows_here + counter
    items = item_lengths.shape[0]
    near_item, near_valid = row_items(near_rows, group_rows, item_lengths, item_group)
    far_item, far_valid = row_items(far_rows, group_rows, item_lengths, item_group)
    near_code = jnp.where(near_valid, near_item, items + near_rows)
    far_code = jnp.where(far_valid, far_item, items + far_rows)
    all_code = jnp.concatenate([near_code, far_code])
    picks = (
        (near_item[:, None] == jnp.arange(items, dtype=jnp.int32)[None, :]) & near_valid[:, None]
    ).astype(bf16)
    embed = jnp.dot(picks, time_embedding, preferred_element_type=f32)

    count = lax.axis_size("rows") * pair_size
    share, hidden = up_weight.shape
    width = query_weight.shape[1]
    blocks = hidden // width
    small = (value_bias, out_bias, down_bias, first_gain, first_shift, second_gain, second_shift)
    table_share = kernel_params.shape[0]
    block = jnp.concatenate(
        [
            jnp.pad(jnp.stack(small), ((0, 0), (0, 256 - share))),
            jnp.pad(up_bias.reshape(1, -1), ((0, 0), (0, 256 - blocks * share))),
            jnp.pad(kernel_params[None], ((0, 7), (0, 256 - table_share))),
        ]
    )
    gathered = gather_small(block, count)
    value_b, out_b, down_b, gain_one, shift_one, gain_two, shift_two = joined(gathered[:, :7, :share])
    up_b = joined(gathered[:, 7:8, : blocks * share])[0]
    table = joined(gathered[:, 8:9, :table_share])[0]
    wide = lax.all_gather(
        jnp.concatenate([query_weight, key_weight, value_weight, out_weight], axis=1), AXES, axis=0, tiled=True
    )
    stack = jnp.concatenate([up_weight[:, n * width : (n + 1) * width] for n in range(blocks)] + [down_weight], axis=0)
    stack = lax.all_gather(stack, AXES, axis=0, tiled=False)
    up_w = jnp.concatenate(
        [stack[:, n * share : (n + 1) * share].reshape(width, width) for n in range(blocks)], axis=1
    )
    down_w = stack[:, blocks * share :].reshape(hidden, width)

    means, widths, mix = table[:KERN], table[KERN : 2 * KERN], table[2 * KERN :].reshape(KERN, HEADS)
    norm = 1.0 / (widths * math.sqrt(2.0 * math.pi))
    curve = (-0.5 * math.log2(math.e)) / (widths * widths)
    mix_low = (mix * norm[:, None] * math.log2(math.e)).astype(bf16)
    coord_low = coordinates.astype(bf16)
    coord_all = jnp.concatenate([coord_low, swap_sides(coord_low)], axis=1).astype(f32)
    near = coordinates.astype(f32).T
    bias, phi = pair_bias(near, coord_all, near_code[:, None], all_code[None], means, curve, mix_low)

    bias, wide = lax.optimization_barrier((bias, wide))
    query_w, key_w, value_w, out_w = [wide[:, n * width : (n + 1) * width] for n in range(4)]
    h_zero = atoms.astype(f32) + embed
    normed, pull_one = jax.vjp(layer_norm, h_zero, gain_one, shift_one)
    normed_low = normed.astype(bf16)
    query = jnp.dot(normed_low, query_w, preferred_element_type=f32).astype(bf16)
    keys = jnp.dot(normed_low, key_w, preferred_element_type=f32).astype(bf16)
    values = (jnp.dot(normed_low, value_w, preferred_element_type=f32) + value_b).astype(bf16)
    keys_all = jnp.concatenate([keys, swap_sides(keys)], axis=0)
    values_all = jnp.concatenate([values, swap_sides(values)], axis=0)
    q4, k4, v4 = by_group(query), by_group(keys_all), by_group(values_all)
    kt4, vt4 = by_group_t(keys_all), by_group_t(values_all)
    ones = jnp.ones((NG, group_rows, 1), bf16)
    vx4 = jnp.concatenate([v4, ones, jnp.zeros((NG, group_rows, 256 - GW - 1), bf16)], axis=2)
    expo, mixed4, inverse4 = attend(q4, kt4, vx4, bias)
    mixed = from_group(mixed4.astype(bf16))

    h_one = h_zero + jnp.dot(mixed, out_w, preferred_element_type=f32) + out_b
    second, pull_two = jax.vjp(layer_norm, h_one, gain_two, shift_two)
    second_low = second.astype(bf16)
    up_pre = jnp.dot(second_low, up_w, preferred_element_type=f32) + up_b
    below = 0.5 + 0.5 * lax.erf(up_pre * (2.0**-0.5))
    act_low = (up_pre * below).astype(bf16)
    slope = (below + up_pre * jnp.exp(-0.5 * up_pre * up_pre) * (2.0 * math.pi) ** -0.5).astype(bf16)
    h_two = h_one + jnp.dot(act_low, down_w, preferred_element_type=f32) + down_b
    layer_out = jnp.where(near_valid[:, None], h_two, 0.0).astype(bf16)

    grad_two = jnp.where(near_valid[:, None], cotangent.astype(f32), 0.0)
    grad_ffn = grad_two.astype(bf16)
    down_bias_grad = col_sum(grad_ffn)
    down_shards = Shards(left_dot(act_low, grad_ffn)[None], (0, 1))
    down_shards.exchange()
    grad_up = (right_dot(grad_ffn, down_w) * slope.astype(f32)).astype(bf16)
    up_bias_grad = col_sum(grad_up)
    up_shards = Shards(left_dot(second_low, grad_up)[None], (1, 0))
    up_shards.exchange()
    grad_part, second_gain_grad, second_shift_grad = pull_two(right_dot(grad_up, up_w))
    grad_one = grad_two + grad_part
    grad_att = grad_one.astype(bf16)
    out_bias_grad = col_sum(grad_att)
    out_weight_grad = left_dot(mixed, grad_att)
    grad_mixed = right_dot(grad_att, out_w).astype(bf16)
    scaled4 = (by_group(grad_mixed).astype(f32) * inverse4).astype(bf16)
    down_shards.exchange()
    up_shards.exchange()

    half = NG // 2
    done = []
    for n in range(2):
        scaled4 = tied((down_shards, up_shards), scaled4, begin=True)
        done.append(attend_back(q4, scaled4, mixed4, k4, vt4, expo, n * half, half))
        if n == 0:
            scaled4 = tied((down_shards, up_shards), (scaled4, done[0]), begin=False)[0]
            down_shards.exchange()
            up_shards.exchange()
    scores_grad = [d[0] for d in done]
    dq4, dkt, dvt = [jnp.concatenate([d[m] for d in done], axis=0) for m in (1, 2, 3)]
    dq4, dkt, dvt = tied((down_shards, up_shards), (dq4, dkt, dvt), begin=False)
    down_shards.exchange()
    up_shards.exchange()

    grad_query = from_group(dq4)
    dkt = dkt.reshape(-1, group_rows) * (HEAD**-0.5)
    dvt = dvt.reshape(-1, group_rows)
    back_keys = swap_sides(dkt[:, rows_here:].astype(bf16)).astype(f32)
    back_values = swap_sides(dvt[:, rows_here:].astype(bf16)).astype(f32)
    grad_keys = (dkt[:, :rows_here] + back_keys).astype(bf16).T
    grad_values = (dvt[:, :rows_here] + back_values).astype(bf16).T
    value_bias_grad = col_sum(grad_values)
    square_shards = Shards(
        jnp.stack(
            [
                left_dot(normed_low, grad_query),
                left_dot(normed_low, grad_keys),
                left_dot(normed_low, grad_values),
                out_weight_grad,
            ]
        ),
        (0, 1),
    )
    square_shards.exchange()
    grad_normed = (
        right_dot(grad_query, query_w) + right_dot(grad_keys, key_w) + right_dot(grad_values, value_w)
    )
    grad_zero, first_gain_grad, first_shift_grad = pull_one(grad_normed)
    atoms_grad = grad_one + grad_zero

    tiles = rows_here // 32
    pieces = 4
    moments = 0.0
    square_shards.exchange()
    down_shards.exchange()
    up_shards.exchange()
    shards = (square_shards, down_shards, up_shards)
    for n in range(pieces):
        near = tied(shards, (near, atoms_grad), begin=True)[0]
        piece = bias_back(near, coord_all, means, curve, scores_grad, phi, n * tiles // pieces, tiles // pieces)
        piece = tied(shards, piece, begin=False)
        for s in shards:
            s.exchange()
        moments = moments + piece
    zeroth = moments[:HEADS].T * norm[:, None]
    first = (moments[HEADS : 2 * HEADS] + moments[2 * HEADS : 3 * HEADS]).T * norm[:, None]
    twice = (moments[3 * HEADS : 4 * HEADS] + moments[4 * HEADS :]).T * norm[:, None]
    m_zero, m_one, m_two = [jnp.sum(mix * r, axis=1) for r in (zeroth, first, twice)]
    offset = means - CENTRE
    mean_grad = (m_one - offset * m_zero) / widths**2
    width_grad = (m_two - 2.0 * offset * m_one + offset * offset * m_zero) / widths**3 - m_zero / widths
    table_grad = jnp.concatenate([mean_grad, width_grad, zeroth.reshape(-1)])

    cuts = jnp.concatenate(
        [
            jnp.pad(
                cut(
                    jnp.stack(
                        [
                            value_bias_grad,
                            out_bias_grad,
                            down_bias_grad,
                            first_gain_grad,
                            first_shift_grad,
                            second_gain_grad,
                            second_shift_grad,
                        ]
                    ),
                    share,
                ),
                ((0, 0), (0, 0), (0, 256 - share)),
            ),
            jnp.pad(cut(up_bias_grad[None], blocks * share), ((0, 0), (0, 0), (0, 256 - blocks * share))),
            jnp.pad(cut(table_grad[None], table_share), ((0, 0), (0, 7), (0, 256 - table_share))),
        ],
        axis=1,
    )
    sums = sum_small(cuts)
    square_sum = square_shards.total()
    return (
        layer_out,
        atoms_grad,
        square_sum[0],
        square_sum[1],
        square_sum[2],
        square_sum[3],
        up_shards.total()[0],
        down_shards.total()[0],
        sums[0, :share],
        sums[1, :share],
        sums[7, : blocks * share],
        sums[2, :share],
        sums[3, :share],
        sums[4, :share],
        sums[5, :share],
        sums[6, :share],
        sums[8, :table_share],
    )


def solution(mesh):
    row = P(AXES, None)
    vec = P(AXES)
    in_specs = (row, P(), P(None, AXES), P(), P(), *[row] * 6, *[vec] * 9, row)
    out_specs = (*[row] * 8, *[vec] * 9)
    return jax.shard_map(on_device, mesh=mesh, in_specs=in_specs, out_specs=out_specs, check_vma=False)
```

```python
import functools
import math

import jax
import jax.numpy as jnp
import numpy as np
from jax import lax
from jax.experimental import pallas as pl
from jax.experimental.pallas import tpu as pltpu
from jax.sharding import PartitionSpec as P

HEADS = 32
KERN = 128
HEAD = 24
GH = 8
NG = HEADS // GH
GW = GH * HEAD
MIB = 2**20
CENTRE = 6.0
STORED = 1
AXES = ("rows", "mp")
f32 = jnp.float32
bf16 = jnp.bfloat16


def dot(left, right):
    return jnp.dot(left, right, preferred_element_type=f32)


def turned_dot(left, right):
    return lax.dot_general(left, right, (((1,), (1,)), ((), ())), preferred_element_type=f32)


def sum_dot(left, right):
    return lax.dot_general(left, right, (((0,), (0,)), ((), ())), preferred_element_type=f32)


def whole(shape):
    return pl.BlockSpec(shape, lambda i: (0,) * len(shape))


def after(kernel, inputs, tokens):
    def run(*refs):
        kernel(*refs[:inputs], *refs[inputs + len(tokens) :])

    return run, [pl.BlockSpec(memory_space=pl.ANY)] * len(tokens)


def high_low(value):
    high = value.astype(bf16)
    return high, (value - high.astype(f32)).astype(bf16)


def distances(near_ref, all_ref):
    total = None
    for c in range(3):
        diff = near_ref[:, c : c + 1] - all_ref[c : c + 1, :]
        total = diff * diff if total is None else total + diff * diff
    return jnp.sqrt(total) * 0.25


def bias_kernel(
    pairs_step, near_ref, all_ref, code_near_ref, code_all_ref, means_ref, curve_ref, mix_ref,
    bias_ref, phi_ref, dist_ref, mask_ref,
):
    dist_ref[...] = distances(near_ref, all_ref)
    mask_ref[...] = jnp.where(code_near_ref[:, 0:1] == code_all_ref[0:1, :], 0.0, -1e30)
    rows, span = dist_ref.shape

    def body(step, carry):
        for q in range(pairs_step):
            pair = step * pairs_step + q
            drow = [dist_ref[pl.ds(pair * 2 + e, 1), :] for e in range(2)]
            mrow = [mask_ref[pl.ds(pair * 2 + e, 1), :] for e in range(2)]
            for lane in range(0, span, 256):
                tall = []
                for e in range(2):
                    wide = []
                    for low in (lane, lane + 128):
                        u = drow[e][:, low : low + 128] - means_ref[...]
                        wide.append(jnp.exp2((u * curve_ref[...]) * u).astype(bf16))
                    wide = jnp.concatenate(wide, axis=1)
                    if e < STORED:
                        phi_ref[pair * STORED + e, :, lane : lane + 256] = wide
                    tall.append(wide)
                out = dot(mix_ref[...], jnp.concatenate(tall, axis=0)).reshape(NG, 2, GH, 256)
                out = jnp.concatenate(
                    [out[:, e : e + 1] + mrow[e][:, lane : lane + 256].reshape(1, 1, 1, 256) for e in range(2)],
                    axis=1,
                )
                bias_ref[:, pl.ds(pl.multiple_of(pair * 16, 16), 16), lane : lane + 256] = out.reshape(
                    NG, 16, 256
                ).astype(bf16)
        return carry

    lax.fori_loop(0, rows // 2 // pairs_step, body, 0)


def lane_wide(values):
    return jnp.broadcast_to(values[:, None], (KERN, 128))


def pair_bias(near, coord_all, code_near, code_all, means, curve, mix_low, tile=32, pairs_step=8):
    rows, span = near.shape[0], coord_all.shape[1]
    m4 = mix_low.T.reshape(NG, GH, KERN)
    zero = jnp.zeros_like(m4)
    left = jnp.stack([jnp.concatenate([m4, zero], -1), jnp.concatenate([zero, m4], -1)], axis=1)
    left = left.reshape(2 * HEADS, 2 * KERN)
    return pl.pallas_call(
        functools.partial(bias_kernel, pairs_step),
        grid=(rows // tile,),
        in_specs=[
            pl.BlockSpec((tile, 3), lambda i: (i, 0)),
            whole((3, span)),
            pl.BlockSpec((tile, 1), lambda i: (i, 0)),
            whole((1, span)),
            whole((KERN, 128)),
            whole((KERN, 128)),
            whole((2 * HEADS, 2 * KERN)),
        ],
        out_specs=[
            pl.BlockSpec((NG, tile * GH, span), lambda i: (0, i, 0)),
            pl.BlockSpec((tile * STORED // 2, KERN, span), lambda i: (i, 0, 0)),
        ],
        out_shape=[
            jax.ShapeDtypeStruct((NG, rows * GH, span), bf16),
            jax.ShapeDtypeStruct((rows * STORED // 2, KERN, span), bf16),
        ],
        scratch_shapes=[pltpu.VMEM((tile, span), f32), pltpu.VMEM((tile, span), f32)],
        compiler_params=pltpu.CompilerParams(vmem_limit_bytes=50 * MIB),
        cost_estimate=pl.CostEstimate(flops=rows * 140 * 10**6, bytes_accessed=MIB, transcendentals=0),
        name="bias",
    )(near, coord_all, code_near, code_all, lane_wide(means), lane_wide(curve), left)


def repeat_tables(tile):
    row = np.arange(tile * GH)
    repeat = row[:, None] // GH == np.arange(tile)[None, :]
    own = row[:, None] % GH == np.arange(GW)[None, :] // HEAD
    return repeat, own


def project_kernel(
    atoms_ref, code_ref, time_ref, gain_ref, shift_ref, bias_ref, wide_ref,
    h_ref, q_ref, k_ref, v_ref,
):
    width = atoms_ref.shape[1]
    items = lax.broadcasted_iota(jnp.int32, (1, time_ref.shape[0]), 1)
    picks = (code_ref[...] == items).astype(f32).astype(bf16)
    h_zero = atoms_ref[...].astype(f32) + dot(picks, time_ref[...])
    h_ref[...] = h_zero
    centre = h_zero - jnp.mean(h_zero, axis=1, keepdims=True)
    rate = lax.rsqrt(jnp.mean(centre * centre, axis=1, keepdims=True) + 1e-05)
    normed = (centre * rate * gain_ref[...] + shift_ref[...]).astype(bf16)
    tile = h_zero.shape[0]
    lane = lax.broadcasted_iota(jnp.int32, (tile, 256 - GW), 1)
    ones = jnp.where(lane == 0, 1.0, 0.0)
    for n, out_ref in ((1, k_ref), (2, v_ref), (0, q_ref)):
        out = dot(normed, wide_ref[:, n * width : (n + 1) * width])
        if n == 2:
            out = out + bias_ref[...]
        for g in range(NG):
            part = out[:, g * GW : (g + 1) * GW]
            if n == 2:
                part = jnp.concatenate([part, ones], axis=1)
            out_ref[g] = part.astype(bf16)


def project(atoms, code, time_embedding, gain, shift, value_bias, wide, tile=256):
    rows, width = atoms.shape
    return pl.pallas_call(
        project_kernel,
        grid=(rows // tile,),
        in_specs=[
            pl.BlockSpec((tile, width), lambda i: (i, 0)),
            pl.BlockSpec((tile, 1), lambda i: (i, 0)),
            whole(time_embedding.shape),
            *[whole((1, width))] * 3,
            whole((width, 3 * width)),
        ],
        out_specs=[
            pl.BlockSpec((tile, width), lambda i: (i, 0)),
            *[pl.BlockSpec((NG, tile, GW), lambda i: (0, i, 0))] * 2,
            pl.BlockSpec((NG, tile, 256), lambda i: (0, i, 0)),
        ],
        out_shape=[
            jax.ShapeDtypeStruct((rows, width), f32),
            *[jax.ShapeDtypeStruct((NG, rows, GW), bf16)] * 2,
            jax.ShapeDtypeStruct((NG, rows, 256), bf16),
        ],
        compiler_params=pltpu.CompilerParams(vmem_limit_bytes=40 * MIB),
        cost_estimate=pl.CostEstimate(flops=rows * 16 * 10**6, bytes_accessed=MIB, transcendentals=0),
        name="project",
    )(atoms, code, time_embedding, gain[None], shift[None], value_bias[None], wide)


def project_back_kernel(
    h_ref, grad_one_ref, q0_ref, q1_ref, k0_ref, k1_ref, v0_ref, v1_ref, kc0_ref, kc1_ref, vc0_ref, vc1_ref,
    gain_ref, shift_ref, wide_ref, out_grad_ref,
    atoms_grad_ref, grads_ref, sums_ref, normed_s, grad_s,
):
    rows, width = h_ref.shape
    for g in range(NG):
        q_ref, k_ref, v_ref, kc_ref, vc_ref = (
            (q0_ref, k0_ref, v0_ref, kc0_ref, vc0_ref) if g < NG // 2 else (q1_ref, k1_ref, v1_ref, kc1_ref, vc1_ref)
        )
        m = g % (NG // 2)
        cols = slice(g * GW, (g + 1) * GW)
        grad_s[0, :, cols] = q_ref[m]
        grad_s[1, :, cols] = (k_ref[m] + kc_ref[m].astype(f32)).T.astype(bf16)
        grad_s[2, :, cols] = (v_ref[m] + vc_ref[m].astype(f32)).T.astype(bf16)
    h_zero = h_ref[...]
    centre = h_zero - jnp.mean(h_zero, axis=1, keepdims=True)
    rate = lax.rsqrt(jnp.mean(centre * centre, axis=1, keepdims=True) + 1e-05)
    hat = centre * rate
    normed_s[...] = (hat * gain_ref[...] + shift_ref[...]).astype(bf16)
    grads_ref[3] = out_grad_ref[...]
    grad = None
    for n in range(3):
        grads_ref[n] = sum_dot(normed_s[...], grad_s[n]).astype(bf16)
        part = turned_dot(grad_s[n], wide_ref[:, n * width : (n + 1) * width])
        grad = part if grad is None else grad + part
    g = grad * gain_ref[...]
    atoms_grad_ref[...] = grad_one_ref[...] + rate * (
        g - jnp.mean(g, axis=1, keepdims=True) - hat * jnp.mean(g * hat, axis=1, keepdims=True)
    )
    sums_ref[...] = jnp.zeros_like(sums_ref)
    sums_ref[0:1, :] = jnp.sum(grad * hat, axis=0, keepdims=True)
    sums_ref[1:2, :] = jnp.sum(grad, axis=0, keepdims=True)
    sums_ref[2:3, :] = dot(jnp.ones((8, rows), bf16), grad_s[2])[0:1]


def project_back(h_zero, grad_one, pairs, gain, shift, wide, out_grad, tokens=()):
    rows, width = h_zero.shape
    once = pl.Buffered(1)
    kernel, token_specs = after(project_back_kernel, 16, tokens)
    return pl.pallas_call(
        kernel,
        grid=(1,),
        in_specs=[
            whole((rows, width)),
            whole((rows, width)),
            *[whole(p.shape) for p in pairs],
            *[whole((1, width))] * 2,
            pl.BlockSpec((width, 3 * width), lambda i: (0, 0), pipeline_mode=once),
            whole((width, width)),
            *token_specs,
        ],
        out_specs=[whole((rows, width)), whole((NG, width, width)), whole((8, width))],
        out_shape=[
            jax.ShapeDtypeStruct((rows, width), f32),
            jax.ShapeDtypeStruct((4, width, width), bf16),
            jax.ShapeDtypeStruct((8, width), f32),
        ],
        scratch_shapes=[pltpu.VMEM((rows, width), bf16), pltpu.VMEM((3, rows, width), bf16)],
        compiler_params=pltpu.CompilerParams(vmem_limit_bytes=56 * MIB),
        cost_estimate=pl.CostEstimate(flops=rows * 30 * 10**6, bytes_accessed=MIB, transcendentals=0),
        name="project_back",
    )(h_zero, grad_one, *pairs, gain[None], shift[None], wide, out_grad, *tokens)


def attend_kernel(
    tiles, q_ref, k0_ref, k1_ref, v0_ref, v1_ref, b_ref, rep_ref, rept_ref, own_ref, scaled_ref,
    e_ref, mixed_ref, inv_ref, qa, qb, sa, sb, ea, oa, ob, wa, wb,
):
    keys, values = (k0_ref, k1_ref), (v0_ref, v1_ref)
    query, scores, outs, wides = (qa, qb), (sa, sb), (oa, ob), (wa, wb)
    rows, span = sa.shape
    held = rows // GH
    units = NG * tiles
    parts, chunk, ahead = 4, 8, 3
    step, some = span // parts, rows // parts
    pid = pl.program_id(0)

    def place(unit):
        unit = jnp.clip(unit, 0, units - 1)
        group = unit // tiles
        return group, pl.ds(pl.multiple_of((unit - group * tiles) * held, held), held)

    def spread(unit, par):
        g, i = place(unit)
        query[par][...] = (dot(rep_ref[...], q_ref[g, i, :]) * scaled_ref[...]).astype(bf16)

    def score(unit, par, part):
        g, _ = place(unit)
        cols = slice(part * step, (part + 1) * step)
        there = slice(part % 2 * step, (part % 2 + 1) * step)
        scores[par][:, cols] = turned_dot(query[par][...], keys[part // 2][g, there, :])

    def soften(par, part):
        chunks = range(part * some, (part + 1) * some, chunk)
        held_x = {}
        for n in range(len(chunks) + ahead):
            if n < len(chunks):
                here = slice(chunks[n], chunks[n] + chunk)
                x = scores[par][here, :] + b_ref[par, here, :].astype(f32)
                held_x[n] = x, jnp.max(x, axis=1, keepdims=True)
            if n >= ahead:
                here = slice(chunks[n - ahead], chunks[n - ahead] + chunk)
                x, top = held_x.pop(n - ahead)
                e = jnp.exp2(x - top).astype(bf16)
                e_ref[par, here, :] = e
                if par == 1:
                    ea[here, :] = e

    def mix(unit, par, part):
        g, _ = place(unit)
        here = slice(part * some, (part + 1) * some)
        source = e_ref.at[0] if par == 0 else ea
        half = span // 2
        outs[par][here, :] = dot(source[here, :half], v0_ref[g]) + dot(source[here, half:], v1_ref[g])

    def scale(par, part):
        here = slice(part * some, (part + 1) * some)
        out = outs[par][here, :]
        inv = 1.0 / out[:, GW : GW + 1]
        own = own_ref[here, :]
        wides[par][here, :] = jnp.concatenate(
            [*high_low(out[:, :GW] * inv * own), *high_low(inv * own)], axis=1
        )

    def gather(unit, par):
        g, i = place(unit)
        out = dot(rept_ref[...], wides[par][...])
        mixed_ref[g, i, :] = out[:, :GW] + out[:, GW : 2 * GW]
        inv_ref[g, i, :] = out[:, 2 * GW : 3 * GW] + out[:, 3 * GW :]

    @pl.when(pid == 0)
    def _():
        spread(0, 0)
        for part in range(parts):
            score(0, 0, part)
        spread(1, 1)
        ea[...] = jnp.ones_like(ea)
        for ref in (oa, ob):
            ref[...] = jnp.ones_like(ref)
        for ref in (wa, wb):
            ref[...] = jnp.zeros_like(ref)

    for par in range(2):
        unit = pid * 2 + par
        gather(unit - 3, 1 - par)
        for part in range(parts):
            score(unit + 1, 1 - par, part)
            scale(par, part)
            mix(unit - 1, 1 - par, part)
            soften(par, part)
        spread(unit + 2, par)

    @pl.when(pid == units // 2 - 1)
    def _():
        for part in range(parts):
            scale(0, part)
            mix(units - 1, 1, part)
        gather(units - 3, 1)
        gather(units - 2, 0)
        for part in range(parts):
            scale(1, part)
        gather(units - 1, 1)


def attend(q4, keys, values, bias, tile=64):
    rows = q4.shape[1]
    span = 2 * rows
    tiles = rows // tile
    repeat, own = repeat_tables(tile)
    deep = tile * GH
    bias = bias.reshape(NG * tiles, deep, span)
    big = pl.BlockSpec((2, deep, span), lambda i: (i, 0, 0))
    scale = HEAD**-0.5 * math.log2(math.e)
    e, mixed, inv = pl.pallas_call(
        functools.partial(attend_kernel, tiles),
        grid=(NG * tiles // 2,),
        in_specs=[
            whole((NG, rows, GW)),
            *[whole((NG, rows, GW))] * 2,
            *[whole((NG, rows, 256))] * 2,
            big,
            whole((deep, tile)),
            whole((tile, deep)),
            whole((deep, GW)),
            whole((deep, GW)),
        ],
        out_specs=[big, whole((NG, rows, GW)), whole((NG, rows, GW))],
        out_shape=[
            jax.ShapeDtypeStruct((NG * tiles, deep, span), bf16),
            jax.ShapeDtypeStruct((NG, rows, GW), f32),
            jax.ShapeDtypeStruct((NG, rows, GW), f32),
        ],
        scratch_shapes=[pltpu.VMEM((deep, GW), bf16)] * 2
        + [pltpu.VMEM((deep, span), f32)] * 2
        + [pltpu.VMEM((deep, span), bf16)]
        + [pltpu.VMEM((deep, 256), f32)] * 2
        + [pltpu.VMEM((deep, 4 * GW), bf16)] * 2,
        compiler_params=pltpu.CompilerParams(vmem_limit_bytes=50 * MIB),
        cost_estimate=pl.CostEstimate(flops=rows * 100 * 10**6, bytes_accessed=MIB, transcendentals=0),
        name="attend",
    )(
        q4, *keys, *values, bias, jnp.asarray(repeat, bf16), jnp.asarray(repeat.T, bf16),
        jnp.asarray(own, f32), jnp.asarray(own * scale, f32),
    )
    return e.reshape(NG, rows * GH, span), mixed, inv


def attend_back_kernel(
    tiles, q_ref, gs_ref, mx_ref, k0_ref, k1_ref, v0_ref, v1_ref, e_ref, rep_ref, rept_ref, own_ref, ownt_ref,
    ds_ref, dq_ref, dk_near_ref, dk_far_ref, dv_near_ref, dv_far_ref,
    ga, gb, da, db, qta, qtb, gta, gtb, sa, sb, kept, oa, ob, wa, wb, dk, dv,
):
    keys, values = (k0_ref, k1_ref), (v0_ref, v1_ref)
    grads, deltas, queries_t, grads_t = (ga, gb), (da, db), (qta, qtb), (gta, gtb)
    scores, outs, wides = (sa, sb), (oa, ob), (wa, wb)
    deep, span = sa.shape
    held = deep // GH
    units = q_ref.shape[0] * tiles
    parts, chunk = 4, 8
    step, some = span // parts, deep // parts
    scale = HEAD**-0.5
    pid = pl.program_id(0)

    def place(unit):
        unit = jnp.clip(unit, 0, units - 1)
        group = unit // tiles
        return group, pl.ds(pl.multiple_of((unit - group * tiles) * held, held), held)

    def begin(unit, par):
        g, i = place(unit)
        gs = gs_ref[g, i, :]
        high, low = high_low(gs.astype(f32) * mx_ref[g, i, :])
        wide = dot(rep_ref[...], jnp.concatenate([gs, high, low], axis=1))
        own = own_ref[...]
        grads[par][...] = (wide[:, :GW] * own).astype(bf16)
        deltas[par][...] = jnp.sum((wide[:, GW : 2 * GW] + wide[:, 2 * GW :]) * own, axis=1, keepdims=True)
        grads_t[par][...] = (sum_dot(gs, rept_ref[...]) * ownt_ref[...]).astype(bf16)

    def turn_query(unit, par):
        g, i = place(unit)
        queries_t[par][...] = (sum_dot(q_ref[g, i, :], rept_ref[...]) * ownt_ref[...]).astype(bf16)

    def grad_probs(unit, par, part):
        g, _ = place(unit)
        cols = slice(part * step, (part + 1) * step)
        there = slice(part % 2 * step, (part % 2 + 1) * step)
        scores[par][:, cols] = turned_dot(grads[par][...], values[part // 2][g, there, :GW])

    def soften(par, part):
        for c in range(part * some, (part + 1) * some, chunk):
            here = slice(c, c + chunk)
            ds = (e_ref[par, here, :].astype(f32) * (scores[par][here, :] - deltas[par][here, :])).astype(bf16)
            ds_ref[par, here, :] = ds
            if par == 1:
                kept[here, :] = ds

    def value_grad(unit, par, part):
        g, _ = place(unit)
        cols = slice(part * step, (part + 1) * step)
        dv[g, :, cols] += dot(grads_t[par][...], e_ref[par, :, cols])

    def key_grad(unit, par, part):
        g, _ = place(unit)
        cols = slice(part * step, (part + 1) * step)
        source = ds_ref.at[0] if par == 0 else kept
        dk[g, :, cols] += dot(queries_t[par][...], source[:, cols])

    def query_grad(unit, par, part):
        g, _ = place(unit)
        here = slice(part * some, (part + 1) * some)
        source = ds_ref.at[0] if par == 0 else kept
        half = span // 2
        outs[par][here, :] = dot(source[here, :half], k0_ref[g]) + dot(source[here, half:], k1_ref[g])

    def mask(par):
        wides[par][...] = (outs[par][...] * own_ref[...]).astype(bf16)

    def gather(unit, par):
        g, i = place(unit)
        dq_ref[g, i, :] = (dot(rept_ref[...], wides[par][...]) * scale).astype(bf16)

    @pl.when(pid == 0)
    def _():
        dk[...] = jnp.zeros_like(dk)
        dv[...] = jnp.zeros_like(dv)
        begin(0, 0)
        for part in range(parts):
            grad_probs(0, 0, part)
        begin(1, 1)
        queries_t[1][...] = jnp.zeros_like(queries_t[1])
        kept[...] = jnp.zeros_like(kept)
        for ref in (oa, ob, wa, wb):
            ref[...] = jnp.zeros_like(ref)

    for par in range(2):
        unit = pid * 2 + par
        gather(unit - 3, 1 - par)
        mask(par)
        for part in range(parts):
            grad_probs(unit + 1, 1 - par, part)
            value_grad(unit, par, part)
            key_grad(unit - 1, 1 - par, part)
            query_grad(unit - 1, 1 - par, part)
            soften(par, part)
        turn_query(unit, par)
        begin(unit + 2, par)

    @pl.when(pid == units // 2 - 1)
    def _():
        last = units - 1
        gather(last - 2, 1)
        mask(0)
        for part in range(parts):
            key_grad(last, 1, part)
            query_grad(last, 1, part)
        gather(last - 1, 0)
        mask(1)
        gather(last, 1)
        half = span // 2
        dk_near_ref[...] = dk[:, :, :half] * scale
        dk_far_ref[...] = (dk[:, :, half:] * scale).astype(bf16)
        dv_near_ref[...] = dv[:, :, :half]
        dv_far_ref[...] = dv[:, :, half:].astype(bf16)


def attend_back(q4, gs4, mx4, keys, values, e, first, groups, tokens=(), tile=64):
    rows = q4.shape[1]
    span = 2 * rows
    tiles = rows // tile
    deep = tile * GH
    repeat, own = repeat_tables(tile)
    e = e.reshape(NG * tiles, deep, span)
    block = first // groups
    ahead = first * tiles // 2
    held = lambda wide: pl.BlockSpec((groups, rows, wide), lambda i: (block, 0, 0))
    near = jax.ShapeDtypeStruct((groups, GW, rows), f32)
    far = jax.ShapeDtypeStruct((groups, GW, rows), bf16)
    kernel, token_specs = after(functools.partial(attend_back_kernel, tiles), 12, tokens)
    ds, *rest = pl.pallas_call(
        kernel,
        grid=(groups * tiles // 2,),
        in_specs=[
            *[held(GW)] * 5,
            *[held(256)] * 2,
            pl.BlockSpec((2, deep, span), lambda i: (i + ahead, 0, 0)),
            whole((deep, tile)),
            whole((tile, deep)),
            whole((deep, GW)),
            whole((GW, deep)),
            *token_specs,
        ],
        out_specs=[
            pl.BlockSpec((2, deep, span), lambda i: (i, 0, 0)),
            whole((groups, rows, GW)),
            *[whole((groups, GW, rows))] * 4,
        ],
        out_shape=[
            jax.ShapeDtypeStruct((groups * tiles, deep, span), bf16),
            jax.ShapeDtypeStruct((groups, rows, GW), bf16),
            near,
            far,
            near,
            far,
        ],
        scratch_shapes=[pltpu.VMEM((deep, GW), bf16)] * 2
        + [pltpu.VMEM((deep, 1), f32)] * 2
        + [pltpu.VMEM((GW, deep), bf16)] * 4
        + [pltpu.VMEM((deep, span), f32)] * 2
        + [pltpu.VMEM((deep, span), bf16)]
        + [pltpu.VMEM((deep, GW), f32)] * 2
        + [pltpu.VMEM((deep, GW), bf16)] * 2
        + [pltpu.VMEM((groups, GW, span), f32)] * 2,
        compiler_params=pltpu.CompilerParams(vmem_limit_bytes=50 * MIB),
        cost_estimate=pl.CostEstimate(flops=rows * groups * 40 * 10**6, bytes_accessed=MIB, transcendentals=0),
        name="attend_back",
    )(
        q4, gs4, mx4, *keys, *values, e, jnp.asarray(repeat, bf16), jnp.asarray(repeat.T, bf16),
        jnp.asarray(own, f32), jnp.asarray(own.T, f32), *tokens,
    )
    return (ds.reshape(groups, rows * GH, span), *rest)


def feed_kernel(
    row_steps, h_ref, mixed_ref, inv_ref, valid_ref, cot_ref, out_w_ref, up_w_ref, down_w_ref,
    out_b_ref, up_b_ref, down_b_ref, gain_ref, shift_ref,
    layer_ref, grad_one_ref, gs_ref, down_grad_ref, up_grad_ref, out_grad_ref, sums_ref, up_sums_ref,
    act_s, gup_s, second_s, gatt_s, gffn_s, mixed_s, up_s, gact_s,
):
    step = pl.program_id(0)
    tile, width = h_ref.shape
    hidden = up_w_ref.shape[1]
    some = 32

    @pl.when(step == 0)
    def _():
        sums_ref[...] = jnp.zeros_like(sums_ref)

    @pl.when(step < row_steps)
    def _():
        here = pl.ds(pl.multiple_of(step * tile, tile), tile)
        h_one = h_ref[...] + out_b_ref[...]
        for g in range(NG):
            mixed = mixed_ref[g].astype(bf16)
            mixed_s[g, here, :] = mixed
            h_one = h_one + dot(mixed, out_w_ref[g * GW : (g + 1) * GW, :])
        centre = h_one - jnp.mean(h_one, axis=1, keepdims=True)
        rate = lax.rsqrt(jnp.mean(centre * centre, axis=1, keepdims=True) + 1e-05)
        second = (centre * rate * gain_ref[...] + shift_ref[...]).astype(bf16)
        second_s[here, :] = second
        grad_two = cot_ref[...].astype(f32) * valid_ref[...]
        grad_ffn = grad_two.astype(bf16)
        gffn_s[here, :] = grad_ffn
        h_two = h_one + down_b_ref[...]
        grad_second = None
        for low in range(0, hidden, width):
            cols = slice(low, low + width)
            up_s[...] = dot(second, up_w_ref[:, cols]) + up_b_ref[:, cols]
            gact_s[...] = turned_dot(grad_ffn, down_w_ref[cols, :])

            def bend(n, carry):
                rows = pl.ds(pl.multiple_of(n * some, some), some)
                at = pl.ds(pl.multiple_of(step * tile + n * some, some), some)
                up = up_s[rows, :]
                below = 0.5 + 0.5 * lax.erf(up * (2.0**-0.5))
                slope = below + up * (jnp.exp(-0.5 * up * up) * (2.0 * math.pi) ** -0.5)
                act_s[at, cols] = (up * below).astype(bf16)
                gup_s[at, cols] = (gact_s[rows, :] * slope).astype(bf16)
                return carry

            lax.fori_loop(0, tile // some, bend, 0)
            h_two = h_two + dot(act_s[here, cols], down_w_ref[cols, :])
            part = turned_dot(gup_s[here, cols], up_w_ref[:, cols])
            grad_second = part if grad_second is None else grad_second + part
        layer_ref[...] = (h_two * valid_ref[...]).astype(bf16)
        hat = centre * rate
        sums_ref[0:1, :] += jnp.sum(grad_second * hat, axis=0, keepdims=True)
        sums_ref[1:2, :] += jnp.sum(grad_second, axis=0, keepdims=True)
        g = grad_second * gain_ref[...]
        grad_one = grad_two + rate * (
            g - jnp.mean(g, axis=1, keepdims=True) - hat * jnp.mean(g * hat, axis=1, keepdims=True)
        )
        grad_one_ref[...] = grad_one
        grad_att = grad_one.astype(bf16)
        gatt_s[here, :] = grad_att
        for g in range(NG):
            grad_mixed = turned_dot(grad_att, out_w_ref[g * GW : (g + 1) * GW, :]).astype(bf16)
            gs_ref[g] = (grad_mixed.astype(f32) * inv_ref[g]).astype(bf16)

    for n in range(WEIGHT_STEPS):

        @pl.when(step == row_steps + n)
        def _():
            size = hidden // WEIGHT_STEPS
            cols = slice(n * size, (n + 1) * size)
            down_grad_ref[...] = sum_dot(act_s[:, cols], gffn_s[...]).astype(bf16)
            up_grad_ref[...] = sum_dot(second_s[...], gup_s[:, cols]).astype(bf16)
            ones = jnp.ones((8, act_s.shape[0]), bf16)
            up_sums_ref[...] = dot(ones, gup_s[:, cols])
            if n < NG:
                out_grad_ref[n * GW : (n + 1) * GW, :] = sum_dot(mixed_s[n], gatt_s[...]).astype(bf16)
            if n == WEIGHT_STEPS - 1:
                sums_ref[2:3, :] = dot(ones, gatt_s[...])[0:1]
                sums_ref[3:4, :] = dot(ones, gffn_s[...])[0:1]


WEIGHT_STEPS = 8


def feed_forward(h_zero, mixed4, inverse4, valid, cotangent, wide, down_w, vectors, tile=256):
    rows, width = h_zero.shape
    hidden = down_w.shape[0]
    row_steps = rows // tile
    last = row_steps - 1
    size = hidden // WEIGHT_STEPS
    row = lambda i: (jnp.minimum(i, last), 0)
    row4 = lambda i: (0, jnp.minimum(i, last), 0)
    after = lambda i: jnp.maximum(i - row_steps, 0)
    once = pl.Buffered(1)
    return pl.pallas_call(
        functools.partial(feed_kernel, row_steps),
        grid=(row_steps + WEIGHT_STEPS,),
        in_specs=[
            pl.BlockSpec((tile, width), row),
            pl.BlockSpec((NG, tile, GW), row4),
            pl.BlockSpec((NG, tile, GW), row4),
            pl.BlockSpec((tile, 1), row),
            pl.BlockSpec((tile, width), row),
            pl.BlockSpec((width, width), lambda i: (0, 3), pipeline_mode=once),
            pl.BlockSpec((width, hidden), lambda i: (0, 1), pipeline_mode=once),
            pl.BlockSpec((hidden, width), lambda i: (0, 0), pipeline_mode=once),
            *[whole((1, v.shape[0])) for v in vectors],
        ],
        out_specs=[
            pl.BlockSpec((tile, width), row),
            pl.BlockSpec((tile, width), row),
            pl.BlockSpec((NG, tile, GW), row4),
            pl.BlockSpec((size, width), lambda i: (after(i), 0)),
            pl.BlockSpec((width, size), lambda i: (0, after(i))),
            whole((width, width)),
            whole((8, width)),
            pl.BlockSpec((8, size), lambda i: (0, after(i))),
        ],
        out_shape=[
            jax.ShapeDtypeStruct((rows, width), bf16),
            jax.ShapeDtypeStruct((rows, width), f32),
            jax.ShapeDtypeStruct((NG, rows, GW), bf16),
            jax.ShapeDtypeStruct((hidden, width), bf16),
            jax.ShapeDtypeStruct((width, hidden), bf16),
            jax.ShapeDtypeStruct((width, width), bf16),
            jax.ShapeDtypeStruct((8, width), f32),
            jax.ShapeDtypeStruct((8, hidden), f32),
        ],
        scratch_shapes=[
            pltpu.VMEM((rows, hidden), bf16),
            pltpu.VMEM((rows, hidden), bf16),
            pltpu.VMEM((rows, width), bf16),
            pltpu.VMEM((rows, width), bf16),
            pltpu.VMEM((rows, width), bf16),
            pltpu.VMEM((NG, rows, GW), bf16),
            pltpu.VMEM((tile, width), f32),
            pltpu.VMEM((tile, width), f32),
        ],
        compiler_params=pltpu.CompilerParams(vmem_limit_bytes=56 * MIB),
        cost_estimate=pl.CostEstimate(flops=rows * 110 * 10**6, bytes_accessed=MIB, transcendentals=0),
        name="feed_forward",
    )(h_zero, mixed4, inverse4, valid, cotangent, wide, wide, down_w, *[v[None] for v in vectors])


def bias_back_kernel(
    pairs_step, near_ref, all_ref, means_ref, curve_ref, ds0_ref, ds1_ref, phi_ref, out_ref, dist_ref
):
    dist_ref[...] = distances(near_ref, all_ref)
    rows, span = dist_ref.shape

    @pl.when(pl.program_id(0) == 0)
    def _():
        out_ref[...] = jnp.zeros_like(out_ref)

    def body(step, acc):
        for q in range(pairs_step):
            pair = step * pairs_step + q
            here = pl.ds(pl.multiple_of(pair * 16, 16), 16)
            both = jnp.concatenate([ds0_ref[:, here, :].astype(f32), ds1_ref[:, here, :].astype(f32)], axis=0)
            for e in range(2):
                d = dist_ref[pl.ds(pair * 2 + e, 1), :]
                if e < STORED:
                    phi = phi_ref[pair * STORED + e]
                else:
                    wide = []
                    for lane in range(0, span, 128):
                        u = d[:, lane : lane + 128] - means_ref[...]
                        wide.append(jnp.exp2((u * curve_ref[...]) * u).astype(bf16))
                    phi = jnp.concatenate(wide, axis=1)
                d = d - CENTRE
                s = both[:, e * GH : (e + 1) * GH, :].reshape(HEADS, span)
                one = s * d
                x = jnp.concatenate([s.astype(bf16), *high_low(one), *high_low(one * d)], axis=0)
                acc = acc + lax.dot_general(
                    x, phi, (((1,), (1,)), ((), ())), preferred_element_type=f32
                )
        return acc

    out_ref[...] += lax.fori_loop(0, rows // 2 // pairs_step, body, jnp.zeros(out_ref.shape, f32))


def bias_back(near, coord_all, means, curve, ds, phi, first, count, tokens=(), tile=32, pairs_step=4):
    span = coord_all.shape[1]
    rows = count * tile
    kernel, token_specs = after(functools.partial(bias_back_kernel, pairs_step), 7, tokens)
    return pl.pallas_call(
        kernel,
        grid=(count,),
        in_specs=[
            pl.BlockSpec((tile, 3), lambda i: (i + first, 0)),
            whole((3, span)),
            whole((KERN, 128)),
            whole((KERN, 128)),
            pl.BlockSpec((NG // 2, tile * GH, span), lambda i: (0, i + first, 0)),
            pl.BlockSpec((NG // 2, tile * GH, span), lambda i: (0, i + first, 0)),
            pl.BlockSpec((tile * STORED // 2, KERN, span), lambda i: (i + first, 0, 0)),
            *token_specs,
        ],
        out_specs=whole((5 * HEADS, KERN)),
        out_shape=jax.ShapeDtypeStruct((5 * HEADS, KERN), f32),
        scratch_shapes=[pltpu.VMEM((tile, span), f32)],
        compiler_params=pltpu.CompilerParams(vmem_limit_bytes=50 * MIB),
        cost_estimate=pl.CostEstimate(flops=rows * 190 * 10**6, bytes_accessed=MIB, transcendentals=0),
        name="bias_back",
    )(near, coord_all, lane_wide(means), lane_wide(curve), *ds, phi, *tokens)


def row_items(global_rows, group_rows, lengths, groups):
    count = lengths.shape[0]
    order = jnp.arange(count, dtype=jnp.int32)
    earlier = (groups[:, None] == groups[None, :]) & (order[None, :] < order[:, None])
    starts = jnp.sum(jnp.where(earlier, lengths[None, :], 0), axis=1)
    group_of = global_rows // group_rows
    place = global_rows - group_of * group_rows
    hits = (
        (groups[None, :] == group_of[:, None])
        & (place[:, None] >= starts[None, :])
        & (place[:, None] < starts[None, :] + lengths[None, :])
    )
    item = jnp.sum(jnp.where(hits, order[None, :], 0), axis=1)
    return (item, jnp.any(hits, axis=1))


PIECES = (2, 6, 4, 2, 2)


def swap_sides(block):
    return lax.ppermute(block, "mp", [(0, 1), (1, 0)])


class Shards:
    def __init__(self, partial, first_bits):
        chips = lax.axis_size("rows")
        bits = chips.bit_length() - 1
        stack, rows, columns = partial.shape
        self.kept = partial.reshape(stack, *[2] * bits, 2, rows // (2 * chips), columns)
        self.come = None
        self.left = list(range(bits))[::-1]
        self.order = [None] + [b for b in first_bits if b < bits] + [b for b in range(bits) if b not in first_bits]

    def half(self, axis, index):
        part = lax.dynamic_index_in_dim(self.kept, index, axis, keepdims=False)
        if self.come is None:
            return part
        come = lax.dynamic_index_in_dim(self.come, index, axis, keepdims=False)
        return part.astype(f32) + come.astype(f32)

    def prepare(self):
        self.bit = self.order.pop(0)
        if self.bit is None:
            axis, mine = 1 + len(self.left), lax.axis_index("mp")
        else:
            axis, mine = 1 + self.left.index(self.bit), (lax.axis_index("rows") >> self.bit) & 1
            self.left.remove(self.bit)
        self.send = self.half(axis, 1 - mine).astype(bf16)
        self.kept = self.half(axis, mine)

    def launch(self):
        chips = lax.axis_size("rows")
        if self.bit is None:
            self.come = swap_sides(self.send)
        else:
            self.come = lax.ppermute(self.send, "rows", [(n, n ^ (1 << self.bit)) for n in range(chips)])

    def total(self):
        while self.order:
            self.prepare()
            self.launch()
        return self.kept.astype(f32) + self.come.astype(f32)


def beside(shards, run, inputs):
    shards = [s for s in shards if s.order]
    for s in shards:
        s.prepare()
    held = [(s.send, s.kept) for s in shards]
    held, inputs = lax.optimization_barrier((held, inputs))
    for s, (send, kept) in zip(shards, held):
        s.send, s.kept = send, kept
        s.launch()
    out = run(*inputs)
    came, out = lax.optimization_barrier(([s.come for s in shards], out))
    for s, come in zip(shards, came):
        s.come = come
    return out


def everyone(visit):
    side_count = lax.axis_size("mp")
    count = lax.axis_size("rows") * side_count
    me = lax.axis_index("rows") * side_count + lax.axis_index("mp")

    def body(step, carry):
        visit(step, lax.rem(me + step, count), lax.rem(me + count - step, count))
        return carry

    lax.fori_loop(1, count, body, 0)
    return me


def address(device):
    side_count = lax.axis_size("mp")
    return (device // side_count, lax.rem(device, side_count))


def meet_everyone():
    barrier = pltpu.get_barrier_semaphore()

    def greet(step, target, source):
        pl.semaphore_signal(
            barrier, inc=1, device_id=address(target), device_id_type=pl.DeviceIdType.MESH
        )

    everyone(greet)
    pl.semaphore_wait(barrier, lax.axis_size("rows") * lax.axis_size("mp") - 1)


def remote(source_ref, target_ref, send_sem, recv_sem, device):
    return pltpu.make_async_remote_copy(
        src_ref=source_ref,
        dst_ref=target_ref,
        send_sem=send_sem,
        recv_sem=recv_sem,
        device_id=address(device),
        device_id_type=pl.DeviceIdType.MESH,
    )


def gather_kernel(*refs):
    *x_refs, out_ref, block_ref, send_sem, recv_sem = refs
    count, rows, lanes = out_ref.shape
    side_count = lax.axis_size("mp")
    me = lax.axis_index("rows") * side_count + lax.axis_index("mp")
    block = [
        jnp.concatenate([r[...].astype(f32), jnp.zeros((1, lanes - r.shape[1]), f32)], axis=1) for r in x_refs
    ]
    block.append(jnp.zeros((rows - len(block), lanes), f32))
    block = jnp.concatenate(block, axis=0).astype(bf16)
    block_ref[...] = block
    meet_everyone()
    out_ref[me] = block

    def send(step, target, source):
        remote(block_ref, out_ref.at[me], send_sem.at[step], recv_sem.at[step], target).start()

    def wait(step, target, source):
        remote(block_ref, out_ref.at[source], send_sem.at[step], recv_sem.at[step], target).wait()

    everyone(send)
    everyone(wait)


def gather_small(vectors, count):
    return pl.pallas_call(
        gather_kernel,
        out_shape=jax.ShapeDtypeStruct((count, 16, 256), bf16),
        in_specs=[pl.BlockSpec(memory_space=pltpu.VMEM)] * len(vectors),
        out_specs=pl.BlockSpec(memory_space=pltpu.VMEM),
        scratch_shapes=[
            pltpu.VMEM((16, 256), bf16),
            pltpu.SemaphoreType.DMA((count,)),
            pltpu.SemaphoreType.DMA((count,)),
        ],
        compiler_params=pltpu.CompilerParams(
            collective_id=1, has_side_effects=True, vmem_limit_bytes=16 * MIB
        ),
        name="gather_small",
    )(*[v[None] for v in vectors])


def sum_kernel(x_ref, out_ref, come_ref, send_sem, recv_sem):
    side_count = lax.axis_size("mp")
    me = lax.axis_index("rows") * side_count + lax.axis_index("mp")
    meet_everyone()

    def send(step, target, source):
        remote(x_ref.at[target], come_ref.at[step], send_sem.at[step], recv_sem.at[step], target).start()

    def wait(step, target, source):
        remote(x_ref.at[target], come_ref.at[step], send_sem.at[step], recv_sem.at[step], target).wait()

    everyone(send)
    come_ref[0] = x_ref[me]
    everyone(wait)
    out_ref[...] = jnp.sum(come_ref[...].astype(f32), axis=0)


def sum_small(blocks):
    count = blocks.shape[0]
    return pl.pallas_call(
        sum_kernel,
        out_shape=jax.ShapeDtypeStruct(blocks.shape[1:], f32),
        in_specs=[pl.BlockSpec(memory_space=pltpu.VMEM)],
        out_specs=pl.BlockSpec(memory_space=pltpu.VMEM),
        scratch_shapes=[
            pltpu.VMEM(blocks.shape, blocks.dtype),
            pltpu.SemaphoreType.DMA((count,)),
            pltpu.SemaphoreType.DMA((count,)),
        ],
        compiler_params=pltpu.CompilerParams(
            collective_id=2, has_side_effects=True, vmem_limit_bytes=16 * MIB
        ),
        name="sum_small",
    )(blocks)


def lay_tables(share, count):
    lane = np.arange(share * count)
    place = lane[None, :] % share == np.arange(share)[:, None]
    mark = lane[None, :] // share == np.arange(count)[:, None]
    return jnp.asarray(place, bf16), jnp.asarray(mark, f32)


def joined(shares):
    count, vectors, share = shares.shape
    place, mark = lay_tables(share, count)
    wide = dot(shares.reshape(count * vectors, share), place).reshape(count, vectors, count * share)
    return jnp.sum(wide * mark[:, None, :], axis=0)


def cut(vectors, share):
    number, size = vectors.shape
    place, mark = lay_tables(share, size // share)
    wide = (vectors[None] * mark[:, None, :]).astype(bf16)
    out = lax.dot_general(wide, place, (((2,), (1,)), ((), ())), preferred_element_type=f32)
    return out.astype(bf16)


def on_device(
    atoms,
    time_embedding,
    coordinates,
    item_lengths,
    item_group,
    query_weight,
    key_weight,
    value_weight,
    out_weight,
    up_weight,
    down_weight,
    value_bias,
    out_bias,
    up_bias,
    down_bias,
    first_gain,
    first_shift,
    second_gain,
    second_shift,
    kernel_params,
    cotangent,
):
    rows_here = atoms.shape[0]
    pair_size = lax.axis_size("mp")
    side = lax.axis_index("mp")
    pair_index = lax.axis_index("rows")
    group_rows = rows_here * pair_size
    counter = jnp.arange(rows_here, dtype=jnp.int32)
    near_rows = (pair_index * pair_size + side) * rows_here + counter
    far_rows = (pair_index * pair_size + 1 - side) * rows_here + counter
    items = item_lengths.shape[0]
    near_item, near_valid = row_items(near_rows, group_rows, item_lengths, item_group)
    far_item, far_valid = row_items(far_rows, group_rows, item_lengths, item_group)
    near_code = jnp.where(near_valid, near_item, items + near_rows)
    far_code = jnp.where(far_valid, far_item, items + far_rows)
    all_code = jnp.concatenate([near_code, far_code])
    item = jnp.where(near_valid, near_item, -1)[:, None]
    valid = near_valid.astype(f32)[:, None]

    count = lax.axis_size("rows") * pair_size
    share, hidden = up_weight.shape
    width = query_weight.shape[1]
    blocks = hidden // width
    small = (value_bias, out_bias, down_bias, first_gain, first_shift, second_gain, second_shift)
    table_share = kernel_params.shape[0]
    gathered = gather_small((*small, up_bias, kernel_params), count)
    value_b, out_b, down_b, gain_one, shift_one, gain_two, shift_two = joined(gathered[:, :7, :share])
    up_b = joined(gathered[:, 7:8, : blocks * share])[0]
    table = joined(gathered[:, 8:9, :table_share])[0]
    wide = lax.all_gather(
        jnp.concatenate([query_weight, key_weight, value_weight, out_weight, up_weight], axis=1),
        AXES,
        axis=0,
        tiled=True,
    )
    down_w = lax.all_gather(down_weight, AXES, axis=0, tiled=True)

    means, widths, mix = table[:KERN], table[KERN : 2 * KERN], table[2 * KERN :].reshape(KERN, HEADS)
    norm = 1.0 / (widths * math.sqrt(2.0 * math.pi))
    curve = (-0.5 * math.log2(math.e)) / (widths * widths)
    mix_low = (mix * norm[:, None] * math.log2(math.e)).astype(bf16)
    coord_low = coordinates.astype(bf16)
    coord_all = jnp.concatenate([coord_low, swap_sides(coord_low)], axis=1).astype(f32)
    near = coordinates.astype(f32).T
    bias, phi = pair_bias(near, coord_all, near_code[:, None], all_code[None], means, curve, mix_low)

    bias, wide = lax.optimization_barrier((bias, wide))
    h_zero, q4, k4, v4 = project(atoms, item, time_embedding, gain_one, shift_one, value_b, wide)
    keys, values = (k4, swap_sides(k4)), (v4, swap_sides(v4))
    expo, mixed4, inverse4 = attend(q4, keys, values, bias)
    layer_out, grad_one, scaled4, down_grad, up_grad, out_grad, sums_two, up_sums = feed_forward(
        h_zero, mixed4, inverse4, valid, cotangent, wide, down_w, (out_b, up_b, down_b, gain_two, shift_two)
    )

    down_shards = Shards(down_grad[None], (0, 1))
    up_shards = Shards(up_grad[None], (1, 0))
    feed_shards = (down_shards, up_shards)
    half = NG // 2
    done = []
    for n in range(2):

        def run(scaled4):
            return attend_back(q4, scaled4, mixed4, keys, values, expo, n * half, half), scaled4

        out, scaled4 = beside(feed_shards, run, (scaled4,))
        done.append(out)
    scores_grad = [d[0] for d in done]
    turned = [(d[2], swap_sides(d[3]), d[4], swap_sides(d[5])) for d in done]
    pairs = [done[0][1], done[1][1]]
    for m in (0, 2, 1, 3):
        pairs += [turned[0][m], turned[1][m]]
    atoms_grad, square_grads, sums_one = beside(
        feed_shards,
        lambda h_zero, *pairs: project_back(h_zero, grad_one, pairs, gain_one, shift_one, wide, out_grad),
        (h_zero, *pairs),
    )
    square_shards = Shards(square_grads, (0, 1))

    tiles = rows_here // 32
    moments = 0.0
    first = 0
    for sixteenths in PIECES:
        size = sixteenths * tiles // 16
        piece, near = beside(
            (square_shards, *feed_shards),
            lambda near: (bias_back(near, coord_all, means, curve, scores_grad, phi, first, size), near),
            (near,),
        )
        moments = moments + piece
        first += size
    zeroth = moments[:HEADS].T * norm[:, None]
    first = (moments[HEADS : 2 * HEADS] + moments[2 * HEADS : 3 * HEADS]).T * norm[:, None]
    twice = (moments[3 * HEADS : 4 * HEADS] + moments[4 * HEADS :]).T * norm[:, None]
    m_zero, m_one, m_two = [jnp.sum(mix * r, axis=1) for r in (zeroth, first, twice)]
    offset = means - CENTRE
    mean_grad = (m_one - offset * m_zero) / widths**2
    width_grad = (m_two - 2.0 * offset * m_one + offset * offset * m_zero) / widths**3 - m_zero / widths
    table_grad = jnp.concatenate([mean_grad, width_grad, zeroth.reshape(-1)])

    cuts = jnp.concatenate(
        [
            jnp.pad(
                cut(
                    jnp.stack(
                        [sums_one[2], sums_two[2], sums_two[3], sums_one[0], sums_one[1], sums_two[0], sums_two[1]]
                    ),
                    share,
                ),
                ((0, 0), (0, 0), (0, 256 - share)),
            ),
            jnp.pad(cut(up_sums[0:1], blocks * share), ((0, 0), (0, 0), (0, 256 - blocks * share))),
            jnp.pad(cut(table_grad[None], table_share), ((0, 0), (0, 7), (0, 256 - table_share))),
        ],
        axis=1,
    )
    sums = sum_small(cuts)
    square_sum = square_shards.total()
    return (
        layer_out,
        atoms_grad,
        square_sum[0],
        square_sum[1],
        square_sum[2],
        square_sum[3],
        up_shards.total()[0],
        down_shards.total()[0],
        sums[0, :share],
        sums[1, :share],
        sums[7, : blocks * share],
        sums[2, :share],
        sums[3, :share],
        sums[4, :share],
        sums[5, :share],
        sums[6, :share],
        sums[8, :table_share],
    )


def solution(mesh):
    row = P(AXES, None)
    vec = P(AXES)
    in_specs = (row, P(), P(None, AXES), P(), P(), *[row] * 6, *[vec] * 9, row)
    out_specs = (*[row] * 8, *[vec] * 9)
    return jax.shard_map(on_device, mesh=mesh, in_specs=in_specs, out_specs=out_specs, check_vma=False)
```

```python
import functools
import math

import jax
import jax.numpy as jnp
import numpy as np
from jax import lax
from jax.experimental import pallas as pl
from jax.experimental.pallas import tpu as pltpu
from jax.sharding import PartitionSpec as P

HEADS = 32
KERN = 128
HEAD = 24
GH = 8
NG = HEADS // GH
GW = GH * HEAD
MIB = 2**20
CENTRE = 6.0
STORED = 1
AXES = ("rows", "mp")
f32 = jnp.float32
bf16 = jnp.bfloat16


def dot(left, right):
    return jnp.dot(left, right, preferred_element_type=f32)


def turned_dot(left, right):
    return lax.dot_general(left, right, (((1,), (1,)), ((), ())), preferred_element_type=f32)


def sum_dot(left, right):
    return lax.dot_general(left, right, (((0,), (0,)), ((), ())), preferred_element_type=f32)


def whole(shape):
    return pl.BlockSpec(shape, lambda i: (0,) * len(shape))


def after(kernel, inputs, tokens):
    def run(*refs):
        kernel(*refs[:inputs], *refs[inputs + len(tokens) :])

    return run, [pl.BlockSpec(memory_space=pl.ANY)] * len(tokens)


def high_low(value):
    high = value.astype(bf16)
    return high, (value - high.astype(f32)).astype(bf16)


def distances(near_ref, all_ref):
    total = None
    for c in range(3):
        diff = near_ref[:, c : c + 1] - all_ref[c : c + 1, :]
        total = diff * diff if total is None else total + diff * diff
    return jnp.sqrt(total) * 0.25


def bias_kernel(
    pairs_step, near_ref, all_ref, code_near_ref, code_all_ref, means_ref, curve_ref, mix_ref,
    bias_ref, phi_ref, dist_ref, mask_ref,
):
    dist_ref[...] = distances(near_ref, all_ref)
    mask_ref[...] = jnp.where(code_near_ref[:, 0:1] == code_all_ref[0:1, :], 0.0, -1e30)
    rows, span = dist_ref.shape

    def body(step, carry):
        for q in range(pairs_step):
            pair = step * pairs_step + q
            drow = [dist_ref[pl.ds(pair * 2 + e, 1), :] for e in range(2)]
            mrow = [mask_ref[pl.ds(pair * 2 + e, 1), :] for e in range(2)]
            for lane in range(0, span, 256):
                tall = []
                for e in range(2):
                    wide = []
                    for low in (lane, lane + 128):
                        u = drow[e][:, low : low + 128] - means_ref[...]
                        wide.append(jnp.exp2((u * curve_ref[...]) * u).astype(bf16))
                    wide = jnp.concatenate(wide, axis=1)
                    if e < STORED:
                        phi_ref[pair * STORED + e, :, lane : lane + 256] = wide
                    tall.append(wide)
                out = dot(mix_ref[...], jnp.concatenate(tall, axis=0)).reshape(NG, 2, GH, 256)
                out = jnp.concatenate(
                    [out[:, e : e + 1] + mrow[e][:, lane : lane + 256].reshape(1, 1, 1, 256) for e in range(2)],
                    axis=1,
                )
                bias_ref[:, pl.ds(pl.multiple_of(pair * 16, 16), 16), lane : lane + 256] = out.reshape(
                    NG, 16, 256
                ).astype(bf16)
        return carry

    lax.fori_loop(0, rows // 2 // pairs_step, body, 0)


def lane_wide(values):
    return jnp.broadcast_to(values[:, None], (KERN, 128))


def pair_bias(near, coord_all, code_near, code_all, means, curve, mix_low, tile=32, pairs_step=16):
    rows, span = near.shape[0], coord_all.shape[1]
    m4 = mix_low.T.reshape(NG, GH, KERN)
    zero = jnp.zeros_like(m4)
    left = jnp.stack([jnp.concatenate([m4, zero], -1), jnp.concatenate([zero, m4], -1)], axis=1)
    left = left.reshape(2 * HEADS, 2 * KERN)
    return pl.pallas_call(
        functools.partial(bias_kernel, pairs_step),
        grid=(rows // tile,),
        in_specs=[
            pl.BlockSpec((tile, 3), lambda i: (i, 0)),
            whole((3, span)),
            pl.BlockSpec((tile, 1), lambda i: (i, 0)),
            whole((1, span)),
            whole((KERN, 128)),
            whole((KERN, 128)),
            whole((2 * HEADS, 2 * KERN)),
        ],
        out_specs=[
            pl.BlockSpec((NG, tile * GH, span), lambda i: (0, i, 0)),
            pl.BlockSpec((tile * STORED // 2, KERN, span), lambda i: (i, 0, 0)),
        ],
        out_shape=[
            jax.ShapeDtypeStruct((NG, rows * GH, span), bf16),
            jax.ShapeDtypeStruct((rows * STORED // 2, KERN, span), bf16),
        ],
        scratch_shapes=[pltpu.VMEM((tile, span), f32), pltpu.VMEM((tile, span), f32)],
        compiler_params=pltpu.CompilerParams(vmem_limit_bytes=50 * MIB),
        cost_estimate=pl.CostEstimate(flops=1000, bytes_accessed=1000, transcendentals=0),
        name="bias",
    )(near, coord_all, code_near, code_all, lane_wide(means), lane_wide(curve), left)


def repeat_tables(tile):
    row = np.arange(tile * GH)
    repeat = row[:, None] // GH == np.arange(tile)[None, :]
    own = row[:, None] % GH == np.arange(GW)[None, :] // HEAD
    return repeat, own


def project_kernel(
    atoms_ref, code_ref, time_ref, gain_ref, shift_ref, bias_ref, wide_ref,
    h_ref, q_ref, kv_ref,
):
    width = atoms_ref.shape[1]
    items = lax.broadcasted_iota(jnp.int32, (1, time_ref.shape[0]), 1)
    picks = (code_ref[...] == items).astype(f32).astype(bf16)
    h_zero = atoms_ref[...].astype(f32) + dot(picks, time_ref[...])
    h_ref[...] = h_zero
    centre = h_zero - jnp.mean(h_zero, axis=1, keepdims=True)
    rate = lax.rsqrt(jnp.mean(centre * centre, axis=1, keepdims=True) + 1e-05)
    normed = (centre * rate * gain_ref[...] + shift_ref[...]).astype(bf16)
    tile = h_zero.shape[0]
    lane = lax.broadcasted_iota(jnp.int32, (tile, 256 - GW), 1)
    ones = jnp.where(lane == 0, 1.0, 0.0)
    for n in (1, 2, 0):
        out = dot(normed, wide_ref[:, n * width : (n + 1) * width])
        if n == 2:
            out = out + bias_ref[...]
        for g in range(NG):
            part = out[:, g * GW : (g + 1) * GW]
            if n == 0:
                q_ref[g] = part.astype(bf16)
            else:
                part = jnp.concatenate([part, ones if n == 2 else jnp.zeros_like(ones)], axis=1)
                kv_ref[n - 1, g] = part.astype(bf16)


def project(atoms, code, time_embedding, gain, shift, value_bias, wide, tile=256):
    rows, width = atoms.shape
    return pl.pallas_call(
        project_kernel,
        grid=(rows // tile,),
        in_specs=[
            pl.BlockSpec((tile, width), lambda i: (i, 0)),
            pl.BlockSpec((tile, 1), lambda i: (i, 0)),
            whole(time_embedding.shape),
            *[whole((1, width))] * 3,
            whole((width, 3 * width)),
        ],
        out_specs=[
            pl.BlockSpec((tile, width), lambda i: (i, 0)),
            pl.BlockSpec((NG, tile, GW), lambda i: (0, i, 0)),
            pl.BlockSpec((2, NG, tile, 256), lambda i: (0, 0, i, 0)),
        ],
        out_shape=[
            jax.ShapeDtypeStruct((rows, width), f32),
            jax.ShapeDtypeStruct((NG, rows, GW), bf16),
            jax.ShapeDtypeStruct((2, NG, rows, 256), bf16),
        ],
        compiler_params=pltpu.CompilerParams(vmem_limit_bytes=40 * MIB),
        cost_estimate=pl.CostEstimate(flops=1000, bytes_accessed=1000, transcendentals=0),
        name="project",
    )(atoms, code, time_embedding, gain[None], shift[None], value_bias[None], wide)


def project_back_kernel(
    h_ref, grad_one_ref, q0_ref, q1_ref, k0_ref, k1_ref, v0_ref, v1_ref, kc0_ref, kc1_ref, vc0_ref, vc1_ref,
    gain_ref, shift_ref, wide_ref, out_grad_ref,
    atoms_grad_ref, grads_ref, sums_ref, normed_s, grad_s,
):
    rows, width = h_ref.shape
    for g in range(NG):
        q_ref, k_ref, v_ref, kc_ref, vc_ref = (
            (q0_ref, k0_ref, v0_ref, kc0_ref, vc0_ref) if g < NG // 2 else (q1_ref, k1_ref, v1_ref, kc1_ref, vc1_ref)
        )
        m = g % (NG // 2)
        cols = slice(g * GW, (g + 1) * GW)
        grad_s[0, :, cols] = q_ref[m]
        grad_s[1, :, cols] = (k_ref[m] + kc_ref[m].astype(f32)).T.astype(bf16)
        grad_s[2, :, cols] = (v_ref[m] + vc_ref[m].astype(f32)).T.astype(bf16)
    h_zero = h_ref[...]
    centre = h_zero - jnp.mean(h_zero, axis=1, keepdims=True)
    rate = lax.rsqrt(jnp.mean(centre * centre, axis=1, keepdims=True) + 1e-05)
    hat = centre * rate
    normed_s[...] = (hat * gain_ref[...] + shift_ref[...]).astype(bf16)
    grads_ref[3] = out_grad_ref[...]
    grad = None
    for n in range(3):
        grads_ref[n] = sum_dot(normed_s[...], grad_s[n]).astype(bf16)
        part = turned_dot(grad_s[n], wide_ref[:, n * width : (n + 1) * width])
        grad = part if grad is None else grad + part
    g = grad * gain_ref[...]
    atoms_grad_ref[...] = grad_one_ref[...] + rate * (
        g - jnp.mean(g, axis=1, keepdims=True) - hat * jnp.mean(g * hat, axis=1, keepdims=True)
    )
    sums_ref[...] = jnp.zeros_like(sums_ref)
    sums_ref[0:1, :] = jnp.sum(grad * hat, axis=0, keepdims=True)
    sums_ref[1:2, :] = jnp.sum(grad, axis=0, keepdims=True)
    sums_ref[2:3, :] = dot(jnp.ones((8, rows), bf16), grad_s[2])[0:1]


def project_back(h_zero, grad_one, pairs, gain, shift, wide, out_grad, tokens=()):
    rows, width = h_zero.shape
    once = pl.Buffered(1)
    kernel, token_specs = after(project_back_kernel, 16, tokens)
    return pl.pallas_call(
        kernel,
        grid=(1,),
        in_specs=[
            whole((rows, width)),
            whole((rows, width)),
            *[whole(p.shape) for p in pairs],
            *[whole((1, width))] * 2,
            pl.BlockSpec((width, 3 * width), lambda i: (0, 0), pipeline_mode=once),
            whole((width, width)),
            *token_specs,
        ],
        out_specs=[whole((rows, width)), whole((NG, width, width)), whole((8, width))],
        out_shape=[
            jax.ShapeDtypeStruct((rows, width), f32),
            jax.ShapeDtypeStruct((4, width, width), bf16),
            jax.ShapeDtypeStruct((8, width), f32),
        ],
        scratch_shapes=[pltpu.VMEM((rows, width), bf16), pltpu.VMEM((3, rows, width), bf16)],
        compiler_params=pltpu.CompilerParams(vmem_limit_bytes=56 * MIB),
        cost_estimate=pl.CostEstimate(flops=1000, bytes_accessed=1000, transcendentals=0),
        name="project_back",
    )(h_zero, grad_one, *pairs, gain[None], shift[None], wide, out_grad, *tokens)


def attend_kernel(
    tiles, q_ref, near_ref, far_ref, b_ref, rep_ref, rept_ref, own_ref, scaled_ref,
    e_ref, mixed_ref, inv_ref, qa, qb, sa, sb, ea, oa, ob, wa, wb,
):
    keys, values = (near_ref.at[0], far_ref.at[0]), (near_ref.at[1], far_ref.at[1])
    query, scores, outs, wides = (qa, qb), (sa, sb), (oa, ob), (wa, wb)
    rows, span = sa.shape
    held = rows // GH
    units = NG * tiles
    parts, chunk, ahead = 4, 8, 3
    step, some = span // parts, rows // parts
    pid = pl.program_id(0)

    def place(unit):
        unit = jnp.clip(unit, 0, units - 1)
        group = unit // tiles
        return group, pl.ds(pl.multiple_of((unit - group * tiles) * held, held), held)

    def spread(unit, par):
        g, i = place(unit)
        query[par][...] = (dot(rep_ref[...], q_ref[g, i, :]) * scaled_ref[...]).astype(bf16)

    def score(unit, par, part):
        g, _ = place(unit)
        cols = slice(part * step, (part + 1) * step)
        there = slice(part % 2 * step, (part % 2 + 1) * step)
        scores[par][:, cols] = turned_dot(query[par][...], keys[part // 2][g, there, :GW])

    def soften(par, part):
        chunks = range(part * some, (part + 1) * some, chunk)
        held_x = {}
        for n in range(len(chunks) + ahead):
            if n < len(chunks):
                here = slice(chunks[n], chunks[n] + chunk)
                x = scores[par][here, :] + b_ref[par, here, :].astype(f32)
                held_x[n] = x, jnp.max(x, axis=1, keepdims=True)
            if n >= ahead:
                here = slice(chunks[n - ahead], chunks[n - ahead] + chunk)
                x, top = held_x.pop(n - ahead)
                e = jnp.exp2(x - top).astype(bf16)
                e_ref[par, here, :] = e
                if par == 1:
                    ea[here, :] = e

    def mix(unit, par, part):
        g, _ = place(unit)
        here = slice(part * some, (part + 1) * some)
        source = e_ref.at[0] if par == 0 else ea
        half = span // 2
        outs[par][here, :] = dot(source[here, :half], values[0][g]) + dot(source[here, half:], values[1][g])

    def scale(par, part):
        here = slice(part * some, (part + 1) * some)
        out = outs[par][here, :]
        inv = 1.0 / out[:, GW : GW + 1]
        own = own_ref[here, :]
        wides[par][here, :] = jnp.concatenate(
            [*high_low(out[:, :GW] * inv * own), *high_low(inv * own)], axis=1
        )

    def gather(unit, par):
        g, i = place(unit)
        out = dot(rept_ref[...], wides[par][...])
        mixed_ref[g, i, :] = out[:, :GW] + out[:, GW : 2 * GW]
        inv_ref[g, i, :] = out[:, 2 * GW : 3 * GW] + out[:, 3 * GW :]

    @pl.when(pid == 0)
    def _():
        spread(0, 0)
        for part in range(parts):
            score(0, 0, part)
        spread(1, 1)
        ea[...] = jnp.ones_like(ea)
        for ref in (oa, ob):
            ref[...] = jnp.ones_like(ref)
        for ref in (wa, wb):
            ref[...] = jnp.zeros_like(ref)

    for par in range(2):
        unit = pid * 2 + par
        for part in range(parts):
            score(unit + 1, 1 - par, part)
            scale(par, part)
            mix(unit - 1, 1 - par, part)
            if part == 1:
                spread(unit + 2, par)
            if part == 2:
                gather(unit - 3, 1 - par)
            soften(par, part)

    @pl.when(pid == units // 2 - 1)
    def _():
        for part in range(parts):
            scale(0, part)
            mix(units - 1, 1, part)
        gather(units - 3, 1)
        gather(units - 2, 0)
        for part in range(parts):
            scale(1, part)
        gather(units - 1, 1)


def attend(q4, near, far, bias, tile=64):
    rows = q4.shape[1]
    span = 2 * rows
    tiles = rows // tile
    repeat, own = repeat_tables(tile)
    deep = tile * GH
    bias = bias.reshape(NG * tiles, deep, span)
    big = pl.BlockSpec((2, deep, span), lambda i: (i, 0, 0))
    scale = HEAD**-0.5 * math.log2(math.e)
    e, mixed, inv = pl.pallas_call(
        functools.partial(attend_kernel, tiles),
        grid=(NG * tiles // 2,),
        in_specs=[
            whole((NG, rows, GW)),
            *[whole((2, NG, rows, 256))] * 2,
            big,
            whole((deep, tile)),
            whole((tile, deep)),
            whole((deep, GW)),
            whole((deep, GW)),
        ],
        out_specs=[big, whole((NG, rows, GW)), whole((NG, rows, GW))],
        out_shape=[
            jax.ShapeDtypeStruct((NG * tiles, deep, span), bf16),
            jax.ShapeDtypeStruct((NG, rows, GW), f32),
            jax.ShapeDtypeStruct((NG, rows, GW), f32),
        ],
        scratch_shapes=[pltpu.VMEM((deep, GW), bf16)] * 2
        + [pltpu.VMEM((deep, span), f32)] * 2
        + [pltpu.VMEM((deep, span), bf16)]
        + [pltpu.VMEM((deep, 256), f32)] * 2
        + [pltpu.VMEM((deep, 4 * GW), bf16)] * 2,
        compiler_params=pltpu.CompilerParams(vmem_limit_bytes=50 * MIB),
        cost_estimate=pl.CostEstimate(flops=1000, bytes_accessed=1000, transcendentals=0),
        name="attend",
    )(
        q4, near, far, bias, jnp.asarray(repeat, bf16), jnp.asarray(repeat.T, bf16),
        jnp.asarray(own, f32), jnp.asarray(own * scale, f32),
    )
    return e.reshape(NG, rows * GH, span), mixed, inv


def attend_back_kernel(
    tiles, q_ref, gs_ref, mx_ref, near_ref, far_ref, e_ref, rep_ref, rept_ref, own_ref, ownt_ref,
    ds_ref, dq_ref, dk_near_ref, dk_far_ref, dv_near_ref, dv_far_ref,
    ga, gb, da, db, qta, qtb, gta, gtb, sa, sb, kept, oa, ob, wa, wb, dk, dv,
):
    keys, values = (near_ref.at[0], far_ref.at[0]), (near_ref.at[1], far_ref.at[1])
    grads, deltas, queries_t, grads_t = (ga, gb), (da, db), (qta, qtb), (gta, gtb)
    scores, outs, wides = (sa, sb), (oa, ob), (wa, wb)
    deep, span = sa.shape
    held = deep // GH
    units = q_ref.shape[0] * tiles
    parts, chunk = 4, 8
    step, some = span // parts, deep // parts
    scale = HEAD**-0.5
    pid = pl.program_id(0)

    def place(unit):
        unit = jnp.clip(unit, 0, units - 1)
        group = unit // tiles
        return group, pl.ds(pl.multiple_of((unit - group * tiles) * held, held), held)

    def begin_scores(unit, par):
        g, i = place(unit)
        grads[par][...] = (dot(rep_ref[...], gs_ref[g, i, :]) * own_ref[...]).astype(bf16)

    def begin_rest(unit, par):
        g, i = place(unit)
        gs = gs_ref[g, i, :]
        wide = dot(rep_ref[...], jnp.concatenate(high_low(gs.astype(f32) * mx_ref[g, i, :]), axis=1))
        deltas[par][...] = jnp.sum((wide[:, :GW] + wide[:, GW:]) * own_ref[...], axis=1, keepdims=True)
        grads_t[par][...] = (sum_dot(gs, rept_ref[...]) * ownt_ref[...]).astype(bf16)

    def turn_query(unit, par):
        g, i = place(unit)
        queries_t[par][...] = (sum_dot(q_ref[g, i, :], rept_ref[...]) * ownt_ref[...]).astype(bf16)

    def grad_probs(unit, par, part):
        g, _ = place(unit)
        cols = slice(part * step, (part + 1) * step)
        there = slice(part % 2 * step, (part % 2 + 1) * step)
        scores[par][:, cols] = turned_dot(grads[par][...], values[part // 2][g, there, :GW])

    def soften(par, part):
        for c in range(part * some, (part + 1) * some, chunk):
            here = slice(c, c + chunk)
            ds = (e_ref[par, here, :].astype(f32) * (scores[par][here, :] - deltas[par][here, :])).astype(bf16)
            ds_ref[par, here, :] = ds
            if par == 1:
                kept[here, :] = ds

    def value_grad(unit, par, part):
        g, _ = place(unit)
        cols = slice(part * step, (part + 1) * step)
        dv[g, :, cols] += dot(grads_t[par][...], e_ref[par, :, cols])

    def key_grad(unit, par, part):
        g, _ = place(unit)
        cols = slice(part * step, (part + 1) * step)
        source = ds_ref.at[0] if par == 0 else kept
        dk[g, :, cols] += dot(queries_t[par][...], source[:, cols])

    def query_grad(unit, par, part):
        g, _ = place(unit)
        here = slice(part * some, (part + 1) * some)
        source = ds_ref.at[0] if par == 0 else kept
        half = span // 2
        outs[par][here, :] = dot(source[here, :half], keys[0][g, :, :GW]) + dot(
            source[here, half:], keys[1][g, :, :GW]
        )

    def mask(par):
        wides[par][...] = (outs[par][...] * own_ref[...]).astype(bf16)

    def gather(unit, par):
        g, i = place(unit)
        dq_ref[g, i, :] = (dot(rept_ref[...], wides[par][...]) * scale).astype(bf16)

    @pl.when(pid == 0)
    def _():
        dk[...] = jnp.zeros_like(dk)
        dv[...] = jnp.zeros_like(dv)
        begin_scores(0, 0)
        for part in range(parts):
            grad_probs(0, 0, part)
        begin_scores(1, 1)
        begin_rest(0, 0)
        queries_t[1][...] = jnp.zeros_like(queries_t[1])
        kept[...] = jnp.zeros_like(kept)
        for ref in (oa, ob, wa, wb):
            ref[...] = jnp.zeros_like(ref)

    for par in range(2):
        unit = pid * 2 + par
        for part in range(parts):
            grad_probs(unit + 1, 1 - par, part)
            value_grad(unit, par, part)
            if part == 0:
                begin_scores(unit + 2, par)
                gather(unit - 3, 1 - par)
            if part == 1:
                begin_rest(unit + 1, 1 - par)
            if part == 2:
                turn_query(unit, par)
            if part == 3:
                mask(par)
            key_grad(unit - 1, 1 - par, part)
            query_grad(unit - 1, 1 - par, part)
            soften(par, part)

    @pl.when(pid == units // 2 - 1)
    def _():
        last = units - 1
        gather(last - 2, 1)
        mask(0)
        for part in range(parts):
            key_grad(last, 1, part)
            query_grad(last, 1, part)
        gather(last - 1, 0)
        mask(1)
        gather(last, 1)
        half = span // 2
        dk_near_ref[...] = dk[:, :, :half] * scale
        dk_far_ref[...] = (dk[:, :, half:] * scale).astype(bf16)
        dv_near_ref[...] = dv[:, :, :half]
        dv_far_ref[...] = dv[:, :, half:].astype(bf16)


def attend_back(q4, gs4, mx4, near_kv, far_kv, e, first, groups, tokens=(), tile=64):
    rows = q4.shape[1]
    span = 2 * rows
    tiles = rows // tile
    deep = tile * GH
    repeat, own = repeat_tables(tile)
    e = e.reshape(NG * tiles, deep, span)
    block = first // groups
    ahead = first * tiles // 2
    held = lambda wide: pl.BlockSpec((groups, rows, wide), lambda i: (block, 0, 0))
    near = jax.ShapeDtypeStruct((groups, GW, rows), f32)
    far = jax.ShapeDtypeStruct((groups, GW, rows), bf16)
    kernel, token_specs = after(functools.partial(attend_back_kernel, tiles), 10, tokens)
    ds, *rest = pl.pallas_call(
        kernel,
        grid=(groups * tiles // 2,),
        in_specs=[
            *[held(GW)] * 3,
            *[pl.BlockSpec((2, groups, rows, 256), lambda i: (0, block, 0, 0))] * 2,
            pl.BlockSpec((2, deep, span), lambda i: (i + ahead, 0, 0)),
            whole((deep, tile)),
            whole((tile, deep)),
            whole((deep, GW)),
            whole((GW, deep)),
            *token_specs,
        ],
        out_specs=[
            pl.BlockSpec((2, deep, span), lambda i: (i, 0, 0)),
            whole((groups, rows, GW)),
            *[whole((groups, GW, rows))] * 4,
        ],
        out_shape=[
            jax.ShapeDtypeStruct((groups * tiles, deep, span), bf16),
            jax.ShapeDtypeStruct((groups, rows, GW), bf16),
            near,
            far,
            near,
            far,
        ],
        scratch_shapes=[pltpu.VMEM((deep, GW), bf16)] * 2
        + [pltpu.VMEM((deep, 1), f32)] * 2
        + [pltpu.VMEM((GW, deep), bf16)] * 4
        + [pltpu.VMEM((deep, span), f32)] * 2
        + [pltpu.VMEM((deep, span), bf16)]
        + [pltpu.VMEM((deep, GW), f32)] * 2
        + [pltpu.VMEM((deep, GW), bf16)] * 2
        + [pltpu.VMEM((groups, GW, span), f32)] * 2,
        compiler_params=pltpu.CompilerParams(vmem_limit_bytes=50 * MIB),
        cost_estimate=pl.CostEstimate(flops=1000, bytes_accessed=1000, transcendentals=0),
        name="attend_back",
    )(
        q4, gs4, mx4, near_kv, far_kv, e, jnp.asarray(repeat, bf16), jnp.asarray(repeat.T, bf16),
        jnp.asarray(own, f32), jnp.asarray(own.T, f32), *tokens,
    )
    return (ds.reshape(groups, rows * GH, span), *rest)


def feed_kernel(
    row_steps, h_ref, mixed_ref, inv_ref, valid_ref, cot_ref, out_w_ref, up_w_ref, down_w_ref,
    out_b_ref, up_b_ref, down_b_ref, gain_ref, shift_ref,
    layer_ref, grad_one_ref, gs_ref, down_grad_ref, up_grad_ref, out_grad_ref, sums_ref, up_sums_ref,
    act_s, gup_s, second_s, gatt_s, gffn_s, mixed_s, up_s, gact_s,
):
    step = pl.program_id(0)
    tile, width = h_ref.shape
    hidden = up_w_ref.shape[1]
    some = 32

    @pl.when(step == 0)
    def _():
        sums_ref[...] = jnp.zeros_like(sums_ref)

    @pl.when(step < row_steps)
    def _():
        here = pl.ds(pl.multiple_of(step * tile, tile), tile)
        h_one = h_ref[...] + out_b_ref[...]
        for g in range(NG):
            mixed = mixed_ref[g].astype(bf16)
            mixed_s[g, here, :] = mixed
            h_one = h_one + dot(mixed, out_w_ref[g * GW : (g + 1) * GW, :])
        centre = h_one - jnp.mean(h_one, axis=1, keepdims=True)
        rate = lax.rsqrt(jnp.mean(centre * centre, axis=1, keepdims=True) + 1e-05)
        second = (centre * rate * gain_ref[...] + shift_ref[...]).astype(bf16)
        second_s[here, :] = second
        grad_two = cot_ref[...].astype(f32) * valid_ref[...]
        grad_ffn = grad_two.astype(bf16)
        gffn_s[here, :] = grad_ffn
        h_two = h_one + down_b_ref[...]
        grad_second = None
        for low in range(0, hidden, width):
            cols = slice(low, low + width)
            up_s[...] = dot(second, up_w_ref[:, cols]) + up_b_ref[:, cols]
            gact_s[...] = turned_dot(grad_ffn, down_w_ref[cols, :])

            def bend(n, carry):
                rows = pl.ds(pl.multiple_of(n * some, some), some)
                at = pl.ds(pl.multiple_of(step * tile + n * some, some), some)
                up = up_s[rows, :]
                below = 0.5 + 0.5 * lax.erf(up * (2.0**-0.5))
                slope = below + up * (jnp.exp(-0.5 * up * up) * (2.0 * math.pi) ** -0.5)
                act_s[at, cols] = (up * below).astype(bf16)
                gup_s[at, cols] = (gact_s[rows, :] * slope).astype(bf16)
                return carry

            lax.fori_loop(0, tile // some, bend, 0)
            h_two = h_two + dot(act_s[here, cols], down_w_ref[cols, :])
            part = turned_dot(gup_s[here, cols], up_w_ref[:, cols])
            grad_second = part if grad_second is None else grad_second + part
        layer_ref[...] = (h_two * valid_ref[...]).astype(bf16)
        hat = centre * rate
        sums_ref[0:1, :] += jnp.sum(grad_second * hat, axis=0, keepdims=True)
        sums_ref[1:2, :] += jnp.sum(grad_second, axis=0, keepdims=True)
        g = grad_second * gain_ref[...]
        grad_one = grad_two + rate * (
            g - jnp.mean(g, axis=1, keepdims=True) - hat * jnp.mean(g * hat, axis=1, keepdims=True)
        )
        grad_one_ref[...] = grad_one
        grad_att = grad_one.astype(bf16)
        gatt_s[here, :] = grad_att
        for g in range(NG):
            grad_mixed = turned_dot(grad_att, out_w_ref[g * GW : (g + 1) * GW, :]).astype(bf16)
            gs_ref[g] = (grad_mixed.astype(f32) * inv_ref[g]).astype(bf16)

    for n in range(WEIGHT_STEPS):

        @pl.when(step == row_steps + n)
        def _():
            size = hidden // WEIGHT_STEPS
            cols = slice(n * size, (n + 1) * size)
            down_grad_ref[...] = sum_dot(act_s[:, cols], gffn_s[...]).astype(bf16)
            up_grad_ref[...] = sum_dot(second_s[...], gup_s[:, cols]).astype(bf16)
            ones = jnp.ones((8, act_s.shape[0]), bf16)
            up_sums_ref[...] = dot(ones, gup_s[:, cols])
            if n < NG:
                out_grad_ref[n * GW : (n + 1) * GW, :] = sum_dot(mixed_s[n], gatt_s[...]).astype(bf16)
            if n == WEIGHT_STEPS - 1:
                sums_ref[2:3, :] = dot(ones, gatt_s[...])[0:1]
                sums_ref[3:4, :] = dot(ones, gffn_s[...])[0:1]


WEIGHT_STEPS = 8


def feed_forward(h_zero, mixed4, inverse4, valid, cotangent, wide, down_w, vectors, tile=256):
    rows, width = h_zero.shape
    hidden = down_w.shape[0]
    row_steps = rows // tile
    last = row_steps - 1
    size = hidden // WEIGHT_STEPS
    row = lambda i: (jnp.minimum(i, last), 0)
    row4 = lambda i: (0, jnp.minimum(i, last), 0)
    after = lambda i: jnp.maximum(i - row_steps, 0)
    once = pl.Buffered(1)
    return pl.pallas_call(
        functools.partial(feed_kernel, row_steps),
        grid=(row_steps + WEIGHT_STEPS,),
        in_specs=[
            pl.BlockSpec((tile, width), row),
            pl.BlockSpec((NG, tile, GW), row4),
            pl.BlockSpec((NG, tile, GW), row4),
            pl.BlockSpec((tile, 1), row),
            pl.BlockSpec((tile, width), row),
            pl.BlockSpec((width, width), lambda i: (0, 3), pipeline_mode=once),
            pl.BlockSpec((width, hidden), lambda i: (0, 1), pipeline_mode=once),
            pl.BlockSpec((hidden, width), lambda i: (0, 0), pipeline_mode=once),
            *[whole((1, v.shape[0])) for v in vectors],
        ],
        out_specs=[
            pl.BlockSpec((tile, width), row),
            pl.BlockSpec((tile, width), row),
            pl.BlockSpec((NG, tile, GW), row4),
            pl.BlockSpec((size, width), lambda i: (after(i), 0)),
            pl.BlockSpec((width, size), lambda i: (0, after(i))),
            whole((width, width)),
            whole((8, width)),
            pl.BlockSpec((8, size), lambda i: (0, after(i))),
        ],
        out_shape=[
            jax.ShapeDtypeStruct((rows, width), bf16),
            jax.ShapeDtypeStruct((rows, width), f32),
            jax.ShapeDtypeStruct((NG, rows, GW), bf16),
            jax.ShapeDtypeStruct((hidden, width), bf16),
            jax.ShapeDtypeStruct((width, hidden), bf16),
            jax.ShapeDtypeStruct((width, width), bf16),
            jax.ShapeDtypeStruct((8, width), f32),
            jax.ShapeDtypeStruct((8, hidden), f32),
        ],
        scratch_shapes=[
            pltpu.VMEM((rows, hidden), bf16),
            pltpu.VMEM((rows, hidden), bf16),
            pltpu.VMEM((rows, width), bf16),
            pltpu.VMEM((rows, width), bf16),
            pltpu.VMEM((rows, width), bf16),
            pltpu.VMEM((NG, rows, GW), bf16),
            pltpu.VMEM((tile, width), f32),
            pltpu.VMEM((tile, width), f32),
        ],
        compiler_params=pltpu.CompilerParams(vmem_limit_bytes=56 * MIB),
        cost_estimate=pl.CostEstimate(flops=1000, bytes_accessed=1000, transcendentals=0),
        name="feed_forward",
    )(h_zero, mixed4, inverse4, valid, cotangent, wide, wide, down_w, *[v[None] for v in vectors])


def bias_back_kernel(
    pairs_step, near_ref, all_ref, means_ref, curve_ref, ds0_ref, ds1_ref, phi_ref, out_ref, dist_ref
):
    dist_ref[...] = distances(near_ref, all_ref)
    rows, span = dist_ref.shape

    @pl.when(pl.program_id(0) == 0)
    def _():
        out_ref[...] = jnp.zeros_like(out_ref)

    def body(step, acc):
        for q in range(pairs_step):
            pair = step * pairs_step + q
            here = pl.ds(pl.multiple_of(pair * 16, 16), 16)
            both = jnp.concatenate([ds0_ref[:, here, :].astype(f32), ds1_ref[:, here, :].astype(f32)], axis=0)
            for e in range(2):
                d = dist_ref[pl.ds(pair * 2 + e, 1), :]
                if e < STORED:
                    phi = phi_ref[pair * STORED + e]
                else:
                    wide = []
                    for lane in range(0, span, 128):
                        u = d[:, lane : lane + 128] - means_ref[...]
                        wide.append(jnp.exp2((u * curve_ref[...]) * u).astype(bf16))
                    phi = jnp.concatenate(wide, axis=1)
                d = d - CENTRE
                s = both[:, e * GH : (e + 1) * GH, :].reshape(HEADS, span)
                one = s * d
                x = jnp.concatenate([s.astype(bf16), *high_low(one), *high_low(one * d)], axis=0)
                acc = acc + lax.dot_general(
                    x, phi, (((1,), (1,)), ((), ())), preferred_element_type=f32
                )
        return acc

    out_ref[...] += lax.fori_loop(0, rows // 2 // pairs_step, body, jnp.zeros(out_ref.shape, f32))


def bias_back(near, coord_all, means, curve, ds, phi, first, count, tokens=(), tile=32, pairs_step=16):
    span = coord_all.shape[1]
    rows = count * tile
    kernel, token_specs = after(functools.partial(bias_back_kernel, pairs_step), 7, tokens)
    return pl.pallas_call(
        kernel,
        grid=(count,),
        in_specs=[
            pl.BlockSpec((tile, 3), lambda i: (i + first, 0)),
            whole((3, span)),
            whole((KERN, 128)),
            whole((KERN, 128)),
            pl.BlockSpec((NG // 2, tile * GH, span), lambda i: (0, i + first, 0)),
            pl.BlockSpec((NG // 2, tile * GH, span), lambda i: (0, i + first, 0)),
            pl.BlockSpec((tile * STORED // 2, KERN, span), lambda i: (i + first, 0, 0)),
            *token_specs,
        ],
        out_specs=whole((5 * HEADS, KERN)),
        out_shape=jax.ShapeDtypeStruct((5 * HEADS, KERN), f32),
        scratch_shapes=[pltpu.VMEM((tile, span), f32)],
        compiler_params=pltpu.CompilerParams(vmem_limit_bytes=50 * MIB),
        cost_estimate=pl.CostEstimate(flops=1000, bytes_accessed=1000, transcendentals=0),
        name="bias_back",
    )(near, coord_all, lane_wide(means), lane_wide(curve), *ds, phi, *tokens)


def row_items(global_rows, group_rows, lengths, groups):
    count = lengths.shape[0]
    order = jnp.arange(count, dtype=jnp.int32)
    earlier = (groups[:, None] == groups[None, :]) & (order[None, :] < order[:, None])
    starts = jnp.sum(jnp.where(earlier, lengths[None, :], 0), axis=1)
    group_of = global_rows // group_rows
    place = global_rows - group_of * group_rows
    hits = (
        (groups[None, :] == group_of[:, None])
        & (place[:, None] >= starts[None, :])
        & (place[:, None] < starts[None, :] + lengths[None, :])
    )
    item = jnp.sum(jnp.where(hits, order[None, :], 0), axis=1)
    return (item, jnp.any(hits, axis=1))


PIECES = (1, 3, 2, 1, 1)


def swap_sides(block):
    return lax.ppermute(block, "mp", [(0, 1), (1, 0)])


class Shards:
    def __init__(self, partial, first_bits):
        chips = lax.axis_size("rows")
        bits = chips.bit_length() - 1
        stack, rows, columns = partial.shape
        self.kept = partial.reshape(stack, *[2] * bits, 2, rows // (2 * chips), columns)
        self.come = None
        self.left = list(range(bits))[::-1]
        self.order = [None] + [b for b in first_bits if b < bits] + [b for b in range(bits) if b not in first_bits]

    def half(self, axis, index):
        part = lax.dynamic_index_in_dim(self.kept, index, axis, keepdims=False)
        if self.come is None:
            return part
        come = lax.dynamic_index_in_dim(self.come, index, axis, keepdims=False)
        return part.astype(f32) + come.astype(f32)

    def prepare(self):
        self.bit = self.order.pop(0)
        if self.bit is None:
            axis, mine = 1 + len(self.left), lax.axis_index("mp")
        else:
            axis, mine = 1 + self.left.index(self.bit), (lax.axis_index("rows") >> self.bit) & 1
            self.left.remove(self.bit)
        self.send = self.half(axis, 1 - mine).astype(bf16)
        self.kept = self.half(axis, mine)

    def launch(self):
        chips = lax.axis_size("rows")
        if self.bit is None:
            self.come = swap_sides(self.send)
        else:
            self.come = lax.ppermute(self.send, "rows", [(n, n ^ (1 << self.bit)) for n in range(chips)])

    def total(self):
        while self.order:
            self.prepare()
            self.launch()
        return self.kept.astype(f32) + self.come.astype(f32)


def beside(shards, run, inputs):
    shards = [s for s in shards if s.order]
    for s in shards:
        s.prepare()
    held = [(s.send, s.kept) for s in shards]
    held, inputs = lax.optimization_barrier((held, inputs))
    for s, (send, kept) in zip(shards, held):
        s.send, s.kept = send, kept
        s.launch()
    out = run(*inputs)
    came, out = lax.optimization_barrier(([s.come for s in shards], out))
    for s, come in zip(shards, came):
        s.come = come
    return out


def everyone(visit):
    side_count = lax.axis_size("mp")
    count = lax.axis_size("rows") * side_count
    me = lax.axis_index("rows") * side_count + lax.axis_index("mp")

    def body(step, carry):
        visit(step, lax.rem(me + step, count), lax.rem(me + count - step, count))
        return carry

    lax.fori_loop(1, count, body, 0)
    return me


def address(device):
    side_count = lax.axis_size("mp")
    return (device // side_count, lax.rem(device, side_count))


def meet_everyone():
    barrier = pltpu.get_barrier_semaphore()

    def greet(step, target, source):
        pl.semaphore_signal(
            barrier, inc=1, device_id=address(target), device_id_type=pl.DeviceIdType.MESH
        )

    everyone(greet)
    pl.semaphore_wait(barrier, lax.axis_size("rows") * lax.axis_size("mp") - 1)


def remote(source_ref, target_ref, send_sem, recv_sem, device):
    return pltpu.make_async_remote_copy(
        src_ref=source_ref,
        dst_ref=target_ref,
        send_sem=send_sem,
        recv_sem=recv_sem,
        device_id=address(device),
        device_id_type=pl.DeviceIdType.MESH,
    )


def gather_kernel(*refs):
    *x_refs, out_ref, block_ref, send_sem, recv_sem = refs
    count, rows, lanes = out_ref.shape
    side_count = lax.axis_size("mp")
    me = lax.axis_index("rows") * side_count + lax.axis_index("mp")
    block = [
        jnp.concatenate([r[...].astype(f32), jnp.zeros((r.shape[0], lanes - r.shape[1]), f32)], axis=1)
        for r in x_refs
    ]
    block.append(jnp.zeros((rows - sum(r.shape[0] for r in x_refs), lanes), f32))
    block = jnp.concatenate(block, axis=0).astype(bf16)
    block_ref[...] = block
    meet_everyone()
    out_ref[me] = block

    def send(step, target, source):
        remote(block_ref, out_ref.at[me], send_sem.at[step], recv_sem.at[step], target).start()

    def wait(step, target, source):
        remote(block_ref, out_ref.at[source], send_sem.at[step], recv_sem.at[step], target).wait()

    everyone(send)
    everyone(wait)


def gather_small(vectors, count):
    return pl.pallas_call(
        gather_kernel,
        out_shape=jax.ShapeDtypeStruct((count, 16, 256), bf16),
        in_specs=[pl.BlockSpec(memory_space=pltpu.VMEM)] * len(vectors),
        out_specs=pl.BlockSpec(memory_space=pltpu.VMEM),
        scratch_shapes=[
            pltpu.VMEM((16, 256), bf16),
            pltpu.SemaphoreType.DMA((count,)),
            pltpu.SemaphoreType.DMA((count,)),
        ],
        compiler_params=pltpu.CompilerParams(
            collective_id=1, has_side_effects=True, vmem_limit_bytes=16 * MIB
        ),
        name="gather_small",
    )(*vectors)


def sum_kernel(x_ref, out_ref, come_ref, send_sem, recv_sem):
    side_count = lax.axis_size("mp")
    me = lax.axis_index("rows") * side_count + lax.axis_index("mp")
    meet_everyone()

    def send(step, target, source):
        remote(x_ref.at[target], come_ref.at[step], send_sem.at[step], recv_sem.at[step], target).start()

    def wait(step, target, source):
        remote(x_ref.at[target], come_ref.at[step], send_sem.at[step], recv_sem.at[step], target).wait()

    everyone(send)
    come_ref[0] = x_ref[me]
    everyone(wait)
    out_ref[...] = jnp.sum(come_ref[...].astype(f32), axis=0)


def sum_small(blocks):
    count = blocks.shape[0]
    return pl.pallas_call(
        sum_kernel,
        out_shape=jax.ShapeDtypeStruct(blocks.shape[1:], f32),
        in_specs=[pl.BlockSpec(memory_space=pltpu.VMEM)],
        out_specs=pl.BlockSpec(memory_space=pltpu.VMEM),
        scratch_shapes=[
            pltpu.VMEM(blocks.shape, blocks.dtype),
            pltpu.SemaphoreType.DMA((count,)),
            pltpu.SemaphoreType.DMA((count,)),
        ],
        compiler_params=pltpu.CompilerParams(
            collective_id=2, has_side_effects=True, vmem_limit_bytes=16 * MIB
        ),
        name="sum_small",
    )(blocks)


def lay_tables(share, count):
    lane = np.arange(share * count)
    place = lane[None, :] % share == np.arange(share)[:, None]
    mark = lane[None, :] // share == np.arange(count)[:, None]
    return jnp.asarray(place, bf16), jnp.asarray(mark, f32)


def joined(shares):
    count, vectors, share = shares.shape
    place, mark = lay_tables(share, count)
    wide = dot(shares.reshape(count * vectors, share), place).reshape(count, vectors, count * share)
    return jnp.sum(wide * mark[:, None, :], axis=0)


def cut(vectors, share):
    number, size = vectors.shape
    place, mark = lay_tables(share, size // share)
    wide = (vectors[None] * mark[:, None, :]).astype(bf16)
    out = lax.dot_general(wide, place, (((2,), (1,)), ((), ())), preferred_element_type=f32)
    return out.astype(bf16)


def on_device(
    atoms,
    time_embedding,
    coordinates,
    item_lengths,
    item_group,
    query_weight,
    key_weight,
    value_weight,
    out_weight,
    up_weight,
    down_weight,
    value_bias,
    out_bias,
    up_bias,
    down_bias,
    first_gain,
    first_shift,
    second_gain,
    second_shift,
    kernel_params,
    cotangent,
):
    rows_here = atoms.shape[0]
    pair_size = lax.axis_size("mp")
    side = lax.axis_index("mp")
    pair_index = lax.axis_index("rows")
    group_rows = rows_here * pair_size
    counter = jnp.arange(rows_here, dtype=jnp.int32)
    near_rows = (pair_index * pair_size + side) * rows_here + counter
    far_rows = (pair_index * pair_size + 1 - side) * rows_here + counter
    items = item_lengths.shape[0]
    near_item, near_valid = row_items(near_rows, group_rows, item_lengths, item_group)
    far_item, far_valid = row_items(far_rows, group_rows, item_lengths, item_group)
    near_code = jnp.where(near_valid, near_item, items + near_rows)
    far_code = jnp.where(far_valid, far_item, items + far_rows)
    all_code = jnp.concatenate([near_code, far_code])
    item = jnp.where(near_valid, near_item, -1)[:, None]
    valid = near_valid.astype(f32)[:, None]

    count = lax.axis_size("rows") * pair_size
    share, hidden = up_weight.shape
    width = query_weight.shape[1]
    blocks = hidden // width
    small = (value_bias, out_bias, down_bias, first_gain, first_shift, second_gain, second_shift)
    table_share = kernel_params.shape[0]
    gathered = gather_small((jnp.stack(small), up_bias[None], kernel_params[None]), count)
    value_b, out_b, down_b, gain_one, shift_one, gain_two, shift_two = joined(gathered[:, :7, :share])
    up_b = joined(gathered[:, 7:8, : blocks * share])[0]
    table = joined(gathered[:, 8:9, :table_share])[0]
    wide = lax.all_gather(
        jnp.concatenate([query_weight, key_weight, value_weight, out_weight, up_weight], axis=1),
        AXES,
        axis=0,
        tiled=True,
    )
    down_w = lax.all_gather(down_weight, AXES, axis=0, tiled=True)

    means, widths, mix = table[:KERN], table[KERN : 2 * KERN], table[2 * KERN :].reshape(KERN, HEADS)
    norm = 1.0 / (widths * math.sqrt(2.0 * math.pi))
    curve = (-0.5 * math.log2(math.e)) / (widths * widths)
    mix_low = (mix * norm[:, None] * math.log2(math.e)).astype(bf16)
    coord_low = coordinates.astype(bf16)
    coord_all = jnp.concatenate([coord_low, swap_sides(coord_low)], axis=1).astype(f32)
    near = coordinates.astype(f32).T
    bias, phi = pair_bias(near, coord_all, near_code[:, None], all_code[None], means, curve, mix_low)

    bias, wide = lax.optimization_barrier((bias, wide))
    h_zero, q4, near_kv = project(atoms, item, time_embedding, gain_one, shift_one, value_b, wide)
    far_kv = swap_sides(near_kv)
    expo, mixed4, inverse4 = attend(q4, near_kv, far_kv, bias)
    layer_out, grad_one, scaled4, down_grad, up_grad, out_grad, sums_two, up_sums = feed_forward(
        h_zero, mixed4, inverse4, valid, cotangent, wide, down_w, (out_b, up_b, down_b, gain_two, shift_two)
    )

    down_shards = Shards(down_grad[None], (0, 1))
    up_shards = Shards(up_grad[None], (1, 0))
    feed_shards = (down_shards, up_shards)
    half = NG // 2
    done = []
    for n in range(2):

        def run(scaled4):
            return attend_back(q4, scaled4, mixed4, near_kv, far_kv, expo, n * half, half), scaled4

        out, scaled4 = beside(feed_shards, run, (scaled4,))
        done.append(out)
    scores_grad = [d[0] for d in done]
    turned = [(d[2], swap_sides(d[3]), d[4], swap_sides(d[5])) for d in done]
    pairs = [done[0][1], done[1][1]]
    for m in (0, 2, 1, 3):
        pairs += [turned[0][m], turned[1][m]]
    atoms_grad, square_grads, sums_one = beside(
        feed_shards,
        lambda h_zero, *pairs: project_back(h_zero, grad_one, pairs, gain_one, shift_one, wide, out_grad),
        (h_zero, *pairs),
    )
    square_shards = Shards(square_grads, (0, 1))

    tiles = rows_here // 32
    moments = 0.0
    first = 0
    for eighths in PIECES:
        size = eighths * tiles // 8
        piece, near = beside(
            (square_shards, *feed_shards),
            lambda near: (bias_back(near, coord_all, means, curve, scores_grad, phi, first, size), near),
            (near,),
        )
        moments = moments + piece
        first += size
    zeroth = moments[:HEADS].T * norm[:, None]
    first = (moments[HEADS : 2 * HEADS] + moments[2 * HEADS : 3 * HEADS]).T * norm[:, None]
    twice = (moments[3 * HEADS : 4 * HEADS] + moments[4 * HEADS :]).T * norm[:, None]
    m_zero, m_one, m_two = [jnp.sum(mix * r, axis=1) for r in (zeroth, first, twice)]
    offset = means - CENTRE
    mean_grad = (m_one - offset * m_zero) / widths**2
    width_grad = (m_two - 2.0 * offset * m_one + offset * offset * m_zero) / widths**3 - m_zero / widths
    table_grad = jnp.concatenate([mean_grad, width_grad, zeroth.reshape(-1)])

    cuts = jnp.concatenate(
        [
            jnp.pad(
                cut(
                    jnp.stack(
                        [sums_one[2], sums_two[2], sums_two[3], sums_one[0], sums_one[1], sums_two[0], sums_two[1]]
                    ),
                    share,
                ),
                ((0, 0), (0, 0), (0, 256 - share)),
            ),
            jnp.pad(cut(up_sums[0:1], blocks * share), ((0, 0), (0, 0), (0, 256 - blocks * share))),
            jnp.pad(cut(table_grad[None], table_share), ((0, 0), (0, 7), (0, 256 - table_share))),
        ],
        axis=1,
    )
    sums = sum_small(cuts)
    square_sum = square_shards.total()
    return (
        layer_out,
        atoms_grad,
        square_sum[0],
        square_sum[1],
        square_sum[2],
        square_sum[3],
        up_shards.total()[0],
        down_shards.total()[0],
        sums[0, :share],
        sums[1, :share],
        sums[7, : blocks * share],
        sums[2, :share],
        sums[3, :share],
        sums[4, :share],
        sums[5, :share],
        sums[6, :share],
        sums[8, :table_share],
    )


def solution(mesh):
    row = P(AXES, None)
    vec = P(AXES)
    in_specs = (row, P(), P(None, AXES), P(), P(), *[row] * 6, *[vec] * 9, row)
    out_specs = (*[row] * 8, *[vec] * 9)
    return jax.shard_map(on_device, mesh=mesh, in_specs=in_specs, out_specs=out_specs, check_vma=False)
```

```python
import functools
import math

import jax
import jax.numpy as jnp
import numpy as np
from jax import lax
from jax.experimental import pallas as pl
from jax.experimental.pallas import tpu as pltpu
from jax.sharding import PartitionSpec as P

HEADS = 32
KERN = 128
HEAD = 24
GH = 8
NG = HEADS // GH
GW = GH * HEAD
MIB = 2**20
CENTRE = 6.0
STORED = 1
AXES = ("rows", "mp")
f32 = jnp.float32
bf16 = jnp.bfloat16


def dot(left, right):
    return jnp.dot(left, right, preferred_element_type=f32)


def turned_dot(left, right):
    return lax.dot_general(left, right, (((1,), (1,)), ((), ())), preferred_element_type=f32)


def sum_dot(left, right):
    return lax.dot_general(left, right, (((0,), (0,)), ((), ())), preferred_element_type=f32)


def whole(shape):
    return pl.BlockSpec(shape, lambda i: (0,) * len(shape))


def after(kernel, inputs, tokens):
    def run(*refs):
        kernel(*refs[:inputs], *refs[inputs + len(tokens) :])

    return run, [pl.BlockSpec(memory_space=pl.ANY)] * len(tokens)


def high_low(value):
    high = value.astype(bf16)
    return high, (value - high.astype(f32)).astype(bf16)


def distances(near_ref, all_ref):
    total = None
    for c in range(3):
        diff = near_ref[:, c : c + 1] - all_ref[c : c + 1, :]
        total = diff * diff if total is None else total + diff * diff
    return jnp.sqrt(total) * 0.25


def bias_kernel(
    pairs_step, near_ref, all_ref, code_near_ref, code_all_ref, means_ref, curve_ref, mix_ref,
    bias_ref, phi_ref, dist_ref, mask_ref,
):
    dist_ref[...] = distances(near_ref, all_ref)
    mask_ref[...] = jnp.where(code_near_ref[:, 0:1] == code_all_ref[0:1, :], 0.0, -1e30)
    rows, span = dist_ref.shape

    def body(step, carry):
        for q in range(pairs_step):
            pair = step * pairs_step + q
            drow = [dist_ref[pl.ds(pair * 2 + e, 1), :] for e in range(2)]
            mrow = [mask_ref[pl.ds(pair * 2 + e, 1), :] for e in range(2)]
            for lane in range(0, span, 256):
                tall = []
                for e in range(2):
                    wide = []
                    for low in (lane, lane + 128):
                        u = drow[e][:, low : low + 128] - means_ref[...]
                        wide.append(jnp.exp2((u * curve_ref[...]) * u).astype(bf16))
                    wide = jnp.concatenate(wide, axis=1)
                    if e < STORED:
                        phi_ref[pair * STORED + e, :, lane : lane + 256] = wide
                    tall.append(wide)
                out = dot(mix_ref[...], jnp.concatenate(tall, axis=0)).reshape(NG, 2, GH, 256)
                out = jnp.concatenate(
                    [out[:, e : e + 1] + mrow[e][:, lane : lane + 256].reshape(1, 1, 1, 256) for e in range(2)],
                    axis=1,
                )
                bias_ref[:, pl.ds(pl.multiple_of(pair * 16, 16), 16), lane : lane + 256] = out.reshape(
                    NG, 16, 256
                ).astype(bf16)
        return carry

    lax.fori_loop(0, rows // 2 // pairs_step, body, 0)


def lane_wide(values):
    return jnp.broadcast_to(values[:, None], (KERN, 128))


def pair_bias(near, coord_all, code_near, code_all, means, curve, mix_low, tile=32, pairs_step=16):
    rows, span = near.shape[0], coord_all.shape[1]
    m4 = mix_low.T.reshape(NG, GH, KERN)
    zero = jnp.zeros_like(m4)
    left = jnp.stack([jnp.concatenate([m4, zero], -1), jnp.concatenate([zero, m4], -1)], axis=1)
    left = left.reshape(2 * HEADS, 2 * KERN)
    return pl.pallas_call(
        functools.partial(bias_kernel, pairs_step),
        grid=(rows // tile,),
        in_specs=[
            pl.BlockSpec((tile, 3), lambda i: (i, 0)),
            whole((3, span)),
            pl.BlockSpec((tile, 1), lambda i: (i, 0)),
            whole((1, span)),
            whole((KERN, 128)),
            whole((KERN, 128)),
            whole((2 * HEADS, 2 * KERN)),
        ],
        out_specs=[
            pl.BlockSpec((NG, tile * GH, span), lambda i: (0, i, 0)),
            pl.BlockSpec((tile * STORED // 2, KERN, span), lambda i: (i, 0, 0)),
        ],
        out_shape=[
            jax.ShapeDtypeStruct((NG, rows * GH, span), bf16),
            jax.ShapeDtypeStruct((rows * STORED // 2, KERN, span), bf16),
        ],
        scratch_shapes=[pltpu.VMEM((tile, span), f32), pltpu.VMEM((tile, span), f32)],
        compiler_params=pltpu.CompilerParams(vmem_limit_bytes=50 * MIB),
        cost_estimate=pl.CostEstimate(flops=1000, bytes_accessed=1000, transcendentals=0),
        name="bias",
    )(near, coord_all, code_near, code_all, lane_wide(means), lane_wide(curve), left)


def repeat_tables(tile):
    row = np.arange(tile * GH)
    repeat = row[:, None] // GH == np.arange(tile)[None, :]
    own = row[:, None] % GH == np.arange(GW)[None, :] // HEAD
    return repeat, own


def project_kernel(
    atoms_ref, code_ref, time_ref, gain_ref, shift_ref, bias_ref, wide_ref,
    h_ref, q_ref, kv_ref,
):
    width = atoms_ref.shape[1]
    items = lax.broadcasted_iota(jnp.int32, (1, time_ref.shape[0]), 1)
    picks = (code_ref[...] == items).astype(f32).astype(bf16)
    h_zero = atoms_ref[...].astype(f32) + dot(picks, time_ref[...])
    h_ref[...] = h_zero
    centre = h_zero - jnp.mean(h_zero, axis=1, keepdims=True)
    rate = lax.rsqrt(jnp.mean(centre * centre, axis=1, keepdims=True) + 1e-05)
    normed = (centre * rate * gain_ref[...] + shift_ref[...]).astype(bf16)
    tile = h_zero.shape[0]
    lane = lax.broadcasted_iota(jnp.int32, (tile, 256 - GW), 1)
    ones = jnp.where(lane == 0, 1.0, 0.0)
    for n in (1, 2, 0):
        out = dot(normed, wide_ref[:, n * width : (n + 1) * width])
        if n == 2:
            out = out + bias_ref[...]
        for g in range(NG):
            part = out[:, g * GW : (g + 1) * GW]
            if n == 0:
                q_ref[g] = part.astype(bf16)
            else:
                part = jnp.concatenate([part, ones if n == 2 else jnp.zeros_like(ones)], axis=1)
                kv_ref[n - 1, g] = part.astype(bf16)


def project(atoms, code, time_embedding, gain, shift, value_bias, wide, tile=256):
    rows, width = atoms.shape
    return pl.pallas_call(
        project_kernel,
        grid=(rows // tile,),
        in_specs=[
            pl.BlockSpec((tile, width), lambda i: (i, 0)),
            pl.BlockSpec((tile, 1), lambda i: (i, 0)),
            whole(time_embedding.shape),
            *[whole((1, width))] * 3,
            whole((width, 3 * width)),
        ],
        out_specs=[
            pl.BlockSpec((tile, width), lambda i: (i, 0)),
            pl.BlockSpec((NG, tile, GW), lambda i: (0, i, 0)),
            pl.BlockSpec((2, NG, tile, 256), lambda i: (0, 0, i, 0)),
        ],
        out_shape=[
            jax.ShapeDtypeStruct((rows, width), f32),
            jax.ShapeDtypeStruct((NG, rows, GW), bf16),
            jax.ShapeDtypeStruct((2, NG, rows, 256), bf16),
        ],
        compiler_params=pltpu.CompilerParams(vmem_limit_bytes=40 * MIB),
        cost_estimate=pl.CostEstimate(flops=1000, bytes_accessed=1000, transcendentals=0),
        name="project",
    )(atoms, code, time_embedding, gain[None], shift[None], value_bias[None], wide)


def project_back_kernel(
    h_ref, grad_one_ref, q0_ref, q1_ref, k0_ref, k1_ref, v0_ref, v1_ref, kc0_ref, kc1_ref, vc0_ref, vc1_ref,
    gain_ref, shift_ref, wide_ref, out_grad_ref,
    atoms_grad_ref, grads_ref, sums_ref, normed_s, grad_s,
):
    rows, width = h_ref.shape
    for g in range(NG):
        q_ref, k_ref, v_ref, kc_ref, vc_ref = (
            (q0_ref, k0_ref, v0_ref, kc0_ref, vc0_ref) if g < NG // 2 else (q1_ref, k1_ref, v1_ref, kc1_ref, vc1_ref)
        )
        m = g % (NG // 2)
        cols = slice(g * GW, (g + 1) * GW)
        grad_s[0, :, cols] = q_ref[m]
        grad_s[1, :, cols] = (k_ref[m] + kc_ref[m].astype(f32)).T.astype(bf16)
        grad_s[2, :, cols] = (v_ref[m] + vc_ref[m].astype(f32)).T.astype(bf16)
    h_zero = h_ref[...]
    centre = h_zero - jnp.mean(h_zero, axis=1, keepdims=True)
    rate = lax.rsqrt(jnp.mean(centre * centre, axis=1, keepdims=True) + 1e-05)
    hat = centre * rate
    normed_s[...] = (hat * gain_ref[...] + shift_ref[...]).astype(bf16)
    grads_ref[3] = out_grad_ref[...]
    grad = None
    for n in range(3):
        grads_ref[n] = sum_dot(normed_s[...], grad_s[n]).astype(bf16)
        part = turned_dot(grad_s[n], wide_ref[:, n * width : (n + 1) * width])
        grad = part if grad is None else grad + part
    g = grad * gain_ref[...]
    atoms_grad_ref[...] = grad_one_ref[...] + rate * (
        g - jnp.mean(g, axis=1, keepdims=True) - hat * jnp.mean(g * hat, axis=1, keepdims=True)
    )
    sums_ref[...] = jnp.zeros_like(sums_ref)
    sums_ref[0:1, :] = jnp.sum(grad * hat, axis=0, keepdims=True)
    sums_ref[1:2, :] = jnp.sum(grad, axis=0, keepdims=True)
    sums_ref[2:3, :] = dot(jnp.ones((8, rows), bf16), grad_s[2])[0:1]


def project_back(h_zero, grad_one, pairs, gain, shift, wide, out_grad, tokens=()):
    rows, width = h_zero.shape
    once = pl.Buffered(1)
    kernel, token_specs = after(project_back_kernel, 16, tokens)
    return pl.pallas_call(
        kernel,
        grid=(1,),
        in_specs=[
            whole((rows, width)),
            whole((rows, width)),
            *[whole(p.shape) for p in pairs],
            *[whole((1, width))] * 2,
            pl.BlockSpec((width, 3 * width), lambda i: (0, 0), pipeline_mode=once),
            whole((width, width)),
            *token_specs,
        ],
        out_specs=[whole((rows, width)), whole((NG, width, width)), whole((8, width))],
        out_shape=[
            jax.ShapeDtypeStruct((rows, width), f32),
            jax.ShapeDtypeStruct((4, width, width), bf16),
            jax.ShapeDtypeStruct((8, width), f32),
        ],
        scratch_shapes=[pltpu.VMEM((rows, width), bf16), pltpu.VMEM((3, rows, width), bf16)],
        compiler_params=pltpu.CompilerParams(vmem_limit_bytes=56 * MIB),
        cost_estimate=pl.CostEstimate(flops=1000, bytes_accessed=1000, transcendentals=0),
        name="project_back",
    )(h_zero, grad_one, *pairs, gain[None], shift[None], wide, out_grad, *tokens)


def attend_kernel(
    tiles, q_ref, near_ref, far_ref, b_ref, rep_ref, rept_ref, own_ref, scaled_ref,
    e_ref, mixed_ref, inv_ref, qa, qb, sa, sb, ea, oa, ob, wa, wb,
):
    keys, values = (near_ref.at[0], far_ref.at[0]), (near_ref.at[1], far_ref.at[1])
    query, scores, outs, wides = (qa, qb), (sa, sb), (oa, ob), (wa, wb)
    rows, span = sa.shape
    held = rows // GH
    units = NG * tiles
    parts, chunk, ahead = 4, 8, 3
    step, some = span // parts, rows // parts
    pid = pl.program_id(0)

    def place(unit):
        unit = jnp.clip(unit, 0, units - 1)
        group = unit // tiles
        return group, pl.ds(pl.multiple_of((unit - group * tiles) * held, held), held)

    def spread(unit, par):
        g, i = place(unit)
        query[par][...] = (dot(rep_ref[...], q_ref[g, i, :]) * scaled_ref[...]).astype(bf16)

    def score(unit, par, part):
        g, _ = place(unit)
        cols = slice(part * step, (part + 1) * step)
        there = slice(part % 2 * step, (part % 2 + 1) * step)
        scores[par][:, cols] = turned_dot(query[par][...], keys[part // 2][g, there, :GW])

    def soften(par, part):
        chunks = range(part * some, (part + 1) * some, chunk)
        held_x = {}
        for n in range(len(chunks) + ahead):
            if n < len(chunks):
                here = slice(chunks[n], chunks[n] + chunk)
                x = scores[par][here, :] + b_ref[par, here, :].astype(f32)
                held_x[n] = x, jnp.max(x, axis=1, keepdims=True)
            if n >= ahead:
                here = slice(chunks[n - ahead], chunks[n - ahead] + chunk)
                x, top = held_x.pop(n - ahead)
                e = jnp.exp2(x - top).astype(bf16)
                e_ref[par, here, :] = e
                if par == 1:
                    ea[here, :] = e

    def mix(unit, par, part):
        g, _ = place(unit)
        here = slice(part * some, (part + 1) * some)
        source = e_ref.at[0] if par == 0 else ea
        half = span // 2
        outs[par][here, :] = dot(source[here, :half], values[0][g]) + dot(source[here, half:], values[1][g])

    def scale(par, part):
        here = slice(part * some, (part + 1) * some)
        out = outs[par][here, :]
        inv = 1.0 / out[:, GW : GW + 1]
        own = own_ref[here, :]
        wides[par][here, :] = jnp.concatenate(
            [*high_low(out[:, :GW] * inv * own), *high_low(inv * own)], axis=1
        )

    def gather(unit, par):
        g, i = place(unit)
        out = dot(rept_ref[...], wides[par][...])
        mixed_ref[g, i, :] = out[:, :GW] + out[:, GW : 2 * GW]
        inv_ref[g, i, :] = out[:, 2 * GW : 3 * GW] + out[:, 3 * GW :]

    @pl.when(pid == 0)
    def _():
        spread(0, 0)
        for part in range(parts):
            score(0, 0, part)
        spread(1, 1)
        ea[...] = jnp.ones_like(ea)
        for ref in (oa, ob):
            ref[...] = jnp.ones_like(ref)
        for ref in (wa, wb):
            ref[...] = jnp.zeros_like(ref)

    for par in range(2):
        unit = pid * 2 + par
        for part in range(parts):
            score(unit + 1, 1 - par, part)
            scale(par, part)
            mix(unit - 1, 1 - par, part)
            if part == 1:
                spread(unit + 2, par)
            if part == 2:
                gather(unit - 3, 1 - par)
            soften(par, part)

    @pl.when(pid == units // 2 - 1)
    def _():
        for part in range(parts):
            scale(0, part)
            mix(units - 1, 1, part)
        gather(units - 3, 1)
        gather(units - 2, 0)
        for part in range(parts):
            scale(1, part)
        gather(units - 1, 1)


def attend(q4, near, far, bias, tile=64):
    rows = q4.shape[1]
    span = 2 * rows
    tiles = rows // tile
    repeat, own = repeat_tables(tile)
    deep = tile * GH
    bias = bias.reshape(NG * tiles, deep, span)
    big = pl.BlockSpec((2, deep, span), lambda i: (i, 0, 0))
    scale = HEAD**-0.5 * math.log2(math.e)
    e, mixed, inv = pl.pallas_call(
        functools.partial(attend_kernel, tiles),
        grid=(NG * tiles // 2,),
        in_specs=[
            whole((NG, rows, GW)),
            *[whole((2, NG, rows, 256))] * 2,
            big,
            whole((deep, tile)),
            whole((tile, deep)),
            whole((deep, GW)),
            whole((deep, GW)),
        ],
        out_specs=[big, whole((NG, rows, GW)), whole((NG, rows, GW))],
        out_shape=[
            jax.ShapeDtypeStruct((NG * tiles, deep, span), bf16),
            jax.ShapeDtypeStruct((NG, rows, GW), f32),
            jax.ShapeDtypeStruct((NG, rows, GW), f32),
        ],
        scratch_shapes=[pltpu.VMEM((deep, GW), bf16)] * 2
        + [pltpu.VMEM((deep, span), f32)] * 2
        + [pltpu.VMEM((deep, span), bf16)]
        + [pltpu.VMEM((deep, 256), f32)] * 2
        + [pltpu.VMEM((deep, 4 * GW), bf16)] * 2,
        compiler_params=pltpu.CompilerParams(vmem_limit_bytes=50 * MIB),
        cost_estimate=pl.CostEstimate(flops=1000, bytes_accessed=1000, transcendentals=0),
        name="attend",
    )(
        q4, near, far, bias, jnp.asarray(repeat, bf16), jnp.asarray(repeat.T, bf16),
        jnp.asarray(own, f32), jnp.asarray(own * scale, f32),
    )
    return e.reshape(NG, rows * GH, span), mixed, inv


def attend_back_kernel(
    tiles, q_ref, gs_ref, mx_ref, near_ref, far_ref, e_ref, rep_ref, rept_ref, own_ref, ownt_ref,
    ds_ref, dq_ref, dk_near_ref, dk_far_ref, dv_near_ref, dv_far_ref,
    ga, gb, da, db, qta, qtb, gta, gtb, sa, sb, kept, oa, ob, wa, wb, dk, dv,
):
    keys, values = (near_ref.at[0], far_ref.at[0]), (near_ref.at[1], far_ref.at[1])
    grads, deltas, queries_t, grads_t = (ga, gb), (da, db), (qta, qtb), (gta, gtb)
    scores, outs, wides = (sa, sb), (oa, ob), (wa, wb)
    deep, span = sa.shape
    held = deep // GH
    units = q_ref.shape[0] * tiles
    parts, chunk = 4, 8
    step, some = span // parts, deep // parts
    scale = HEAD**-0.5
    pid = pl.program_id(0)

    def place(unit):
        unit = jnp.clip(unit, 0, units - 1)
        group = unit // tiles
        return group, pl.ds(pl.multiple_of((unit - group * tiles) * held, held), held)

    def begin_scores(unit, par):
        g, i = place(unit)
        grads[par][...] = (dot(rep_ref[...], gs_ref[g, i, :]) * own_ref[...]).astype(bf16)

    def begin_rest(unit, par):
        g, i = place(unit)
        gs = gs_ref[g, i, :]
        wide = dot(rep_ref[...], jnp.concatenate(high_low(gs.astype(f32) * mx_ref[g, i, :]), axis=1))
        deltas[par][...] = jnp.sum((wide[:, :GW] + wide[:, GW:]) * own_ref[...], axis=1, keepdims=True)
        grads_t[par][...] = (sum_dot(gs, rept_ref[...]) * ownt_ref[...]).astype(bf16)

    def turn_query(unit, par):
        g, i = place(unit)
        queries_t[par][...] = (sum_dot(q_ref[g, i, :], rept_ref[...]) * ownt_ref[...]).astype(bf16)

    def grad_probs(unit, par, part):
        g, _ = place(unit)
        cols = slice(part * step, (part + 1) * step)
        there = slice(part % 2 * step, (part % 2 + 1) * step)
        scores[par][:, cols] = turned_dot(grads[par][...], values[part // 2][g, there, :GW])

    def soften(par, part):
        for c in range(part * some, (part + 1) * some, chunk):
            here = slice(c, c + chunk)
            ds = (e_ref[par, here, :].astype(f32) * (scores[par][here, :] - deltas[par][here, :])).astype(bf16)
            ds_ref[par, here, :] = ds
            if par == 1:
                kept[here, :] = ds

    def value_grad(unit, par, part):
        g, _ = place(unit)
        cols = slice(part * step, (part + 1) * step)
        dv[g, :, cols] += dot(grads_t[par][...], e_ref[par, :, cols])

    def key_grad(unit, par, part):
        g, _ = place(unit)
        cols = slice(part * step, (part + 1) * step)
        source = ds_ref.at[0] if par == 0 else kept
        dk[g, :, cols] += dot(queries_t[par][...], source[:, cols])

    def query_grad(unit, par, part):
        g, _ = place(unit)
        here = slice(part * some, (part + 1) * some)
        source = ds_ref.at[0] if par == 0 else kept
        half = span // 2
        outs[par][here, :] = dot(source[here, :half], keys[0][g, :, :GW]) + dot(
            source[here, half:], keys[1][g, :, :GW]
        )

    def mask(par):
        wides[par][...] = (outs[par][...] * own_ref[...]).astype(bf16)

    def gather(unit, par):
        g, i = place(unit)
        dq_ref[g, i, :] = (dot(rept_ref[...], wides[par][...]) * scale).astype(bf16)

    @pl.when(pid == 0)
    def _():
        dk[...] = jnp.zeros_like(dk)
        dv[...] = jnp.zeros_like(dv)
        begin_scores(0, 0)
        for part in range(parts):
            grad_probs(0, 0, part)
        begin_scores(1, 1)
        begin_rest(0, 0)
        queries_t[1][...] = jnp.zeros_like(queries_t[1])
        kept[...] = jnp.zeros_like(kept)
        for ref in (oa, ob, wa, wb):
            ref[...] = jnp.zeros_like(ref)

    for par in range(2):
        unit = pid * 2 + par
        for part in range(parts):
            grad_probs(unit + 1, 1 - par, part)
            value_grad(unit, par, part)
            if part == 0:
                begin_scores(unit + 2, par)
                gather(unit - 3, 1 - par)
            if part == 1:
                begin_rest(unit + 1, 1 - par)
            if part == 2:
                turn_query(unit, par)
            if part == 3:
                mask(par)
            key_grad(unit - 1, 1 - par, part)
            query_grad(unit - 1, 1 - par, part)
            soften(par, part)

    @pl.when(pid == units // 2 - 1)
    def _():
        last = units - 1
        gather(last - 2, 1)
        mask(0)
        for part in range(parts):
            key_grad(last, 1, part)
            query_grad(last, 1, part)
        gather(last - 1, 0)
        mask(1)
        gather(last, 1)
        half = span // 2
        dk_near_ref[...] = dk[:, :, :half] * scale
        dk_far_ref[...] = (dk[:, :, half:] * scale).astype(bf16)
        dv_near_ref[...] = dv[:, :, :half]
        dv_far_ref[...] = dv[:, :, half:].astype(bf16)


def attend_back(q4, gs4, mx4, near_kv, far_kv, e, first, groups, tokens=(), tile=64):
    rows = q4.shape[1]
    span = 2 * rows
    tiles = rows // tile
    deep = tile * GH
    repeat, own = repeat_tables(tile)
    e = e.reshape(NG * tiles, deep, span)
    block = first // groups
    ahead = first * tiles // 2
    held = lambda wide: pl.BlockSpec((groups, rows, wide), lambda i: (block, 0, 0))
    near = jax.ShapeDtypeStruct((groups, GW, rows), f32)
    far = jax.ShapeDtypeStruct((groups, GW, rows), bf16)
    kernel, token_specs = after(functools.partial(attend_back_kernel, tiles), 10, tokens)
    ds, *rest = pl.pallas_call(
        kernel,
        grid=(groups * tiles // 2,),
        in_specs=[
            *[held(GW)] * 3,
            *[pl.BlockSpec((2, groups, rows, 256), lambda i: (0, block, 0, 0))] * 2,
            pl.BlockSpec((2, deep, span), lambda i: (i + ahead, 0, 0)),
            whole((deep, tile)),
            whole((tile, deep)),
            whole((deep, GW)),
            whole((GW, deep)),
            *token_specs,
        ],
        out_specs=[
            pl.BlockSpec((2, deep, span), lambda i: (i, 0, 0)),
            whole((groups, rows, GW)),
            *[whole((groups, GW, rows))] * 4,
        ],
        out_shape=[
            jax.ShapeDtypeStruct((groups * tiles, deep, span), bf16),
            jax.ShapeDtypeStruct((groups, rows, GW), bf16),
            near,
            far,
            near,
            far,
        ],
        scratch_shapes=[pltpu.VMEM((deep, GW), bf16)] * 2
        + [pltpu.VMEM((deep, 1), f32)] * 2
        + [pltpu.VMEM((GW, deep), bf16)] * 4
        + [pltpu.VMEM((deep, span), f32)] * 2
        + [pltpu.VMEM((deep, span), bf16)]
        + [pltpu.VMEM((deep, GW), f32)] * 2
        + [pltpu.VMEM((deep, GW), bf16)] * 2
        + [pltpu.VMEM((groups, GW, span), f32)] * 2,
        compiler_params=pltpu.CompilerParams(vmem_limit_bytes=50 * MIB),
        cost_estimate=pl.CostEstimate(flops=1000, bytes_accessed=1000, transcendentals=0),
        name="attend_back",
    )(
        q4, gs4, mx4, near_kv, far_kv, e, jnp.asarray(repeat, bf16), jnp.asarray(repeat.T, bf16),
        jnp.asarray(own, f32), jnp.asarray(own.T, f32), *tokens,
    )
    return (ds.reshape(groups, rows * GH, span), *rest)


def feed_kernel(
    row_steps, h_ref, mixed_ref, inv_ref, valid_ref, cot_ref, out_w_ref, up_w_ref, down_w_ref,
    out_b_ref, up_b_ref, down_b_ref, gain_ref, shift_ref,
    layer_ref, grad_one_ref, gs_ref, down_grad_ref, up_grad_ref, out_grad_ref, sums_ref, up_sums_ref,
    act_s, gup_s, second_s, gatt_s, gffn_s, mixed_s, up_s, gact_s,
):
    step = pl.program_id(0)
    tile, width = h_ref.shape
    hidden = up_w_ref.shape[1]
    some = 32

    @pl.when(step == 0)
    def _():
        sums_ref[...] = jnp.zeros_like(sums_ref)

    @pl.when(step < row_steps)
    def _():
        here = pl.ds(pl.multiple_of(step * tile, tile), tile)
        h_one = h_ref[...] + out_b_ref[...]
        for g in range(NG):
            mixed = mixed_ref[g].astype(bf16)
            mixed_s[g, here, :] = mixed
            h_one = h_one + dot(mixed, out_w_ref[g * GW : (g + 1) * GW, :])
        centre = h_one - jnp.mean(h_one, axis=1, keepdims=True)
        rate = lax.rsqrt(jnp.mean(centre * centre, axis=1, keepdims=True) + 1e-05)
        second = (centre * rate * gain_ref[...] + shift_ref[...]).astype(bf16)
        second_s[here, :] = second
        grad_two = cot_ref[...].astype(f32) * valid_ref[...]
        grad_ffn = grad_two.astype(bf16)
        gffn_s[here, :] = grad_ffn
        h_two = h_one + down_b_ref[...]
        grad_second = None
        for low in range(0, hidden, width):
            cols = slice(low, low + width)
            up_s[...] = dot(second, up_w_ref[:, cols]) + up_b_ref[:, cols]
            gact_s[...] = turned_dot(grad_ffn, down_w_ref[cols, :])

            def bend(n, carry):
                rows = pl.ds(pl.multiple_of(n * some, some), some)
                at = pl.ds(pl.multiple_of(step * tile + n * some, some), some)
                up = up_s[rows, :]
                below = 0.5 + 0.5 * lax.erf(up * (2.0**-0.5))
                slope = below + up * (jnp.exp(-0.5 * up * up) * (2.0 * math.pi) ** -0.5)
                act_s[at, cols] = (up * below).astype(bf16)
                gup_s[at, cols] = (gact_s[rows, :] * slope).astype(bf16)
                return carry

            lax.fori_loop(0, tile // some, bend, 0)
            h_two = h_two + dot(act_s[here, cols], down_w_ref[cols, :])
            part = turned_dot(gup_s[here, cols], up_w_ref[:, cols])
            grad_second = part if grad_second is None else grad_second + part
        layer_ref[...] = (h_two * valid_ref[...]).astype(bf16)
        hat = centre * rate
        sums_ref[0:1, :] += jnp.sum(grad_second * hat, axis=0, keepdims=True)
        sums_ref[1:2, :] += jnp.sum(grad_second, axis=0, keepdims=True)
        g = grad_second * gain_ref[...]
        grad_one = grad_two + rate * (
            g - jnp.mean(g, axis=1, keepdims=True) - hat * jnp.mean(g * hat, axis=1, keepdims=True)
        )
        grad_one_ref[...] = grad_one
        grad_att = grad_one.astype(bf16)
        gatt_s[here, :] = grad_att
        for g in range(NG):
            grad_mixed = turned_dot(grad_att, out_w_ref[g * GW : (g + 1) * GW, :]).astype(bf16)
            gs_ref[g] = (grad_mixed.astype(f32) * inv_ref[g]).astype(bf16)

    for n in range(WEIGHT_STEPS):

        @pl.when(step == row_steps + n)
        def _():
            size = hidden // WEIGHT_STEPS
            cols = slice(n * size, (n + 1) * size)
            down_grad_ref[...] = sum_dot(act_s[:, cols], gffn_s[...]).astype(bf16)
            up_grad_ref[...] = sum_dot(second_s[...], gup_s[:, cols]).astype(bf16)
            ones = jnp.ones((8, act_s.shape[0]), bf16)
            up_sums_ref[...] = dot(ones, gup_s[:, cols])
            if n < NG:
                out_grad_ref[n * GW : (n + 1) * GW, :] = sum_dot(mixed_s[n], gatt_s[...]).astype(bf16)
            if n == WEIGHT_STEPS - 1:
                sums_ref[2:3, :] = dot(ones, gatt_s[...])[0:1]
                sums_ref[3:4, :] = dot(ones, gffn_s[...])[0:1]


WEIGHT_STEPS = 8


def feed_forward(h_zero, mixed4, inverse4, valid, cotangent, wide, down_w, vectors, tile=256):
    rows, width = h_zero.shape
    hidden = down_w.shape[0]
    row_steps = rows // tile
    last = row_steps - 1
    size = hidden // WEIGHT_STEPS
    row = lambda i: (jnp.minimum(i, last), 0)
    row4 = lambda i: (0, jnp.minimum(i, last), 0)
    after = lambda i: jnp.maximum(i - row_steps, 0)
    once = pl.Buffered(1)
    return pl.pallas_call(
        functools.partial(feed_kernel, row_steps),
        grid=(row_steps + WEIGHT_STEPS,),
        in_specs=[
            pl.BlockSpec((tile, width), row),
            pl.BlockSpec((NG, tile, GW), row4),
            pl.BlockSpec((NG, tile, GW), row4),
            pl.BlockSpec((tile, 1), row),
            pl.BlockSpec((tile, width), row),
            pl.BlockSpec((width, width), lambda i: (0, 3), pipeline_mode=once),
            pl.BlockSpec((width, hidden), lambda i: (0, 1), pipeline_mode=once),
            pl.BlockSpec((hidden, width), lambda i: (0, 0), pipeline_mode=once),
            *[whole((1, v.shape[0])) for v in vectors],
        ],
        out_specs=[
            pl.BlockSpec((tile, width), row),
            pl.BlockSpec((tile, width), row),
            pl.BlockSpec((NG, tile, GW), row4),
            pl.BlockSpec((size, width), lambda i: (after(i), 0)),
            pl.BlockSpec((width, size), lambda i: (0, after(i))),
            whole((width, width)),
            whole((8, width)),
            pl.BlockSpec((8, size), lambda i: (0, after(i))),
        ],
        out_shape=[
            jax.ShapeDtypeStruct((rows, width), bf16),
            jax.ShapeDtypeStruct((rows, width), f32),
            jax.ShapeDtypeStruct((NG, rows, GW), bf16),
            jax.ShapeDtypeStruct((hidden, width), bf16),
            jax.ShapeDtypeStruct((width, hidden), bf16),
            jax.ShapeDtypeStruct((width, width), bf16),
            jax.ShapeDtypeStruct((8, width), f32),
            jax.ShapeDtypeStruct((8, hidden), f32),
        ],
        scratch_shapes=[
            pltpu.VMEM((rows, hidden), bf16),
            pltpu.VMEM((rows, hidden), bf16),
            pltpu.VMEM((rows, width), bf16),
            pltpu.VMEM((rows, width), bf16),
            pltpu.VMEM((rows, width), bf16),
            pltpu.VMEM((NG, rows, GW), bf16),
            pltpu.VMEM((tile, width), f32),
            pltpu.VMEM((tile, width), f32),
        ],
        compiler_params=pltpu.CompilerParams(vmem_limit_bytes=56 * MIB),
        cost_estimate=pl.CostEstimate(flops=1000, bytes_accessed=1000, transcendentals=0),
        name="feed_forward",
    )(h_zero, mixed4, inverse4, valid, cotangent, wide, wide, down_w, *[v[None] for v in vectors])


def bias_back_kernel(
    pairs_step, near_ref, all_ref, means_ref, curve_ref, ds0_ref, ds1_ref, phi_ref, out_ref, dist_ref
):
    dist_ref[...] = distances(near_ref, all_ref)
    rows, span = dist_ref.shape

    @pl.when(pl.program_id(0) == 0)
    def _():
        out_ref[...] = jnp.zeros_like(out_ref)

    def body(step, acc):
        for q in range(pairs_step):
            pair = step * pairs_step + q
            here = pl.ds(pl.multiple_of(pair * 16, 16), 16)
            both = jnp.concatenate([ds0_ref[:, here, :].astype(f32), ds1_ref[:, here, :].astype(f32)], axis=0)
            for e in range(2):
                d = dist_ref[pl.ds(pair * 2 + e, 1), :]
                if e < STORED:
                    phi = phi_ref[pair * STORED + e]
                else:
                    wide = []
                    for lane in range(0, span, 128):
                        u = (d[:, lane : lane + 128] - means_ref[...]).astype(bf16)
                        wide.append(jnp.exp2((u * curve_ref[...]) * u))
                    phi = jnp.concatenate(wide, axis=1)
                d = d - CENTRE
                s = both[:, e * GH : (e + 1) * GH, :].reshape(HEADS, span)
                one = s * d
                x = jnp.concatenate([s.astype(bf16), *high_low(one), *high_low(one * d)], axis=0)
                acc = acc + lax.dot_general(
                    x, phi, (((1,), (1,)), ((), ())), preferred_element_type=f32
                )
        return acc

    out_ref[...] += lax.fori_loop(0, rows // 2 // pairs_step, body, jnp.zeros(out_ref.shape, f32))


def bias_back(near, coord_all, means, curve, ds, phi, first, count, tokens=(), tile=32, pairs_step=16):
    span = coord_all.shape[1]
    rows = count * tile
    kernel, token_specs = after(functools.partial(bias_back_kernel, pairs_step), 7, tokens)
    return pl.pallas_call(
        kernel,
        grid=(count,),
        in_specs=[
            pl.BlockSpec((tile, 3), lambda i: (i + first, 0)),
            whole((3, span)),
            whole((KERN, 128)),
            whole((KERN, 128)),
            pl.BlockSpec((NG // 2, tile * GH, span), lambda i: (0, i + first, 0)),
            pl.BlockSpec((NG // 2, tile * GH, span), lambda i: (0, i + first, 0)),
            pl.BlockSpec((tile * STORED // 2, KERN, span), lambda i: (i + first, 0, 0)),
            *token_specs,
        ],
        out_specs=whole((5 * HEADS, KERN)),
        out_shape=jax.ShapeDtypeStruct((5 * HEADS, KERN), f32),
        scratch_shapes=[pltpu.VMEM((tile, span), f32)],
        compiler_params=pltpu.CompilerParams(vmem_limit_bytes=50 * MIB),
        cost_estimate=pl.CostEstimate(flops=1000, bytes_accessed=1000, transcendentals=0),
        name="bias_back",
    )(near, coord_all, lane_wide(means), lane_wide(curve).astype(bf16), *ds, phi, *tokens)


def row_items(global_rows, group_rows, lengths, groups):
    count = lengths.shape[0]
    order = jnp.arange(count, dtype=jnp.int32)
    earlier = (groups[:, None] == groups[None, :]) & (order[None, :] < order[:, None])
    starts = jnp.sum(jnp.where(earlier, lengths[None, :], 0), axis=1)
    group_of = global_rows // group_rows
    place = global_rows - group_of * group_rows
    hits = (
        (groups[None, :] == group_of[:, None])
        & (place[:, None] >= starts[None, :])
        & (place[:, None] < starts[None, :] + lengths[None, :])
    )
    item = jnp.sum(jnp.where(hits, order[None, :], 0), axis=1)
    return (item, jnp.any(hits, axis=1))


PIECES = (1, 3, 2, 2)


def swap_sides(block):
    return lax.ppermute(block, "mp", [(0, 1), (1, 0)])


class Shards:
    def __init__(self, partial, first_bits, joint):
        chips = lax.axis_size("rows")
        bits = chips.bit_length() - 1
        stack, rows, columns = partial.shape
        self.kept = partial.reshape(stack, *[2] * bits, 2, rows // (2 * chips), columns)
        self.come = []
        order = [b for b in first_bits if b < bits] + [b for b in range(bits) if b not in first_bits]
        self.turn = [0] + [bits - b for b in order] + [bits + 1, bits + 2]
        single = len(order) - 2 if joint else len(order)
        self.order = [None] + [(b,) for b in order[:single]]
        if joint:
            self.order.append(tuple(order[single:]))

    def part(self, axis, places):
        out = None
        for value in [self.kept, *self.come]:
            for place in places:
                value = lax.dynamic_index_in_dim(value, place, axis, keepdims=False)
            if self.come:
                value = value.astype(f32)
            out = value if out is None else out + value
        return out

    def prepare(self):
        bits = self.order.pop(0)
        if bits is None:
            mine = lax.axis_index("mp")
            axis = self.kept.ndim - 3
            self.send = [self.part(axis, [1 - mine]).transpose(self.turn)]
            self.kept = self.part(axis, [mine]).transpose(self.turn)
            self.flips = None
            return
        place = lax.axis_index("rows")
        mine = [(place >> b) & 1 for b in bits]
        self.flips, self.send = [], []
        for m in range(1, 1 << len(bits)):
            flip = [(m >> n) & 1 for n in range(len(bits))]
            self.flips.append(sum(f << b for f, b in zip(flip, bits)))
            self.send.append(self.part(1, [v ^ f for v, f in zip(mine, flip)]).astype(bf16))
        self.kept = self.part(1, mine)

    def launch(self):
        chips = lax.axis_size("rows")
        if self.flips is None:
            self.come = [swap_sides(self.send[0])]
        else:
            self.come = [
                lax.ppermute(send, "rows", [(n, n ^ flip) for n in range(chips)])
                for send, flip in zip(self.send, self.flips)
            ]

    def total(self):
        while self.order:
            self.prepare()
            self.launch()
        return self.kept.astype(f32) + sum(c.astype(f32) for c in self.come)


def beside(shards, run, inputs):
    shards = [s for s in shards if s.order]
    for s in shards:
        s.prepare()
    held = [(s.send, s.kept) for s in shards]
    held, inputs = lax.optimization_barrier((held, inputs))
    for s, (send, kept) in zip(shards, held):
        s.send, s.kept = send, kept
        s.launch()
    out = run(*inputs)
    came, out = lax.optimization_barrier(([s.come for s in shards], out))
    for s, come in zip(shards, came):
        s.come = come
    return out


def everyone(visit):
    side_count = lax.axis_size("mp")
    count = lax.axis_size("rows") * side_count
    me = lax.axis_index("rows") * side_count + lax.axis_index("mp")

    def body(step, carry):
        visit(step, lax.rem(me + step, count), lax.rem(me + count - step, count))
        return carry

    lax.fori_loop(1, count, body, 0)
    return me


def address(device):
    side_count = lax.axis_size("mp")
    return (device // side_count, lax.rem(device, side_count))


def meet_everyone():
    barrier = pltpu.get_barrier_semaphore()

    def greet(step, target, source):
        pl.semaphore_signal(
            barrier, inc=1, device_id=address(target), device_id_type=pl.DeviceIdType.MESH
        )

    everyone(greet)
    pl.semaphore_wait(barrier, lax.axis_size("rows") * lax.axis_size("mp") - 1)


def remote(source_ref, target_ref, send_sem, recv_sem, device):
    return pltpu.make_async_remote_copy(
        src_ref=source_ref,
        dst_ref=target_ref,
        send_sem=send_sem,
        recv_sem=recv_sem,
        device_id=address(device),
        device_id_type=pl.DeviceIdType.MESH,
    )


def gather_kernel(*refs):
    *x_refs, out_ref, block_ref, send_sem, recv_sem = refs
    count, rows, lanes = out_ref.shape
    side_count = lax.axis_size("mp")
    me = lax.axis_index("rows") * side_count + lax.axis_index("mp")
    block = [
        jnp.concatenate([r[...].astype(f32), jnp.zeros((r.shape[0], lanes - r.shape[1]), f32)], axis=1)
        for r in x_refs
    ]
    block.append(jnp.zeros((rows - sum(r.shape[0] for r in x_refs), lanes), f32))
    block = jnp.concatenate(block, axis=0).astype(bf16)
    block_ref[...] = block
    meet_everyone()
    out_ref[me] = block

    def send(step, target, source):
        remote(block_ref, out_ref.at[me], send_sem.at[step], recv_sem.at[step], target).start()

    def wait(step, target, source):
        remote(block_ref, out_ref.at[source], send_sem.at[step], recv_sem.at[step], target).wait()

    everyone(send)
    everyone(wait)


def gather_small(vectors, count):
    return pl.pallas_call(
        gather_kernel,
        out_shape=jax.ShapeDtypeStruct((count, 16, 256), bf16),
        in_specs=[pl.BlockSpec(memory_space=pltpu.VMEM)] * len(vectors),
        out_specs=pl.BlockSpec(memory_space=pltpu.VMEM),
        scratch_shapes=[
            pltpu.VMEM((16, 256), bf16),
            pltpu.SemaphoreType.DMA((count,)),
            pltpu.SemaphoreType.DMA((count,)),
        ],
        compiler_params=pltpu.CompilerParams(
            collective_id=1, has_side_effects=True, vmem_limit_bytes=16 * MIB
        ),
        name="gather_small",
    )(*vectors)


def sum_kernel(x_ref, out_ref, come_ref, send_sem, recv_sem):
    side_count = lax.axis_size("mp")
    me = lax.axis_index("rows") * side_count + lax.axis_index("mp")
    meet_everyone()

    def send(step, target, source):
        remote(x_ref.at[target], come_ref.at[step], send_sem.at[step], recv_sem.at[step], target).start()

    def wait(step, target, source):
        remote(x_ref.at[target], come_ref.at[step], send_sem.at[step], recv_sem.at[step], target).wait()

    everyone(send)
    come_ref[0] = x_ref[me]
    everyone(wait)
    out_ref[...] = jnp.sum(come_ref[...].astype(f32), axis=0)


def sum_small(blocks):
    count = blocks.shape[0]
    return pl.pallas_call(
        sum_kernel,
        out_shape=jax.ShapeDtypeStruct(blocks.shape[1:], f32),
        in_specs=[pl.BlockSpec(memory_space=pltpu.VMEM)],
        out_specs=pl.BlockSpec(memory_space=pltpu.VMEM),
        scratch_shapes=[
            pltpu.VMEM(blocks.shape, blocks.dtype),
            pltpu.SemaphoreType.DMA((count,)),
            pltpu.SemaphoreType.DMA((count,)),
        ],
        compiler_params=pltpu.CompilerParams(
            collective_id=2, has_side_effects=True, vmem_limit_bytes=16 * MIB
        ),
        name="sum_small",
    )(blocks)


def lay_tables(share, count):
    lane = np.arange(share * count)
    place = lane[None, :] % share == np.arange(share)[:, None]
    mark = lane[None, :] // share == np.arange(count)[:, None]
    return jnp.asarray(place, bf16), jnp.asarray(mark, f32)


def joined(shares):
    count, vectors, share = shares.shape
    place, mark = lay_tables(share, count)
    wide = dot(shares.reshape(count * vectors, share), place).reshape(count, vectors, count * share)
    return jnp.sum(wide * mark[:, None, :], axis=0)


def cut(vectors, share):
    number, size = vectors.shape
    place, mark = lay_tables(share, size // share)
    wide = (vectors[None] * mark[:, None, :]).astype(bf16)
    out = lax.dot_general(wide, place, (((2,), (1,)), ((), ())), preferred_element_type=f32)
    return out.astype(bf16)


def on_device(
    atoms,
    time_embedding,
    coordinates,
    item_lengths,
    item_group,
    query_weight,
    key_weight,
    value_weight,
    out_weight,
    up_weight,
    down_weight,
    value_bias,
    out_bias,
    up_bias,
    down_bias,
    first_gain,
    first_shift,
    second_gain,
    second_shift,
    kernel_params,
    cotangent,
):
    rows_here = atoms.shape[0]
    pair_size = lax.axis_size("mp")
    side = lax.axis_index("mp")
    pair_index = lax.axis_index("rows")
    group_rows = rows_here * pair_size
    counter = jnp.arange(rows_here, dtype=jnp.int32)
    near_rows = (pair_index * pair_size + side) * rows_here + counter
    far_rows = (pair_index * pair_size + 1 - side) * rows_here + counter
    items = item_lengths.shape[0]
    near_item, near_valid = row_items(near_rows, group_rows, item_lengths, item_group)
    far_item, far_valid = row_items(far_rows, group_rows, item_lengths, item_group)
    near_code = jnp.where(near_valid, near_item, items + near_rows)
    far_code = jnp.where(far_valid, far_item, items + far_rows)
    all_code = jnp.concatenate([near_code, far_code])
    item = jnp.where(near_valid, near_item, -1)[:, None]
    valid = near_valid.astype(f32)[:, None]

    count = lax.axis_size("rows") * pair_size
    share, hidden = up_weight.shape
    width = query_weight.shape[1]
    blocks = hidden // width
    small = (value_bias, out_bias, down_bias, first_gain, first_shift, second_gain, second_shift)
    table_share = kernel_params.shape[0]
    gathered = gather_small((jnp.stack(small), up_bias[None], kernel_params[None]), count)
    value_b, out_b, down_b, gain_one, shift_one, gain_two, shift_two = joined(gathered[:, :7, :share])
    up_b = joined(gathered[:, 7:8, : blocks * share])[0]
    table = joined(gathered[:, 8:9, :table_share])[0]
    wide = lax.all_gather(
        jnp.concatenate([query_weight, key_weight, value_weight, out_weight, up_weight], axis=1),
        AXES,
        axis=0,
        tiled=True,
    )
    down_w = lax.all_gather(down_weight, AXES, axis=0, tiled=True)

    means, widths, mix = table[:KERN], table[KERN : 2 * KERN], table[2 * KERN :].reshape(KERN, HEADS)
    norm = 1.0 / (widths * math.sqrt(2.0 * math.pi))
    curve = (-0.5 * math.log2(math.e)) / (widths * widths)
    mix_low = (mix * norm[:, None] * math.log2(math.e)).astype(bf16)
    coord_low = coordinates.astype(bf16)
    coord_all = jnp.concatenate([coord_low, swap_sides(coord_low)], axis=1).astype(f32)
    near = coordinates.astype(f32).T
    bias, phi = pair_bias(near, coord_all, near_code[:, None], all_code[None], means, curve, mix_low)

    bias, wide = lax.optimization_barrier((bias, wide))
    h_zero, q4, near_kv = project(atoms, item, time_embedding, gain_one, shift_one, value_b, wide)
    far_kv = swap_sides(near_kv)
    expo, mixed4, inverse4 = attend(q4, near_kv, far_kv, bias)
    layer_out, grad_one, scaled4, down_grad, up_grad, out_grad, sums_two, up_sums = feed_forward(
        h_zero, mixed4, inverse4, valid, cotangent, wide, down_w, (out_b, up_b, down_b, gain_two, shift_two)
    )

    down_shards = Shards(down_grad[None], (0, 1), False)
    up_shards = Shards(up_grad[None], (1, 0), False)
    feed_shards = (down_shards, up_shards)
    half = NG // 2
    done = []
    for n in range(2):

        def run(scaled4):
            return attend_back(q4, scaled4, mixed4, near_kv, far_kv, expo, n * half, half), scaled4

        out, scaled4 = beside(feed_shards, run, (scaled4,))
        done.append(out)
    scores_grad = [d[0] for d in done]
    turned = [(d[2], swap_sides(d[3]), d[4], swap_sides(d[5])) for d in done]
    pairs = [done[0][1], done[1][1]]
    for m in (0, 2, 1, 3):
        pairs += [turned[0][m], turned[1][m]]
    atoms_grad, square_grads, sums_one = beside(
        feed_shards,
        lambda h_zero, *pairs: project_back(h_zero, grad_one, pairs, gain_one, shift_one, wide, out_grad),
        (h_zero, *pairs),
    )
    square_shards = Shards(square_grads, (0, 1), True)

    tiles = rows_here // 32
    moments = 0.0
    first = 0
    for eighths in PIECES:
        size = eighths * tiles // 8
        def run(near):
            send = square_shards.send[0]
            corner = send[(0,) * (send.ndim - 2)][:16, :128]
            return bias_back(near, coord_all, means, curve, scores_grad, phi, first, size, [corner]), near

        piece, near = beside((square_shards, *feed_shards), run, (near,))
        moments = moments + piece
        first += size
    zeroth = moments[:HEADS].T * norm[:, None]
    first = (moments[HEADS : 2 * HEADS] + moments[2 * HEADS : 3 * HEADS]).T * norm[:, None]
    twice = (moments[3 * HEADS : 4 * HEADS] + moments[4 * HEADS :]).T * norm[:, None]
    m_zero, m_one, m_two = [jnp.sum(mix * r, axis=1) for r in (zeroth, first, twice)]
    offset = means - CENTRE
    mean_grad = (m_one - offset * m_zero) / widths**2
    width_grad = (m_two - 2.0 * offset * m_one + offset * offset * m_zero) / widths**3 - m_zero / widths
    table_grad = jnp.concatenate([mean_grad, width_grad, zeroth.reshape(-1)])

    cuts = jnp.concatenate(
        [
            jnp.pad(
                cut(
                    jnp.stack(
                        [sums_one[2], sums_two[2], sums_two[3], sums_one[0], sums_one[1], sums_two[0], sums_two[1]]
                    ),
                    share,
                ),
                ((0, 0), (0, 0), (0, 256 - share)),
            ),
            jnp.pad(cut(up_sums[0:1], blocks * share), ((0, 0), (0, 0), (0, 256 - blocks * share))),
            jnp.pad(cut(table_grad[None], table_share), ((0, 0), (0, 7), (0, 256 - table_share))),
        ],
        axis=1,
    )
    sums = sum_small(cuts)
    square_sum = square_shards.total()
    return (
        layer_out,
        atoms_grad,
        square_sum[0],
        square_sum[1],
        square_sum[2],
        square_sum[3],
        up_shards.total()[0],
        down_shards.total()[0],
        sums[0, :share],
        sums[1, :share],
        sums[7, : blocks * share],
        sums[2, :share],
        sums[3, :share],
        sums[4, :share],
        sums[5, :share],
        sums[6, :share],
        sums[8, :table_share],
    )


def solution(mesh):
    row = P(AXES, None)
    vec = P(AXES)
    in_specs = (row, P(), P(None, AXES), P(), P(), *[row] * 6, *[vec] * 9, row)
    out_specs = (*[row] * 8, *[vec] * 9)
    return jax.shard_map(on_device, mesh=mesh, in_specs=in_specs, out_specs=out_specs, check_vma=False)
```

```python
import functools
import math

import jax
import jax.numpy as jnp
import numpy as np
from jax import lax
from jax.experimental import pallas as pl
from jax.experimental.pallas import tpu as pltpu
from jax.sharding import PartitionSpec as P

HEADS = 32
KERN = 128
HEAD = 24
GH = 8
NG = HEADS // GH
GW = GH * HEAD
MIB = 2**20
CENTRE = 6.0
STORED = 1
AXES = ("rows", "mp")
f32 = jnp.float32
bf16 = jnp.bfloat16


def dot(left, right):
    return jnp.dot(left, right, preferred_element_type=f32)


def turned_dot(left, right):
    return lax.dot_general(left, right, (((1,), (1,)), ((), ())), preferred_element_type=f32)


def sum_dot(left, right):
    return lax.dot_general(left, right, (((0,), (0,)), ((), ())), preferred_element_type=f32)


def whole(shape):
    return pl.BlockSpec(shape, lambda i: (0,) * len(shape))


def after(kernel, inputs, tokens):
    def run(*refs):
        kernel(*refs[:inputs], *refs[inputs + len(tokens) :])

    return run, [pl.BlockSpec(memory_space=pl.ANY)] * len(tokens)


def high_low(value):
    high = value.astype(bf16)
    return high, (value - high.astype(f32)).astype(bf16)


def distances(near_ref, all_ref):
    total = None
    for c in range(3):
        diff = near_ref[:, c : c + 1] - all_ref[c : c + 1, :]
        total = diff * diff if total is None else total + diff * diff
    return jnp.sqrt(total) * 0.25


def bias_kernel(
    pairs_step, near_ref, all_ref, code_near_ref, code_all_ref, means_ref, curve_ref, mix_ref,
    bias_ref, phi_ref, dist_ref, mask_ref,
):
    dist_ref[...] = distances(near_ref, all_ref)
    mask_ref[...] = jnp.where(code_near_ref[:, 0:1] == code_all_ref[0:1, :], 0.0, -1e30)
    rows, span = dist_ref.shape

    def body(step, carry):
        for q in range(pairs_step):
            pair = step * pairs_step + q
            drow = [dist_ref[pl.ds(pair * 2 + e, 1), :] for e in range(2)]
            mrow = [mask_ref[pl.ds(pair * 2 + e, 1), :] for e in range(2)]
            for lane in range(0, span, 256):
                tall = []
                for e in range(2):
                    wide = []
                    for low in (lane, lane + 128):
                        u = drow[e][:, low : low + 128] - means_ref[...]
                        wide.append(jnp.exp2((u * curve_ref[...]) * u).astype(bf16))
                    wide = jnp.concatenate(wide, axis=1)
                    if e < STORED:
                        phi_ref[pair * STORED + e, :, lane : lane + 256] = wide
                    tall.append(wide)
                out = dot(mix_ref[...], jnp.concatenate(tall, axis=0)).reshape(NG, 2, GH, 256)
                out = jnp.concatenate(
                    [out[:, e : e + 1] + mrow[e][:, lane : lane + 256].reshape(1, 1, 1, 256) for e in range(2)],
                    axis=1,
                )
                bias_ref[:, pl.ds(pl.multiple_of(pair * 16, 16), 16), lane : lane + 256] = out.reshape(
                    NG, 16, 256
                ).astype(bf16)
        return carry

    lax.fori_loop(0, rows // 2 // pairs_step, body, 0)


def lane_wide(values):
    return jnp.broadcast_to(values[:, None], (KERN, 128))


def pair_bias(near, coord_all, code_near, code_all, means, curve, mix_low, tile=32, pairs_step=16):
    rows, span = near.shape[0], coord_all.shape[1]
    m4 = mix_low.T.reshape(NG, GH, KERN)
    zero = jnp.zeros_like(m4)
    left = jnp.stack([jnp.concatenate([m4, zero], -1), jnp.concatenate([zero, m4], -1)], axis=1)
    left = left.reshape(2 * HEADS, 2 * KERN)
    return pl.pallas_call(
        functools.partial(bias_kernel, pairs_step),
        grid=(rows // tile,),
        in_specs=[
            pl.BlockSpec((tile, 3), lambda i: (i, 0)),
            whole((3, span)),
            pl.BlockSpec((tile, 1), lambda i: (i, 0)),
            whole((1, span)),
            whole((KERN, 128)),
            whole((KERN, 128)),
            whole((2 * HEADS, 2 * KERN)),
        ],
        out_specs=[
            pl.BlockSpec((NG, tile * GH, span), lambda i: (0, i, 0)),
            pl.BlockSpec((tile * STORED // 2, KERN, span), lambda i: (i, 0, 0)),
        ],
        out_shape=[
            jax.ShapeDtypeStruct((NG, rows * GH, span), bf16),
            jax.ShapeDtypeStruct((rows * STORED // 2, KERN, span), bf16),
        ],
        scratch_shapes=[pltpu.VMEM((tile, span), f32), pltpu.VMEM((tile, span), f32)],
        compiler_params=pltpu.CompilerParams(vmem_limit_bytes=50 * MIB),
        cost_estimate=pl.CostEstimate(flops=1000, bytes_accessed=1000, transcendentals=0),
        name="bias",
    )(near, coord_all, code_near, code_all, lane_wide(means), lane_wide(curve), left)


def repeat_tables(tile):
    row = np.arange(tile * GH)
    repeat = row[:, None] // GH == np.arange(tile)[None, :]
    own = row[:, None] % GH == np.arange(GW)[None, :] // HEAD
    return repeat, own


def project_kernel(
    atoms_ref, code_ref, time_ref, gain_ref, shift_ref, bias_ref, wide_ref,
    h_ref, q_ref, kv_ref,
):
    width = atoms_ref.shape[1]
    items = lax.broadcasted_iota(jnp.int32, (1, time_ref.shape[0]), 1)
    picks = (code_ref[...] == items).astype(f32).astype(bf16)
    h_zero = atoms_ref[...].astype(f32) + dot(picks, time_ref[...])
    h_ref[...] = h_zero
    centre = h_zero - jnp.mean(h_zero, axis=1, keepdims=True)
    rate = lax.rsqrt(jnp.mean(centre * centre, axis=1, keepdims=True) + 1e-05)
    normed = (centre * rate * gain_ref[...] + shift_ref[...]).astype(bf16)
    tile = h_zero.shape[0]
    lane = lax.broadcasted_iota(jnp.int32, (tile, 256 - GW), 1)
    ones = jnp.where(lane == 0, 1.0, 0.0)
    for n in (1, 2, 0):
        out = dot(normed, wide_ref[:, n * width : (n + 1) * width])
        if n == 2:
            out = out + bias_ref[...]
        for g in range(NG):
            part = out[:, g * GW : (g + 1) * GW]
            if n == 0:
                q_ref[g] = part.astype(bf16)
            else:
                part = jnp.concatenate([part, ones if n == 2 else jnp.zeros_like(ones)], axis=1)
                kv_ref[n - 1, g] = part.astype(bf16)


def project(atoms, code, time_embedding, gain, shift, value_bias, wide, tile=256):
    rows, width = atoms.shape
    return pl.pallas_call(
        project_kernel,
        grid=(rows // tile,),
        in_specs=[
            pl.BlockSpec((tile, width), lambda i: (i, 0)),
            pl.BlockSpec((tile, 1), lambda i: (i, 0)),
            whole(time_embedding.shape),
            *[whole((1, width))] * 3,
            whole((width, 3 * width)),
        ],
        out_specs=[
            pl.BlockSpec((tile, width), lambda i: (i, 0)),
            pl.BlockSpec((NG, tile, GW), lambda i: (0, i, 0)),
            pl.BlockSpec((2, NG, tile, 256), lambda i: (0, 0, i, 0)),
        ],
        out_shape=[
            jax.ShapeDtypeStruct((rows, width), f32),
            jax.ShapeDtypeStruct((NG, rows, GW), bf16),
            jax.ShapeDtypeStruct((2, NG, rows, 256), bf16),
        ],
        compiler_params=pltpu.CompilerParams(vmem_limit_bytes=40 * MIB),
        cost_estimate=pl.CostEstimate(flops=1000, bytes_accessed=1000, transcendentals=0),
        name="project",
    )(atoms, code, time_embedding, gain[None], shift[None], value_bias[None], wide)


def project_back_kernel(
    h_ref, grad_one_ref, q0_ref, q1_ref, k0_ref, k1_ref, v0_ref, v1_ref, kc0_ref, kc1_ref, vc0_ref, vc1_ref,
    gain_ref, shift_ref, wide_ref, out_grad_ref,
    atoms_grad_ref, grads_ref, sums_ref, normed_s, grad_s,
):
    rows, width = h_ref.shape
    for g in range(NG):
        q_ref, k_ref, v_ref, kc_ref, vc_ref = (
            (q0_ref, k0_ref, v0_ref, kc0_ref, vc0_ref) if g < NG // 2 else (q1_ref, k1_ref, v1_ref, kc1_ref, vc1_ref)
        )
        m = g % (NG // 2)
        cols = slice(g * GW, (g + 1) * GW)
        grad_s[0, :, cols] = q_ref[m]
        grad_s[1, :, cols] = (k_ref[m] + kc_ref[m].astype(f32)).T.astype(bf16)
        grad_s[2, :, cols] = (v_ref[m] + vc_ref[m].astype(f32)).T.astype(bf16)
    h_zero = h_ref[...]
    centre = h_zero - jnp.mean(h_zero, axis=1, keepdims=True)
    rate = lax.rsqrt(jnp.mean(centre * centre, axis=1, keepdims=True) + 1e-05)
    hat = centre * rate
    normed_s[...] = (hat * gain_ref[...] + shift_ref[...]).astype(bf16)
    grads_ref[3] = out_grad_ref[...]
    grad = None
    for n in range(3):
        grads_ref[n] = sum_dot(normed_s[...], grad_s[n]).astype(bf16)
        part = turned_dot(grad_s[n], wide_ref[:, n * width : (n + 1) * width])
        grad = part if grad is None else grad + part
    g = grad * gain_ref[...]
    atoms_grad_ref[...] = grad_one_ref[...] + rate * (
        g - jnp.mean(g, axis=1, keepdims=True) - hat * jnp.mean(g * hat, axis=1, keepdims=True)
    )
    sums_ref[...] = jnp.zeros_like(sums_ref)
    sums_ref[0:1, :] = jnp.sum(grad * hat, axis=0, keepdims=True)
    sums_ref[1:2, :] = jnp.sum(grad, axis=0, keepdims=True)
    sums_ref[2:3, :] = dot(jnp.ones((8, rows), bf16), grad_s[2])[0:1]


def project_back(h_zero, grad_one, pairs, gain, shift, wide, out_grad, tokens=()):
    rows, width = h_zero.shape
    once = pl.Buffered(1)
    kernel, token_specs = after(project_back_kernel, 16, tokens)
    return pl.pallas_call(
        kernel,
        grid=(1,),
        in_specs=[
            whole((rows, width)),
            whole((rows, width)),
            *[whole(p.shape) for p in pairs],
            *[whole((1, width))] * 2,
            pl.BlockSpec((width, 3 * width), lambda i: (0, 0), pipeline_mode=once),
            whole((width, width)),
            *token_specs,
        ],
        out_specs=[whole((rows, width)), whole((NG, width, width)), whole((8, width))],
        out_shape=[
            jax.ShapeDtypeStruct((rows, width), f32),
            jax.ShapeDtypeStruct((4, width, width), bf16),
            jax.ShapeDtypeStruct((8, width), f32),
        ],
        scratch_shapes=[pltpu.VMEM((rows, width), bf16), pltpu.VMEM((3, rows, width), bf16)],
        compiler_params=pltpu.CompilerParams(vmem_limit_bytes=56 * MIB),
        cost_estimate=pl.CostEstimate(flops=1000, bytes_accessed=1000, transcendentals=0),
        name="project_back",
    )(h_zero, grad_one, *pairs, gain[None], shift[None], wide, out_grad, *tokens)


def attend_kernel(
    tiles, q_ref, near_ref, far_ref, b_ref, rep_ref, rept_ref, own_ref, scaled_ref,
    e_ref, mixed_ref, inv_ref, qa, qb, sa, sb, ea, oa, ob, wa, wb,
):
    keys, values = (near_ref.at[0], far_ref.at[0]), (near_ref.at[1], far_ref.at[1])
    query, scores, outs, wides = (qa, qb), (sa, sb), (oa, ob), (wa, wb)
    rows, span = sa.shape
    held = rows // GH
    units = NG * tiles
    parts, chunk, ahead = 4, 8, 3
    step, some = span // parts, rows // parts
    pid = pl.program_id(0)

    def place(unit):
        unit = jnp.clip(unit, 0, units - 1)
        group = unit // tiles
        return group, pl.ds(pl.multiple_of((unit - group * tiles) * held, held), held)

    def spread(unit, par):
        g, i = place(unit)
        query[par][...] = (dot(rep_ref[...], q_ref[g, i, :]) * scaled_ref[...]).astype(bf16)

    def score(unit, par, part):
        g, _ = place(unit)
        cols = slice(part * step, (part + 1) * step)
        there = slice(part % 2 * step, (part % 2 + 1) * step)
        scores[par][:, cols] = turned_dot(query[par][...], keys[part // 2][g, there, :GW])

    def soften(par, part):
        chunks = range(part * some, (part + 1) * some, chunk)
        held_x = {}
        for n in range(len(chunks) + ahead):
            if n < len(chunks):
                here = slice(chunks[n], chunks[n] + chunk)
                x = scores[par][here, :] + b_ref[par, here, :].astype(f32)
                held_x[n] = x, jnp.max(x, axis=1, keepdims=True)
            if n >= ahead:
                here = slice(chunks[n - ahead], chunks[n - ahead] + chunk)
                x, top = held_x.pop(n - ahead)
                e = jnp.exp2(x - top).astype(bf16)
                e_ref[par, here, :] = e
                if par == 1:
                    ea[here, :] = e

    def mix(unit, par, part):
        g, _ = place(unit)
        here = slice(part * some, (part + 1) * some)
        source = e_ref.at[0] if par == 0 else ea
        half = span // 2
        outs[par][here, :] = dot(source[here, :half], values[0][g]) + dot(source[here, half:], values[1][g])

    def scale(par, part):
        here = slice(part * some, (part + 1) * some)
        out = outs[par][here, :]
        inv = 1.0 / out[:, GW : GW + 1]
        own = own_ref[here, :]
        wides[par][here, :] = jnp.concatenate(
            [*high_low(out[:, :GW] * inv * own), *high_low(inv * own)], axis=1
        )

    def gather(unit, par):
        g, i = place(unit)
        out = dot(rept_ref[...], wides[par][...])
        mixed_ref[g, i, :] = out[:, :GW] + out[:, GW : 2 * GW]
        inv_ref[g, i, :] = out[:, 2 * GW : 3 * GW] + out[:, 3 * GW :]

    @pl.when(pid == 0)
    def _():
        spread(0, 0)
        for part in range(parts):
            score(0, 0, part)
        spread(1, 1)
        ea[...] = jnp.ones_like(ea)
        for ref in (oa, ob):
            ref[...] = jnp.ones_like(ref)
        for ref in (wa, wb):
            ref[...] = jnp.zeros_like(ref)

    for par in range(2):
        unit = pid * 2 + par
        for part in range(parts):
            score(unit + 1, 1 - par, part)
            scale(par, part)
            mix(unit - 1, 1 - par, part)
            if part == 1:
                spread(unit + 2, par)
            if part == 2:
                gather(unit - 3, 1 - par)
            soften(par, part)

    @pl.when(pid == units // 2 - 1)
    def _():
        for part in range(parts):
            scale(0, part)
            mix(units - 1, 1, part)
        gather(units - 3, 1)
        gather(units - 2, 0)
        for part in range(parts):
            scale(1, part)
        gather(units - 1, 1)


def attend(q4, near, far, bias, tile=64):
    rows = q4.shape[1]
    span = 2 * rows
    tiles = rows // tile
    repeat, own = repeat_tables(tile)
    deep = tile * GH
    bias = bias.reshape(NG * tiles, deep, span)
    big = pl.BlockSpec((2, deep, span), lambda i: (i, 0, 0))
    scale = HEAD**-0.5 * math.log2(math.e)
    e, mixed, inv = pl.pallas_call(
        functools.partial(attend_kernel, tiles),
        grid=(NG * tiles // 2,),
        in_specs=[
            whole((NG, rows, GW)),
            *[whole((2, NG, rows, 256))] * 2,
            big,
            whole((deep, tile)),
            whole((tile, deep)),
            whole((deep, GW)),
            whole((deep, GW)),
        ],
        out_specs=[big, whole((NG, rows, GW)), whole((NG, rows, GW))],
        out_shape=[
            jax.ShapeDtypeStruct((NG * tiles, deep, span), bf16),
            jax.ShapeDtypeStruct((NG, rows, GW), f32),
            jax.ShapeDtypeStruct((NG, rows, GW), f32),
        ],
        scratch_shapes=[pltpu.VMEM((deep, GW), bf16)] * 2
        + [pltpu.VMEM((deep, span), f32)] * 2
        + [pltpu.VMEM((deep, span), bf16)]
        + [pltpu.VMEM((deep, 256), f32)] * 2
        + [pltpu.VMEM((deep, 4 * GW), bf16)] * 2,
        compiler_params=pltpu.CompilerParams(vmem_limit_bytes=50 * MIB),
        cost_estimate=pl.CostEstimate(flops=1000, bytes_accessed=1000, transcendentals=0),
        name="attend",
    )(
        q4, near, far, bias, jnp.asarray(repeat, bf16), jnp.asarray(repeat.T, bf16),
        jnp.asarray(own, f32), jnp.asarray(own * scale, f32),
    )
    return e.reshape(NG, rows * GH, span), mixed, inv


def attend_back_kernel(
    tiles, q_ref, gs_ref, mx_ref, near_ref, far_ref, e_ref, rep_ref, rept_ref, own_ref, ownt_ref,
    ds_ref, dq_ref, dk_near_ref, dk_far_ref, dv_near_ref, dv_far_ref,
    ga, gb, da, db, qta, qtb, gta, gtb, sa, sb, kept, oa, ob, wa, wb, dk, dv,
):
    keys, values = (near_ref.at[0], far_ref.at[0]), (near_ref.at[1], far_ref.at[1])
    grads, deltas, queries_t, grads_t = (ga, gb), (da, db), (qta, qtb), (gta, gtb)
    scores, outs, wides = (sa, sb), (oa, ob), (wa, wb)
    deep, span = sa.shape
    held = deep // GH
    units = q_ref.shape[0] * tiles
    parts, chunk = 4, 8
    step, some = span // parts, deep // parts
    scale = HEAD**-0.5
    pid = pl.program_id(0)

    def place(unit):
        unit = jnp.clip(unit, 0, units - 1)
        group = unit // tiles
        return group, pl.ds(pl.multiple_of((unit - group * tiles) * held, held), held)

    def begin_scores(unit, par):
        g, i = place(unit)
        grads[par][...] = (dot(rep_ref[...], gs_ref[g, i, :]) * own_ref[...]).astype(bf16)

    def begin_rest(unit, par):
        g, i = place(unit)
        gs = gs_ref[g, i, :]
        wide = dot(rep_ref[...], jnp.concatenate(high_low(gs.astype(f32) * mx_ref[g, i, :]), axis=1))
        deltas[par][...] = jnp.sum((wide[:, :GW] + wide[:, GW:]) * own_ref[...], axis=1, keepdims=True)
        grads_t[par][...] = (sum_dot(gs, rept_ref[...]) * ownt_ref[...]).astype(bf16)

    def turn_query(unit, par):
        g, i = place(unit)
        queries_t[par][...] = (sum_dot(q_ref[g, i, :], rept_ref[...]) * ownt_ref[...]).astype(bf16)

    def grad_probs(unit, par, part):
        g, _ = place(unit)
        cols = slice(part * step, (part + 1) * step)
        there = slice(part % 2 * step, (part % 2 + 1) * step)
        scores[par][:, cols] = turned_dot(grads[par][...], values[part // 2][g, there, :GW])

    def soften(par, part):
        for c in range(part * some, (part + 1) * some, chunk):
            here = slice(c, c + chunk)
            ds = (e_ref[par, here, :].astype(f32) * (scores[par][here, :] - deltas[par][here, :])).astype(bf16)
            ds_ref[par, here, :] = ds
            if par == 1:
                kept[here, :] = ds

    def value_grad(unit, par, part):
        g, _ = place(unit)
        cols = slice(part * step, (part + 1) * step)
        dv[g, :, cols] += dot(grads_t[par][...], e_ref[par, :, cols])

    def key_grad(unit, par, part):
        g, _ = place(unit)
        cols = slice(part * step, (part + 1) * step)
        source = ds_ref.at[0] if par == 0 else kept
        dk[g, :, cols] += dot(queries_t[par][...], source[:, cols])

    def query_grad(unit, par, part):
        g, _ = place(unit)
        here = slice(part * some, (part + 1) * some)
        source = ds_ref.at[0] if par == 0 else kept
        half = span // 2
        outs[par][here, :] = dot(source[here, :half], keys[0][g, :, :GW]) + dot(
            source[here, half:], keys[1][g, :, :GW]
        )

    def mask(par):
        wides[par][...] = (outs[par][...] * own_ref[...]).astype(bf16)

    def gather(unit, par):
        g, i = place(unit)
        dq_ref[g, i, :] = (dot(rept_ref[...], wides[par][...]) * scale).astype(bf16)

    @pl.when(pid == 0)
    def _():
        dk[...] = jnp.zeros_like(dk)
        dv[...] = jnp.zeros_like(dv)
        begin_scores(0, 0)
        for part in range(parts):
            grad_probs(0, 0, part)
        begin_scores(1, 1)
        begin_rest(0, 0)
        queries_t[1][...] = jnp.zeros_like(queries_t[1])
        kept[...] = jnp.zeros_like(kept)
        for ref in (oa, ob, wa, wb):
            ref[...] = jnp.zeros_like(ref)

    for par in range(2):
        unit = pid * 2 + par
        for part in range(parts):
            grad_probs(unit + 1, 1 - par, part)
            value_grad(unit, par, part)
            if part == 0:
                begin_scores(unit + 2, par)
                gather(unit - 3, 1 - par)
            if part == 1:
                begin_rest(unit + 1, 1 - par)
            if part == 2:
                turn_query(unit, par)
            if part == 3:
                mask(par)
            key_grad(unit - 1, 1 - par, part)
            query_grad(unit - 1, 1 - par, part)
            soften(par, part)

    @pl.when(pid == units // 2 - 1)
    def _():
        last = units - 1
        gather(last - 2, 1)
        mask(0)
        for part in range(parts):
            key_grad(last, 1, part)
            query_grad(last, 1, part)
        gather(last - 1, 0)
        mask(1)
        gather(last, 1)
        half = span // 2
        dk_near_ref[...] = dk[:, :, :half] * scale
        dk_far_ref[...] = (dk[:, :, half:] * scale).astype(bf16)
        dv_near_ref[...] = dv[:, :, :half]
        dv_far_ref[...] = dv[:, :, half:].astype(bf16)


def attend_back(q4, gs4, mx4, near_kv, far_kv, e, first, groups, tokens=(), tile=64):
    rows = q4.shape[1]
    span = 2 * rows
    tiles = rows // tile
    deep = tile * GH
    repeat, own = repeat_tables(tile)
    e = e.reshape(NG * tiles, deep, span)
    block = first // groups
    ahead = first * tiles // 2
    held = lambda wide: pl.BlockSpec((groups, rows, wide), lambda i: (block, 0, 0))
    near = jax.ShapeDtypeStruct((groups, GW, rows), f32)
    far = jax.ShapeDtypeStruct((groups, GW, rows), bf16)
    kernel, token_specs = after(functools.partial(attend_back_kernel, tiles), 10, tokens)
    ds, *rest = pl.pallas_call(
        kernel,
        grid=(groups * tiles // 2,),
        in_specs=[
            *[held(GW)] * 3,
            *[pl.BlockSpec((2, groups, rows, 256), lambda i: (0, block, 0, 0))] * 2,
            pl.BlockSpec((2, deep, span), lambda i: (i + ahead, 0, 0)),
            whole((deep, tile)),
            whole((tile, deep)),
            whole((deep, GW)),
            whole((GW, deep)),
            *token_specs,
        ],
        out_specs=[
            pl.BlockSpec((2, deep, span), lambda i: (i, 0, 0)),
            whole((groups, rows, GW)),
            *[whole((groups, GW, rows))] * 4,
        ],
        out_shape=[
            jax.ShapeDtypeStruct((groups * tiles, deep, span), bf16),
            jax.ShapeDtypeStruct((groups, rows, GW), bf16),
            near,
            far,
            near,
            far,
        ],
        scratch_shapes=[pltpu.VMEM((deep, GW), bf16)] * 2
        + [pltpu.VMEM((deep, 1), f32)] * 2
        + [pltpu.VMEM((GW, deep), bf16)] * 4
        + [pltpu.VMEM((deep, span), f32)] * 2
        + [pltpu.VMEM((deep, span), bf16)]
        + [pltpu.VMEM((deep, GW), f32)] * 2
        + [pltpu.VMEM((deep, GW), bf16)] * 2
        + [pltpu.VMEM((groups, GW, span), f32)] * 2,
        compiler_params=pltpu.CompilerParams(vmem_limit_bytes=50 * MIB),
        cost_estimate=pl.CostEstimate(flops=1000, bytes_accessed=1000, transcendentals=0),
        name="attend_back",
    )(
        q4, gs4, mx4, near_kv, far_kv, e, jnp.asarray(repeat, bf16), jnp.asarray(repeat.T, bf16),
        jnp.asarray(own, f32), jnp.asarray(own.T, f32), *tokens,
    )
    return (ds.reshape(groups, rows * GH, span), *rest)


def feed_kernel(
    row_steps, h_ref, mixed_ref, inv_ref, valid_ref, cot_ref, out_w_ref, up_w_ref, down_w_ref,
    out_b_ref, up_b_ref, down_b_ref, gain_ref, shift_ref,
    layer_ref, grad_one_ref, gs_ref, down_grad_ref, up_grad_ref, out_grad_ref, sums_ref, up_sums_ref,
    act_s, gup_s, second_s, gatt_s, gffn_s, mixed_s, up_s, gact_s,
):
    step = pl.program_id(0)
    tile, width = h_ref.shape
    hidden = up_w_ref.shape[1]
    some = 32

    @pl.when(step == 0)
    def _():
        sums_ref[...] = jnp.zeros_like(sums_ref)

    @pl.when(step < row_steps)
    def _():
        here = pl.ds(pl.multiple_of(step * tile, tile), tile)
        h_one = h_ref[...] + out_b_ref[...]
        for g in range(NG):
            mixed = mixed_ref[g].astype(bf16)
            mixed_s[g, here, :] = mixed
            h_one = h_one + dot(mixed, out_w_ref[g * GW : (g + 1) * GW, :])
        centre = h_one - jnp.mean(h_one, axis=1, keepdims=True)
        rate = lax.rsqrt(jnp.mean(centre * centre, axis=1, keepdims=True) + 1e-05)
        second = (centre * rate * gain_ref[...] + shift_ref[...]).astype(bf16)
        second_s[here, :] = second
        grad_two = cot_ref[...].astype(f32) * valid_ref[...]
        grad_ffn = grad_two.astype(bf16)
        gffn_s[here, :] = grad_ffn
        h_two = h_one + down_b_ref[...]
        grad_second = None
        for low in range(0, hidden, width):
            cols = slice(low, low + width)
            up_s[...] = dot(second, up_w_ref[:, cols]) + up_b_ref[:, cols]
            gact_s[...] = turned_dot(grad_ffn, down_w_ref[cols, :])

            def bend(n, carry):
                rows = pl.ds(pl.multiple_of(n * some, some), some)
                at = pl.ds(pl.multiple_of(step * tile + n * some, some), some)
                up = up_s[rows, :]
                below = 0.5 + 0.5 * lax.erf(up * (2.0**-0.5))
                slope = below + up * (jnp.exp(-0.5 * up * up) * (2.0 * math.pi) ** -0.5)
                act_s[at, cols] = (up * below).astype(bf16)
                gup_s[at, cols] = (gact_s[rows, :] * slope).astype(bf16)
                return carry

            lax.fori_loop(0, tile // some, bend, 0)
            h_two = h_two + dot(act_s[here, cols], down_w_ref[cols, :])
            part = turned_dot(gup_s[here, cols], up_w_ref[:, cols])
            grad_second = part if grad_second is None else grad_second + part
        layer_ref[...] = (h_two * valid_ref[...]).astype(bf16)
        hat = centre * rate
        sums_ref[0:1, :] += jnp.sum(grad_second * hat, axis=0, keepdims=True)
        sums_ref[1:2, :] += jnp.sum(grad_second, axis=0, keepdims=True)
        g = grad_second * gain_ref[...]
        grad_one = grad_two + rate * (
            g - jnp.mean(g, axis=1, keepdims=True) - hat * jnp.mean(g * hat, axis=1, keepdims=True)
        )
        grad_one_ref[...] = grad_one
        grad_att = grad_one.astype(bf16)
        gatt_s[here, :] = grad_att
        for g in range(NG):
            grad_mixed = turned_dot(grad_att, out_w_ref[g * GW : (g + 1) * GW, :]).astype(bf16)
            gs_ref[g] = (grad_mixed.astype(f32) * inv_ref[g]).astype(bf16)

    for n in range(WEIGHT_STEPS):

        @pl.when(step == row_steps + n)
        def _():
            size = hidden // WEIGHT_STEPS
            cols = slice(n * size, (n + 1) * size)
            down_grad_ref[...] = sum_dot(act_s[:, cols], gffn_s[...]).astype(bf16)
            up_grad_ref[...] = sum_dot(second_s[...], gup_s[:, cols]).astype(bf16)
            ones = jnp.ones((8, act_s.shape[0]), bf16)
            up_sums_ref[...] = dot(ones, gup_s[:, cols])
            if n < NG:
                out_grad_ref[n * GW : (n + 1) * GW, :] = sum_dot(mixed_s[n], gatt_s[...]).astype(bf16)
            if n == WEIGHT_STEPS - 1:
                sums_ref[2:3, :] = dot(ones, gatt_s[...])[0:1]
                sums_ref[3:4, :] = dot(ones, gffn_s[...])[0:1]


WEIGHT_STEPS = 4


def feed_forward(h_zero, mixed4, inverse4, valid, cotangent, wide, down_w, vectors, tile=256):
    rows, width = h_zero.shape
    hidden = down_w.shape[0]
    row_steps = rows // tile
    last = row_steps - 1
    size = hidden // WEIGHT_STEPS
    row = lambda i: (jnp.minimum(i, last), 0)
    row4 = lambda i: (0, jnp.minimum(i, last), 0)
    after = lambda i: jnp.maximum(i - row_steps, 0)
    once = pl.Buffered(1)
    return pl.pallas_call(
        functools.partial(feed_kernel, row_steps),
        grid=(row_steps + WEIGHT_STEPS,),
        in_specs=[
            pl.BlockSpec((tile, width), row),
            pl.BlockSpec((NG, tile, GW), row4),
            pl.BlockSpec((NG, tile, GW), row4),
            pl.BlockSpec((tile, 1), row),
            pl.BlockSpec((tile, width), row),
            pl.BlockSpec((width, width), lambda i: (0, 3), pipeline_mode=once),
            pl.BlockSpec((width, hidden), lambda i: (0, 1), pipeline_mode=once),
            pl.BlockSpec((hidden, width), lambda i: (0, 0), pipeline_mode=once),
            *[whole((1, v.shape[0])) for v in vectors],
        ],
        out_specs=[
            pl.BlockSpec((tile, width), row),
            pl.BlockSpec((tile, width), row),
            pl.BlockSpec((NG, tile, GW), row4),
            pl.BlockSpec((size, width), lambda i: (after(i), 0)),
            pl.BlockSpec((width, size), lambda i: (0, after(i))),
            whole((width, width)),
            whole((8, width)),
            pl.BlockSpec((8, size), lambda i: (0, after(i))),
        ],
        out_shape=[
            jax.ShapeDtypeStruct((rows, width), bf16),
            jax.ShapeDtypeStruct((rows, width), f32),
            jax.ShapeDtypeStruct((NG, rows, GW), bf16),
            jax.ShapeDtypeStruct((hidden, width), bf16),
            jax.ShapeDtypeStruct((width, hidden), bf16),
            jax.ShapeDtypeStruct((width, width), bf16),
            jax.ShapeDtypeStruct((8, width), f32),
            jax.ShapeDtypeStruct((8, hidden), f32),
        ],
        scratch_shapes=[
            pltpu.VMEM((rows, hidden), bf16),
            pltpu.VMEM((rows, hidden), bf16),
            pltpu.VMEM((rows, width), bf16),
            pltpu.VMEM((rows, width), bf16),
            pltpu.VMEM((rows, width), bf16),
            pltpu.VMEM((NG, rows, GW), bf16),
            pltpu.VMEM((tile, width), f32),
            pltpu.VMEM((tile, width), f32),
        ],
        compiler_params=pltpu.CompilerParams(vmem_limit_bytes=56 * MIB),
        cost_estimate=pl.CostEstimate(flops=1000, bytes_accessed=1000, transcendentals=0),
        name="feed_forward",
    )(h_zero, mixed4, inverse4, valid, cotangent, wide, wide, down_w, *[v[None] for v in vectors])


def bias_back_kernel(
    pairs_step, near_ref, all_ref, means_ref, curve_ref, ds0_ref, ds1_ref, phi_ref, out_ref, dist_ref
):
    dist_ref[...] = distances(near_ref, all_ref)
    rows, span = dist_ref.shape

    @pl.when(pl.program_id(0) == 0)
    def _():
        out_ref[...] = jnp.zeros_like(out_ref)

    def body(step, acc):
        for q in range(pairs_step):
            pair = step * pairs_step + q
            here = pl.ds(pl.multiple_of(pair * 16, 16), 16)
            both = jnp.concatenate([ds0_ref[:, here, :].astype(f32), ds1_ref[:, here, :].astype(f32)], axis=0)
            for e in range(2):
                d = dist_ref[pl.ds(pair * 2 + e, 1), :]
                if e < STORED:
                    phi = phi_ref[pair * STORED + e]
                else:
                    wide = []
                    for lane in range(0, span, 128):
                        u = (d[:, lane : lane + 128] - means_ref[...]).astype(bf16)
                        wide.append(jnp.exp2((u * curve_ref[...]) * u))
                    phi = jnp.concatenate(wide, axis=1)
                d = d - CENTRE
                s = both[:, e * GH : (e + 1) * GH, :].reshape(HEADS, span)
                one = s * d
                x = jnp.concatenate([s.astype(bf16), *high_low(one), *high_low(one * d)], axis=0)
                acc = acc + lax.dot_general(
                    x, phi, (((1,), (1,)), ((), ())), preferred_element_type=f32
                )
        return acc

    out_ref[...] += lax.fori_loop(0, rows // 2 // pairs_step, body, jnp.zeros(out_ref.shape, f32))


def bias_back(near, coord_all, means, curve, ds, phi, first, count, tokens=(), tile=32, pairs_step=16):
    span = coord_all.shape[1]
    rows = count * tile
    kernel, token_specs = after(functools.partial(bias_back_kernel, pairs_step), 7, tokens)
    return pl.pallas_call(
        kernel,
        grid=(count,),
        in_specs=[
            pl.BlockSpec((tile, 3), lambda i: (i + first, 0)),
            whole((3, span)),
            whole((KERN, 128)),
            whole((KERN, 128)),
            pl.BlockSpec((NG // 2, tile * GH, span), lambda i: (0, i + first, 0)),
            pl.BlockSpec((NG // 2, tile * GH, span), lambda i: (0, i + first, 0)),
            pl.BlockSpec((tile * STORED // 2, KERN, span), lambda i: (i + first, 0, 0)),
            *token_specs,
        ],
        out_specs=whole((5 * HEADS, KERN)),
        out_shape=jax.ShapeDtypeStruct((5 * HEADS, KERN), f32),
        scratch_shapes=[pltpu.VMEM((tile, span), f32)],
        compiler_params=pltpu.CompilerParams(vmem_limit_bytes=50 * MIB),
        cost_estimate=pl.CostEstimate(flops=1000, bytes_accessed=1000, transcendentals=0),
        name="bias_back",
    )(near, coord_all, lane_wide(means), lane_wide(curve).astype(bf16), *ds, phi, *tokens)


def row_items(global_rows, group_rows, lengths, groups):
    count = lengths.shape[0]
    order = jnp.arange(count, dtype=jnp.int32)
    earlier = (groups[:, None] == groups[None, :]) & (order[None, :] < order[:, None])
    starts = jnp.sum(jnp.where(earlier, lengths[None, :], 0), axis=1)
    group_of = global_rows // group_rows
    place = global_rows - group_of * group_rows
    hits = (
        (groups[None, :] == group_of[:, None])
        & (place[:, None] >= starts[None, :])
        & (place[:, None] < starts[None, :] + lengths[None, :])
    )
    item = jnp.sum(jnp.where(hits, order[None, :], 0), axis=1)
    return (item, jnp.any(hits, axis=1))


PIECES = (1, 3, 2, 2)


def swap_sides(block):
    return lax.ppermute(block, "mp", [(0, 1), (1, 0)])


class Shards:
    def __init__(self, partial, first_bits, joint):
        chips = lax.axis_size("rows")
        bits = chips.bit_length() - 1
        stack, rows, columns = partial.shape
        self.kept = partial.reshape(stack, *[2] * bits, 2, rows // (2 * chips), columns)
        self.come = []
        order = [b for b in first_bits if b < bits] + [b for b in range(bits) if b not in first_bits]
        self.turn = [0] + [bits - b for b in order] + [bits + 1, bits + 2]
        single = len(order) - 2 if joint else len(order)
        self.order = [None] + [(b,) for b in order[:single]]
        if joint:
            self.order.append(tuple(order[single:]))

    def part(self, axis, places):
        out = None
        for value in [self.kept, *self.come]:
            for place in places:
                value = lax.dynamic_index_in_dim(value, place, axis, keepdims=False)
            if self.come:
                value = value.astype(f32)
            out = value if out is None else out + value
        return out

    def prepare(self):
        bits = self.order.pop(0)
        if bits is None:
            mine = lax.axis_index("mp")
            axis = self.kept.ndim - 3
            self.send = [self.part(axis, [1 - mine]).transpose(self.turn)]
            self.kept = self.part(axis, [mine]).transpose(self.turn)
            self.flips = None
            return
        place = lax.axis_index("rows")
        mine = [(place >> b) & 1 for b in bits]
        self.flips, self.send = [], []
        for m in range(1, 1 << len(bits)):
            flip = [(m >> n) & 1 for n in range(len(bits))]
            self.flips.append(sum(f << b for f, b in zip(flip, bits)))
            self.send.append(self.part(1, [v ^ f for v, f in zip(mine, flip)]).astype(bf16))
        self.kept = self.part(1, mine)

    def launch(self):
        chips = lax.axis_size("rows")
        if self.flips is None:
            self.come = [swap_sides(self.send[0])]
        else:
            self.come = [
                lax.ppermute(send, "rows", [(n, n ^ flip) for n in range(chips)])
                for send, flip in zip(self.send, self.flips)
            ]

    def total(self):
        while self.order:
            self.prepare()
            self.launch()
        return self.kept.astype(f32) + sum(c.astype(f32) for c in self.come)


def beside(shards, run, inputs):
    shards = [s for s in shards if s.order]
    for s in shards:
        s.prepare()
    held = [(s.send, s.kept) for s in shards]
    held, inputs = lax.optimization_barrier((held, inputs))
    for s, (send, kept) in zip(shards, held):
        s.send, s.kept = send, kept
        s.launch()
    out = run(*inputs)
    came, out = lax.optimization_barrier(([s.come for s in shards], out))
    for s, come in zip(shards, came):
        s.come = come
    return out


def everyone(visit):
    side_count = lax.axis_size("mp")
    count = lax.axis_size("rows") * side_count
    me = lax.axis_index("rows") * side_count + lax.axis_index("mp")

    def body(step, carry):
        visit(step, lax.rem(me + step, count), lax.rem(me + count - step, count))
        return carry

    lax.fori_loop(1, count, body, 0)
    return me


def address(device):
    side_count = lax.axis_size("mp")
    return (device // side_count, lax.rem(device, side_count))


def meet_everyone():
    barrier = pltpu.get_barrier_semaphore()

    def greet(step, target, source):
        pl.semaphore_signal(
            barrier, inc=1, device_id=address(target), device_id_type=pl.DeviceIdType.MESH
        )

    everyone(greet)
    pl.semaphore_wait(barrier, lax.axis_size("rows") * lax.axis_size("mp") - 1)


def remote(source_ref, target_ref, send_sem, recv_sem, device):
    return pltpu.make_async_remote_copy(
        src_ref=source_ref,
        dst_ref=target_ref,
        send_sem=send_sem,
        recv_sem=recv_sem,
        device_id=address(device),
        device_id_type=pl.DeviceIdType.MESH,
    )


def gather_kernel(*refs):
    *x_refs, out_ref, block_ref, send_sem, recv_sem = refs
    count, rows, lanes = out_ref.shape
    side_count = lax.axis_size("mp")
    me = lax.axis_index("rows") * side_count + lax.axis_index("mp")
    block = [
        jnp.concatenate([r[...].astype(f32), jnp.zeros((r.shape[0], lanes - r.shape[1]), f32)], axis=1)
        for r in x_refs
    ]
    block.append(jnp.zeros((rows - sum(r.shape[0] for r in x_refs), lanes), f32))
    block = jnp.concatenate(block, axis=0).astype(bf16)
    block_ref[...] = block
    meet_everyone()
    out_ref[me] = block

    def send(step, target, source):
        remote(block_ref, out_ref.at[me], send_sem.at[step], recv_sem.at[step], target).start()

    def wait(step, target, source):
        remote(block_ref, out_ref.at[source], send_sem.at[step], recv_sem.at[step], target).wait()

    everyone(send)
    everyone(wait)


def gather_small(vectors, count):
    return pl.pallas_call(
        gather_kernel,
        out_shape=jax.ShapeDtypeStruct((count, 16, 256), bf16),
        in_specs=[pl.BlockSpec(memory_space=pltpu.VMEM)] * len(vectors),
        out_specs=pl.BlockSpec(memory_space=pltpu.VMEM),
        scratch_shapes=[
            pltpu.VMEM((16, 256), bf16),
            pltpu.SemaphoreType.DMA((count,)),
            pltpu.SemaphoreType.DMA((count,)),
        ],
        compiler_params=pltpu.CompilerParams(
            collective_id=1, has_side_effects=True, vmem_limit_bytes=16 * MIB
        ),
        name="gather_small",
    )(*vectors)


def sum_kernel(x_ref, out_ref, come_ref, send_sem, recv_sem):
    side_count = lax.axis_size("mp")
    me = lax.axis_index("rows") * side_count + lax.axis_index("mp")
    meet_everyone()

    def send(step, target, source):
        remote(x_ref.at[target], come_ref.at[step], send_sem.at[step], recv_sem.at[step], target).start()

    def wait(step, target, source):
        remote(x_ref.at[target], come_ref.at[step], send_sem.at[step], recv_sem.at[step], target).wait()

    everyone(send)
    come_ref[0] = x_ref[me]
    everyone(wait)
    out_ref[...] = jnp.sum(come_ref[...].astype(f32), axis=0)


def sum_small(blocks):
    count = blocks.shape[0]
    return pl.pallas_call(
        sum_kernel,
        out_shape=jax.ShapeDtypeStruct(blocks.shape[1:], f32),
        in_specs=[pl.BlockSpec(memory_space=pltpu.VMEM)],
        out_specs=pl.BlockSpec(memory_space=pltpu.VMEM),
        scratch_shapes=[
            pltpu.VMEM(blocks.shape, blocks.dtype),
            pltpu.SemaphoreType.DMA((count,)),
            pltpu.SemaphoreType.DMA((count,)),
        ],
        compiler_params=pltpu.CompilerParams(
            collective_id=2, has_side_effects=True, vmem_limit_bytes=16 * MIB
        ),
        name="sum_small",
    )(blocks)


def lay_tables(share, count):
    lane = np.arange(share * count)
    place = lane[None, :] % share == np.arange(share)[:, None]
    mark = lane[None, :] // share == np.arange(count)[:, None]
    return jnp.asarray(place, bf16), jnp.asarray(mark, f32)


def joined(shares):
    count, vectors, share = shares.shape
    place, mark = lay_tables(share, count)
    wide = dot(shares.reshape(count * vectors, share), place).reshape(count, vectors, count * share)
    return jnp.sum(wide * mark[:, None, :], axis=0)


def cut(vectors, share):
    number, size = vectors.shape
    place, mark = lay_tables(share, size // share)
    wide = (vectors[None] * mark[:, None, :]).astype(bf16)
    out = lax.dot_general(wide, place, (((2,), (1,)), ((), ())), preferred_element_type=f32)
    return out.astype(bf16)


def on_device(
    atoms,
    time_embedding,
    coordinates,
    item_lengths,
    item_group,
    query_weight,
    key_weight,
    value_weight,
    out_weight,
    up_weight,
    down_weight,
    value_bias,
    out_bias,
    up_bias,
    down_bias,
    first_gain,
    first_shift,
    second_gain,
    second_shift,
    kernel_params,
    cotangent,
):
    rows_here = atoms.shape[0]
    pair_size = lax.axis_size("mp")
    side = lax.axis_index("mp")
    pair_index = lax.axis_index("rows")
    group_rows = rows_here * pair_size
    counter = jnp.arange(rows_here, dtype=jnp.int32)
    near_rows = (pair_index * pair_size + side) * rows_here + counter
    far_rows = (pair_index * pair_size + 1 - side) * rows_here + counter
    items = item_lengths.shape[0]
    near_item, near_valid = row_items(near_rows, group_rows, item_lengths, item_group)
    far_item, far_valid = row_items(far_rows, group_rows, item_lengths, item_group)
    near_code = jnp.where(near_valid, near_item, items + near_rows)
    far_code = jnp.where(far_valid, far_item, items + far_rows)
    all_code = jnp.concatenate([near_code, far_code])
    item = jnp.where(near_valid, near_item, -1)[:, None]
    valid = near_valid.astype(f32)[:, None]

    count = lax.axis_size("rows") * pair_size
    share, hidden = up_weight.shape
    width = query_weight.shape[1]
    blocks = hidden // width
    small = (value_bias, out_bias, down_bias, first_gain, first_shift, second_gain, second_shift)
    table_share = kernel_params.shape[0]
    gathered = gather_small((jnp.stack(small), up_bias[None], kernel_params[None]), count)
    value_b, out_b, down_b, gain_one, shift_one, gain_two, shift_two = joined(gathered[:, :7, :share])
    up_b = joined(gathered[:, 7:8, : blocks * share])[0]
    table = joined(gathered[:, 8:9, :table_share])[0]
    wide = lax.all_gather(
        jnp.concatenate([query_weight, key_weight, value_weight, out_weight, up_weight], axis=1),
        AXES,
        axis=0,
        tiled=True,
    )
    down_w = lax.all_gather(down_weight, AXES, axis=0, tiled=True)

    means, widths, mix = table[:KERN], table[KERN : 2 * KERN], table[2 * KERN :].reshape(KERN, HEADS)
    norm = 1.0 / (widths * math.sqrt(2.0 * math.pi))
    curve = (-0.5 * math.log2(math.e)) / (widths * widths)
    mix_low = (mix * norm[:, None] * math.log2(math.e)).astype(bf16)
    coord_low = coordinates.astype(bf16)
    coord_all = jnp.concatenate([coord_low, swap_sides(coord_low)], axis=1).astype(f32)
    near = coordinates.astype(f32).T
    bias, phi = pair_bias(near, coord_all, near_code[:, None], all_code[None], means, curve, mix_low)

    bias, wide = lax.optimization_barrier((bias, wide))
    h_zero, q4, near_kv = project(atoms, item, time_embedding, gain_one, shift_one, value_b, wide)
    far_kv = swap_sides(near_kv)
    expo, mixed4, inverse4 = attend(q4, near_kv, far_kv, bias)
    layer_out, grad_one, scaled4, down_grad, up_grad, out_grad, sums_two, up_sums = feed_forward(
        h_zero, mixed4, inverse4, valid, cotangent, wide, down_w, (out_b, up_b, down_b, gain_two, shift_two)
    )

    down_shards = Shards(down_grad[None], (0, 1), False)
    up_shards = Shards(up_grad[None], (1, 0), False)
    feed_shards = (down_shards, up_shards)
    half = NG // 2
    done = []
    for n in range(2):

        def run(scaled4):
            return attend_back(q4, scaled4, mixed4, near_kv, far_kv, expo, n * half, half), scaled4

        out, scaled4 = beside(feed_shards, run, (scaled4,))
        done.append(out)
    scores_grad = [d[0] for d in done]
    turned = [(d[2], swap_sides(d[3]), d[4], swap_sides(d[5])) for d in done]
    pairs = [done[0][1], done[1][1]]
    for m in (0, 2, 1, 3):
        pairs += [turned[0][m], turned[1][m]]
    atoms_grad, square_grads, sums_one = beside(
        feed_shards,
        lambda h_zero, *pairs: project_back(h_zero, grad_one, pairs, gain_one, shift_one, wide, out_grad),
        (h_zero, *pairs),
    )
    square_shards = Shards(square_grads, (0, 1), True)

    tiles = rows_here // 32
    moments = 0.0
    first = 0
    for eighths in PIECES:
        size = eighths * tiles // 8
        def run(near):
            send = square_shards.send[0]
            corner = send[(0,) * (send.ndim - 2)][:16, :128]
            return bias_back(near, coord_all, means, curve, scores_grad, phi, first, size, [corner]), near

        piece, near = beside((square_shards, *feed_shards), run, (near,))
        moments = moments + piece
        first += size
    zeroth = moments[:HEADS].T * norm[:, None]
    first = (moments[HEADS : 2 * HEADS] + moments[2 * HEADS : 3 * HEADS]).T * norm[:, None]
    twice = (moments[3 * HEADS : 4 * HEADS] + moments[4 * HEADS :]).T * norm[:, None]
    m_zero, m_one, m_two = [jnp.sum(mix * r, axis=1) for r in (zeroth, first, twice)]
    offset = means - CENTRE
    mean_grad = (m_one - offset * m_zero) / widths**2
    width_grad = (m_two - 2.0 * offset * m_one + offset * offset * m_zero) / widths**3 - m_zero / widths
    table_grad = jnp.concatenate([mean_grad, width_grad, zeroth.reshape(-1)])

    cuts = jnp.concatenate(
        [
            jnp.pad(
                cut(
                    jnp.stack(
                        [sums_one[2], sums_two[2], sums_two[3], sums_one[0], sums_one[1], sums_two[0], sums_two[1]]
                    ),
                    share,
                ),
                ((0, 0), (0, 0), (0, 256 - share)),
            ),
            jnp.pad(cut(up_sums[0:1], blocks * share), ((0, 0), (0, 0), (0, 256 - blocks * share))),
            jnp.pad(cut(table_grad[None], table_share), ((0, 0), (0, 7), (0, 256 - table_share))),
        ],
        axis=1,
    )
    sums = sum_small(cuts)
    square_sum = square_shards.total()
    return (
        layer_out,
        atoms_grad,
        square_sum[0],
        square_sum[1],
        square_sum[2],
        square_sum[3],
        up_shards.total()[0],
        down_shards.total()[0],
        sums[0, :share],
        sums[1, :share],
        sums[7, : blocks * share],
        sums[2, :share],
        sums[3, :share],
        sums[4, :share],
        sums[5, :share],
        sums[6, :share],
        sums[8, :table_share],
    )


def solution(mesh):
    row = P(AXES, None)
    vec = P(AXES)
    in_specs = (row, P(), P(None, AXES), P(), P(), *[row] * 6, *[vec] * 9, row)
    out_specs = (*[row] * 8, *[vec] * 9)
    return jax.shard_map(on_device, mesh=mesh, in_specs=in_specs, out_specs=out_specs, check_vma=False)
```
